32 devices in a mesh: gx: 8 (over z, x), gz: 4 (over y, core).
Axes of the slice: x: 2, y: 2, z: 4, core: 2. Of those that a mesh axis runs over, the one named last changes fastest.
Arguments:
- right_side: float32 [128, 128, 512], P('gx', None, 'gz'), may hold values from -6 to 6
- reaction: float32 [128, 128, 512], P('gx', None, 'gz'), may hold values from 0.25 to 2
- initial: float32 [128, 128, 512], P('gx', None, 'gz'), may hold values from -3 to 3
- coarse_inverse: float32 [4096, 4096], P(('gx', 'gz')), may hold values from -0.04 to 0.32
Outputs:
- pressure: float32 [128, 128, 512], P('gx', None, 'gz')
- residual: float32 [128, 128, 512], P('gx', None, 'gz')
The draws below stay inside these ranges and needn't reach their ends.
All inputs are finite; a program needn't handle non-finite values.
Results may differ from the reference program's by a relative error of at most 0.0003.
Values sent between devices are 32-bit elements; how exact they have to be, the bound alone decides.
No kernel may reach another device: no remote copies, remote signals or barrier semaphores. Data moves between devices by JAX's collectives and lax.ppermute only.
A program may use at most 192 MiB of HBM per device.

```python
import jax
import jax.numpy as jnp
from jax import lax

NY = 128
LEVELS = 4
COARSE = 16
NX = 128
NZ = 512


def draw_coarse_inverse(key, part):
    key = jax.random.fold_in(key, 7)
    first_key, second_key = jax.random.split(key)
    order = COARSE ** 3
    spread_part = jnp.clip(0.0078125 * jax.random.normal(first_key, (order, order), jnp.float32), -0.03, 0.03)
    diagonal = jax.random.uniform(second_key, (order,), jnp.float32, 0.1, 0.25)
    return spread_part + jnp.eye(order, dtype=jnp.float32) * diagonal[:, None]


def steps_of(key, dims, cuts, smallest, high):
    def one(axis_at, shards_of):
        draws = jax.random.uniform(jax.random.fold_in(jax.random.fold_in(key, 6), axis_at), (shards_of,), jnp.float32, smallest / len(cuts), high / len(cuts))
        return jnp.repeat(jnp.exp(draws), dims[axis_at] // shards_of).reshape((-1,) + (1,) * (len(dims) - axis_at - 1))

    factor_of = one(*cuts[0])
    for cut in cuts[1:]:
        factor_of = factor_of * one(*cut)
    return factor_of


def noise(key, extent, scale, bound, cuts=(), kind=jnp.bfloat16):
    factor_of = steps_of(key, extent, cuts, -0.22, 0.18) if cuts else 1.0
    entries = jax.random.normal(key, extent, jnp.float32) * scale * factor_of
    return jnp.minimum(jnp.maximum(entries, -bound), bound).astype(kind)


def setup_inputs(seed: int = 0) -> dict:
    splits = jax.random.split(jax.random.key(seed), 5)
    return {
        "right_side": noise(splits[0], (NX, NY, NZ), 1.0, 6.0, ((0, 8), (2, 4)), jnp.float32),
        "reaction": jnp.clip(0.25 + 1.75 * jax.random.uniform(splits[1], (NX, NY, NZ), jnp.float32) ** steps_of(splits[1], (NX, NY, NZ), ((0, 8), (2, 4)), -0.2, 0.2), 0.25, 2.0),
        "initial": noise(splits[2], (NX, NY, NZ), 0.5, 3.0, ((0, 8), (2, 4)), jnp.float32),
        "coarse_inverse": draw_coarse_inverse(jax.random.fold_in(splits[4], 71), 0),
    }


RELAX_WEIGHT = 0.8


def operate(field, coefficient):
    padded = jnp.pad(field, 1)
    beside_all = padded[2:, 1:-1, 1:-1] + padded[:-2, 1:-1, 1:-1]
    beside_all = beside_all + padded[1:-1, 2:, 1:-1] + padded[1:-1, :-2, 1:-1]
    beside_all = beside_all + padded[1:-1, 1:-1, 2:] + padded[1:-1, 1:-1, :-2]
    return (6.0 + coefficient) * field - beside_all


def relax(field, source, coefficient):
    return field + RELAX_WEIGHT * (source - operate(field, coefficient)) / (6.0 + coefficient)


def block_sum(values, step_x, step_y, step_z):
    size_x, size_y, size_z = values.shape
    shaped = values.reshape(size_x // step_x, step_x, size_y // step_y, step_y, size_z // step_z, step_z)
    return shaped.sum(axis=(1, 3, 5))


def spread(values, step_x, step_y, step_z):
    return jnp.repeat(jnp.repeat(jnp.repeat(values, step_x, 0), step_y, 1), step_z, 2)


def reference(right_side, reaction, initial, coarse_inverse):
    stored = []
    field, source, coefficient = initial, right_side, reaction
    last_grid = right_side
    for level_no in range(LEVELS):
        field = relax(relax(field, source, coefficient), source, coefficient)
        remainder = source - operate(field, coefficient)
        stored.append((field, source, coefficient))
        if level_no < LEVELS - 1:
            source = 0.5 * block_sum(remainder, 2, 2, 2)
            coefficient = block_sum(coefficient, 2, 2, 2) / 8.0
            field = jnp.zeros_like(source)
        else:
            last_grid = remainder
    step_x = last_grid.shape[0] // COARSE
    step_y = last_grid.shape[1] // COARSE
    step_z = last_grid.shape[2] // COARSE
    coarse_side = 0.25 * block_sum(last_grid, step_x, step_y, step_z).transpose(2, 1, 0).reshape(-1)
    coarse_field = jnp.dot(coarse_inverse, coarse_side, precision=lax.Precision.HIGHEST)
    coarse_grid = coarse_field.reshape(COARSE, COARSE, COARSE).transpose(2, 1, 0)
    lifted = spread(coarse_grid, step_x, step_y, step_z)
    for level_no in reversed(range(LEVELS)):
        field, source, coefficient = stored[level_no]
        field = relax(relax(field + lifted, source, coefficient), source, coefficient)
        if level_no > 0:
            lifted = spread(field, 2, 2, 2)
    return field, source - operate(field, coefficient)
```

```python
import functools
import math

import jax
import jax.numpy as jnp
from jax import lax
from jax.experimental import pallas as pl
from jax.experimental.pallas import tpu as pltpu
from jax.sharding import Mesh
from jax.sharding import PartitionSpec as P

COARSE = 16
RELAX_WEIGHT = 0.8
F32 = jnp.float32
LANES = 128
DEEP = 16
KEEP = 8
GUARD = 8
MIB = 1 << 20


def lanes_of(rows):
    return lax.broadcasted_iota(jnp.int32, (rows, LANES), 1)


def subs_of(rows):
    return lax.broadcasted_iota(jnp.int32, (rows, LANES), 0)


def take_lanes(values, index):
    return jnp.take_along_axis(values, index, axis=1, mode="promise_in_bounds")


def beside_lanes(values, lane, width, step):
    place = lane & (width - 1)
    low = jnp.where(place >= step, pltpu.roll(values, step, 1), 0.0)
    high = jnp.where(place < width - step, pltpu.roll(values, LANES - step, 1), 0.0)
    return low + high


def weight_of(c):
    return jnp.where(c > 0.0, RELAX_WEIGHT / (6.0 + c), 0.0)


def around(ref, at, start, rows, lane, width, lower=True, upper=True):
    center = ref[at, pl.ds(start, rows)]
    total = ref[at, pl.ds(start - 1, rows)] + ref[at, pl.ds(start + 1, rows)]
    total = total + beside_lanes(center, lane, width, 1)
    if lower:
        total = total + ref[at - 1, pl.ds(start, rows)]
    if upper:
        total = total + ref[at + 1, pl.ds(start, rows)]
    return center, total


def halve_two(ref, planes, lane, first, rows):
    index = 2 * (lane & 63)

    def part(start):
        total = None
        for at in planes:
            for odd in (0, 1):
                piece = ref[at, pl.ds(start + odd, rows, stride=2), :]
                total = piece if total is None else total + piece
        total = total + pltpu.roll(total, LANES - 1, 1)
        return take_lanes(total, index)

    return jnp.where(lane < 64, part(first), part(first + 64))


def halve_four(ref, planes, lane8, first):
    total = None
    for at in planes:
        for odd in (0, 1):
            piece = ref[at, pl.ds(first + odd, 16, stride=2), :]
            total = piece if total is None else total + piece
    total = total + pltpu.roll(total, LANES - 1, 1)
    index = (lane8 & 64) + 2 * (lane8 & 31)
    return jnp.where((lane8 & 32) == 0, take_lanes(total[:8], index), take_lanes(total[8:], index))


def call(kernel, name, outs, args, scratch=(), results=None):
    limit = sum(4 * math.prod(s) for s in scratch) + 6 * MIB
    args = [pltpu.with_memory_space_constraint(a, pltpu.VMEM) for a in args]
    shapes = [
        jax.ShapeDtypeStruct(s, F32) if results else pltpu.VMEM(s, F32) for s in outs
    ]
    return pl.pallas_call(
        kernel,
        out_shape=shapes,
        in_specs=[pl.BlockSpec(memory_space=pltpu.VMEM)] * len(args),
        out_specs=[pl.BlockSpec(memory_space=pltpu.VMEM)] * len(outs),
        scratch_shapes=[pltpu.VMEM(s, F32) for s in scratch],
        compiler_params=pltpu.CompilerParams(vmem_limit_bytes=limit),
        name=name,
    )(*args)


def turn_kernel(f_in, c_in, v_in, f_out, c_out, v_out, to_a, to_b):
    odd = lax.axis_index("gc")
    size_x, _, size_z = f_in.shape
    far = size_z - DEEP
    start_a = pl.multiple_of((1 - odd) * far, DEEP)
    start_b = pl.multiple_of(odd * far, DEEP)
    for which, (source, target) in enumerate(((f_in, f_out), (c_in, c_out), (v_in, v_out))):
        for x in range(size_x):
            target[x] = source[x].T
        to_a[which] = target[:, pl.ds(start_a, DEEP), :]
        to_b[which] = target[:, pl.ds(start_b, DEEP), :]


def fill_rows(target, at, own, low, high):
    rows = own.shape[0]
    target[at, pl.ds(GUARD, DEEP)] = low
    target[at, pl.ds(GUARD + DEEP, rows)] = own
    target[at, pl.ds(GUARD + DEEP + rows, DEEP)] = high


def coefficient_kernel(c_in, za, zb, to_a, to_b, padded):
    odd_z = lax.axis_index("gc") == 1
    even_x = lax.axis_index("gx") % 2 == 0
    size_x, size_z, _ = c_in.shape
    wide = size_z + 2 * DEEP
    coarse_rows = size_z // 4 + 2 * GUARD
    lane = lanes_of(coarse_rows)
    for x in (*range(6), *range(size_x - 6, size_x)):
        low = jnp.where(odd_z, za[1, x], zb[1, x])
        high = jnp.where(odd_z, zb[1, x], za[1, x])
        fill_rows(padded, x, c_in[x], low, high)
    sides = []
    for order in (range(size_x), range(size_x - 1, -1, -1)):
        sides.append(
            (
                padded[order[0], pl.ds(GUARD, wide)],
                padded[order[1], pl.ds(GUARD, wide)],
                0.125 * halve_two(padded, order[2:4], lane, GUARD, coarse_rows),
                0.125 * halve_two(padded, order[4:6], lane, GUARD, coarse_rows),
            )
        )
    start = 0
    for left, right in zip(*sides, strict=True):
        rows = pl.ds(start, left.shape[0])
        to_a[rows] = jnp.where(even_x, right, left)
        to_b[rows] = jnp.where(even_x, left, right)
        start += left.shape[0]


def down_kernel(
    f_in, c_in, v_in, za, zb, xa, xb,
    chunk, v_out, f_out, c_out, f1_out, c1_out, to_a, to_b,
    va, vb, c, g, f, f1, c1, u1, w1,
):
    odd_z = lax.axis_index("gc") == 1
    even_x = lax.axis_index("gx") % 2 == 0
    size_x, size_z, _ = f_in.shape
    wide = size_z + 2 * DEEP
    half = wide // 2
    parts = [(GUARD, half), (GUARD + half, half)]
    off = 4
    last = size_x + off - 1
    lane = lanes_of(half)
    zeros8 = jnp.zeros((GUARD, LANES), F32)

    for which, (source, target, shift) in enumerate(((f_in, f, 0), (c_in, c, off), (v_in, va, off))):
        for x in range(size_x):
            low = jnp.where(odd_z, za[which, x], zb[which, x])
            high = jnp.where(odd_z, zb[which, x], za[which, x])
            fill_rows(target, x + shift, source[x], low, high)
    for ref in (va, vb):
        for at in range(2, size_x + 6):
            ref[at, pl.ds(0, GUARD)] = zeros8
            ref[at, pl.ds(GUARD + wide, GUARD)] = zeros8
    for k in range(2):
        rows = pl.ds(k * wide, wide)
        c[off - 1 - k, pl.ds(GUARD, wide)] = jnp.where(even_x, xb[rows], xa[rows])
        c[last + 1 + k, pl.ds(GUARD, wide)] = jnp.where(even_x, xa[rows], xb[rows])
    for at in range(off - 2, last + 3):
        for start, rows in parts:
            g[at, pl.ds(start, rows)] = weight_of(c[at, pl.ds(start, rows)])

    for at in range(off - 1, last + 2):
        for start, rows in parts:
            here = pl.ds(start, rows)
            if at < off:
                vb[at, here] = g[at, here] * va[off, here]
            elif at > last:
                vb[at, here] = g[at, here] * va[last, here]
            else:
                center, total = around(va, at, start, rows, lane, LANES, at > off, at < last)
                vb[at, here] = 0.2 * center + g[at, here] * (total + f[at - off, here])
    for at in range(off - 2, last + 3):
        for start, rows in parts:
            here = pl.ds(start, rows)
            if at == off - 2:
                va[at, here] = g[at, here] * vb[at + 1, here]
            elif at == last + 2:
                va[at, here] = g[at, here] * vb[at - 1, here]
            else:
                center, total = around(vb, at, start, rows, lane, LANES, at > off - 1, at < last + 1)
                if off <= at <= last:
                    total = total + f[at - off, here]
                va[at, here] = 0.2 * center + g[at, here] * total
    for at in range(off - 3, last + 4):
        for start, rows in parts:
            here = pl.ds(start, rows)
            if at == off - 3:
                vb[at, here] = va[at + 1, here]
            elif at == last + 3:
                vb[at, here] = va[at - 1, here]
            else:
                center, total = around(va, at, start, rows, lane, LANES, at > off - 2, at < last + 2)
                if off <= at <= last:
                    total = total + f[at - off, here]
                vb[at, here] = total - (6.0 + c[at, here]) * center

    rows1 = size_z // 4 + 2 * GUARD
    size1 = size_x // 2
    off1 = 5
    here1 = pl.ds(GUARD, rows1)
    lane1 = lanes_of(rows1)
    for x in range(-2, size1 + 2):
        planes = [at for at in (2 * x + off, 2 * x + off + 1) if off - 3 <= at <= last + 3]
        f1[x + off1, here1] = 0.5 * halve_two(vb, planes, lane1, GUARD, rows1)
    for x in range(-1, size1 + 1):
        c1[x + off1, here1] = 0.125 * halve_two(c, (2 * x + off, 2 * x + off + 1), lane1, GUARD, rows1)
    for k in range(2):
        rows = pl.ds(2 * wide + k * rows1, rows1)
        c1[off1 - 2 - k, here1] = jnp.where(even_x, xb[rows], xa[rows])
        c1[off1 + size1 + 1 + k, here1] = jnp.where(even_x, xa[rows], xb[rows])
    low1, high1 = off1 - 2, off1 + size1 + 1
    for at in range(low1 - 1, high1 + 2):
        for ref in (u1, w1):
            ref[at, pl.ds(0, GUARD)] = zeros8
            ref[at, pl.ds(GUARD + rows1, GUARD)] = zeros8
    for at in range(low1, high1 + 1):
        u1[at, here1] = weight_of(c1[at, here1]) * f1[at, here1]
    for at in range(low1 - 1, high1 + 2):
        weight = weight_of(c1[at, here1])
        if at == low1 - 1:
            w1[at, here1] = weight * u1[at + 1, here1]
        elif at == high1 + 1:
            w1[at, here1] = weight * u1[at - 1, here1]
        else:
            center, total = around(u1, at, GUARD, rows1, lane1, 64, at > low1, at < high1)
            w1[at, here1] = 0.2 * center + weight * (total + f1[at, here1])
    for at in range(low1 - 2, high1 + 3):
        if at == low1 - 2:
            u1[at, here1] = w1[at + 1, here1]
        elif at == high1 + 2:
            u1[at, here1] = w1[at - 1, here1]
        else:
            center, total = around(w1, at, GUARD, rows1, lane1, 64, at > low1 - 1, at < high1 + 1)
            if low1 <= at <= high1:
                total = total + f1[at, here1]
            u1[at, here1] = total - (6.0 + c1[at, here1]) * center

    size2 = size_x // 4
    lane8 = lanes_of(8)
    for x in range(-2, size2 + 2):
        chunk[x + 2] = 0.5 * halve_four(u1, (2 * x + off1, 2 * x + off1 + 1), lane8, 2 * GUARD)
    for x in range(size2):
        chunk[size2 + 4 + x] = 0.125 * halve_four(c1, (2 * x + off1, 2 * x + off1 + 1), lane8, 2 * GUARD)

    inner = pl.ds(GUARD + DEEP - KEEP, size_z + 2 * KEEP)
    v_out[...] = va[pl.ds(off - 2, size_x + 4), inner]
    c_out[...] = c[pl.ds(off - 2, size_x + 4), inner]
    f_out[...] = f[:, inner]
    f1_out[...] = f1[pl.ds(off1 - 2, size1 + 4), here1]
    c1_out[...] = c1[pl.ds(off1 - 3, size1 + 6), here1]
    kept = size_z + 2 * KEEP
    start = 0
    for k in range(5):
        rows = pl.ds(start, kept)
        left, right = va[off - 2 + k, inner], va[last + 2 - k, inner]
        to_a[rows] = jnp.where(even_x, right, left)
        to_b[rows] = jnp.where(even_x, left, right)
        start += kept
    for k in range(2):
        rows = pl.ds(start, kept)
        left, right = f[k, inner], f[size_x - 1 - k, inner]
        to_a[rows] = jnp.where(even_x, right, left)
        to_b[rows] = jnp.where(even_x, left, right)
        start += kept
    pairs = [(f1, off1 - 2 + k, off1 + size1 + 1 - k) for k in range(7)]
    pairs += [(c1, off1 + 3 + k, off1 + size1 - 4 - k) for k in range(2)]
    for ref, at_left, at_right in pairs:
        rows = pl.ds(start, rows1)
        left, right = ref[at_left, here1], ref[at_right, here1]
        to_a[rows] = jnp.where(even_x, right, left)
        to_b[rows] = jnp.where(even_x, left, right)
        start += rows1


def around_tile(ref, x, t, step, lane, sub):
    center = ref[x, t]
    total = ref[x - 1, t] + ref[x + 1, t] + beside_lanes(center, lane, 32, step)
    after = pltpu.roll(jnp.where(lane < 32, ref[x, t + 1], center), LANES - 32, 1)
    total = total + pltpu.roll(jnp.where(sub < step, after, center), 8 - step, 0)
    before = pltpu.roll(jnp.where(lane >= 96, ref[x, t - 1], center), 32, 1)
    total = total + pltpu.roll(jnp.where(sub >= 8 - step, before, center), step, 0)
    return center, total


def pair_sums(values, lane, sub):
    partner = jnp.where((lane & 1) == 0, pltpu.roll(values, LANES - 1, 1), pltpu.roll(values, 1, 1))
    values = values + partner
    partner = jnp.where((sub & 1) == 0, pltpu.roll(values, 7, 0), pltpu.roll(values, 1, 0))
    return values + partner


def loop(count, body):
    if count <= 16:
        for i in range(count):
            body(i)
    else:
        lax.fori_loop(0, count, lambda i, _: (body(i), None)[1], None)


def coarse_kernel(
    nx, nz, own, other, inverse,
    window2, window3, e_out,
    v2, f2, g2, c2, u2, v3, f3, g3, c3, u3, turned, flat,
):
    core = lax.axis_index("gc")
    ny = nz // 2
    size2 = (own.shape[1] - 4) // 2
    lane, sub = lanes_of(8), subs_of(8)
    for ref in (v2, f2, g2, c2, u2, v3, f3, g3, u3):
        ref[...] = jnp.zeros(ref.shape, F32)

    def collect(at):
        for y in range(ny):
            for source, t in ((own, 1 + 2 * y + core), (other, 2 + 2 * y - core)):
                for x in range(size2 + 4):
                    f2[size2 * at + x + 2, t] += source[at * ny + y, x]
                for x in range(size2):
                    c2[size2 * at + x + 4, t] = source[at * ny + y, size2 + 4 + x]

    loop(nx, collect)

    def first(at):
        for x in range(4 + 4 * at, 8 + 4 * at) if isinstance(at, int) else [4 + 4 * at + k for k in range(4)]:
            for t in range(1, nz + 1):
                g2[x, t] = RELAX_WEIGHT / (6.0 + c2[x, t])
                u2[x, t] = g2[x, t] * f2[x, t]

    loop(nx, first)

    def second(at):
        for k in range(4):
            x = 4 + 4 * at + k
            for t in range(1, nz + 1):
                center, total = around_tile(u2, x, t, 1, lane, sub)
                v2[x, t] = 0.2 * center + g2[x, t] * (total + f2[x, t])

    loop(nx, second)

    def third(at):
        for k in range(2):
            x3 = 4 + 2 * at + k
            for t in range(1, nz + 1):
                total_r, total_c = 0.0, 0.0
                for x in (4 + 4 * at + 2 * k, 5 + 4 * at + 2 * k):
                    center, total = around_tile(v2, x, t, 1, lane, sub)
                    total_r += f2[x, t] + total - (6.0 + c2[x, t]) * center
                    total_c += c2[x, t]
                f3[x3, t] = 0.5 * pair_sums(total_r, lane, sub)
                c3[x3, t] = 0.125 * pair_sums(total_c, lane, sub)
                g3[x3, t] = RELAX_WEIGHT / (6.0 + c3[x3, t])
                u3[x3, t] = g3[x3, t] * f3[x3, t]

    loop(nx, third)

    def fourth(at):
        for k in range(2):
            x = 4 + 2 * at + k
            for t in range(1, nz + 1):
                center, total = around_tile(u3, x, t, 2, lane, sub)
                v3[x, t] = 0.2 * center + g3[x, t] * (total + f3[x, t])

    loop(nx, fourth)

    step_x = 2 * nx // COARSE
    group = nz // 4

    for t in range(1, nz + 1):
        rows = []
        for xc in range(COARSE):
            total = 0.0
            for k in range(step_x):
                x = 4 + xc * step_x + k
                center, beside = around_tile(v3, x, t, 2, lane, sub)
                total += f3[x, t] + beside - (6.0 + c3[x, t]) * center
            rows.append(jnp.sum(total, axis=0, keepdims=True))
        block = 0.125 * jnp.concatenate(rows, axis=0)
        spread = block
        for k in range(1, group):
            spread = spread + pltpu.roll(block, LANES - 32 * k, 1)
        tall = jnp.concatenate([spread, jnp.zeros((LANES - COARSE, LANES), F32)], axis=0)
        turned[...] = tall.T
        line = jnp.zeros((8, LANES), F32)
        for k in range(8):
            piece = pltpu.roll(turned[pl.ds(2 * k, 8, stride=16), :], 16 * k, 1) if k else turned[pl.ds(0, 8, stride=16), :]
            line = jnp.where((lane >= 16 * k) & (lane < 16 * k + 16), piece, line)
        count = 4 // group
        for q in range(count):
            at = 2 * ((t - 1) * count + q)
            flat[at : at + 2] = line[2 * group * q : 2 * group * q + 2]

    at_x = lax.axis_index("gx")
    at_z = 2 * lax.axis_index("gy") + core
    for k, (fields2, fields3) in enumerate(((v2, v3), (f2, f3), (g2, g3))):
        for t in range(3):
            window2[k, :, t] = fields2[pl.ds(size2 * at_x, size2 + 8), at_z + t]
            window3[k, :, t] = fields3[pl.ds(2 * at_x, 10), at_z + t]

    total = None
    for t in range(inverse.shape[1] // LANES):
        piece = inverse[:, t * LANES : (t + 1) * LANES] * flat[t : t + 1]
        total = piece if total is None else total + piece
    column = jnp.sum(total, axis=1, keepdims=True)
    copies = e_out.shape[0]
    width = -(-copies // LANES) * LANES
    e_out[...] = jnp.broadcast_to(column, (inverse.shape[0], width)).T[:copies]


def up_kernel(
    nx, nz, e, window2, window3, v_in, f_in, c_in, f1_in, c1_in, xa, xb,
    pressure, residual,
    lifted3, u3, w3, turned, u2, w2, f1, c1, u1, w1, lift1, ua, ub, g, lift0,
):
    even_x = lax.axis_index("gx") % 2 == 0
    at_x = lax.axis_index("gx")
    at_z = 2 * lax.axis_index("gy") + lax.axis_index("gc")
    lane, sub = lanes_of(8), subs_of(8)
    zeros8 = jnp.zeros((GUARD, LANES), F32)
    step_x = 2 * nx // COARSE
    group = nz // 4

    for ref in (lifted3, u3, w3, u2, w2):
        ref[...] = jnp.zeros(ref.shape, F32)
    for t in range(1, nz + 1):
        pieces = []
        for q in range(4):
            at = 2 * (((t - 1) * 4 + q) // group)
            pieces.append(e[at : at + 2])
        rows = jnp.concatenate(pieces, axis=0)
        for k in range(8):
            piece = pltpu.roll(rows, LANES - 16 * k, 1) if k else rows
            turned[pl.ds(2 * k, 8, stride=16), :] = piece
            turned[pl.ds(2 * k + 1, 8, stride=16), :] = piece
        lifted = turned[...].T
        for xc in range(COARSE):
            tile = jnp.broadcast_to(lifted[xc : xc + 1], (8, LANES))
            for k in range(step_x):
                lifted3[4 + xc * step_x + k, t] = tile
    for x in range(10):
        for t in range(3):
            u3[x, t + 1] = window3[0, x, t] + lifted3[2 * at_x + x, at_z + t]
    for source, target, margin in ((u3, w3, 1), (w3, u3, 2)):
        for x in range(margin, 10 - margin):
            for t in range(3):
                center, total = around_tile(source, x, t + 1, 2, lane, sub)
                target[x, t + 1] = 0.2 * center + window3[2, x, t] * (total + window3[1, x, t])

    size2 = 4
    planes2 = size2 + 8
    for x in range(planes2):
        for t in range(3):
            u2[x, t + 1] = window2[0, x, t] + u3[2 + x // 2, t + 1]
    for source, target, margin in ((u2, w2, 1), (w2, u2, 2)):
        for x in range(margin, planes2 - margin):
            for t in range(3):
                center, total = around_tile(source, x, t + 1, 1, lane, sub)
                target[x, t + 1] = 0.2 * center + window2[2, x, t] * (total + window2[1, x, t])

    rows1 = f1_in.shape[1]
    size1 = 2 * size2
    off1 = 5
    here1 = pl.ds(GUARD, rows1)
    lane1 = lanes_of(rows1)
    side = lane >> 6
    fine = (lane & 63) >> 1
    for x in range(2, planes2 - 2):
        below, middle, above = u2[x, 1], u2[x, 2], u2[x, 3]
        index = [(((2 * side + q) & 3) << 5) + fine for q in (-1, 0, 1, 2)]
        tiles = [
            jnp.where(side == 0, take_lanes(below, index[0]), take_lanes(middle, index[0]))[4:],
            take_lanes(middle, index[1]),
            take_lanes(middle, index[2]),
            jnp.where(side == 0, take_lanes(middle, index[3]), take_lanes(above, index[3]))[:4],
        ]
        start = 0
        for tile in tiles:
            count = tile.shape[0]
            lift1[x - 2, pl.ds(start, count, stride=2), :] = tile
            lift1[x - 2, pl.ds(start + 1, count, stride=2), :] = tile
            start += 2 * count

    kept = v_in.shape[1]
    base1 = 7 * kept

    def arrived(start, rows):
        a, b = xa[pl.ds(start, rows)], xb[pl.ds(start, rows)]
        return jnp.where(even_x, b, a), jnp.where(even_x, a, b)

    for x in range(-2, size1 + 2):
        f1[x + off1, here1] = f1_in[x + 2]
    for x in range(-3, size1 + 3):
        c1[x + off1, here1] = c1_in[x + 3]
    for k in range(7):
        left, right = arrived(base1 + k * rows1, rows1)
        if k < 4:
            f1[off1 + 1 - k, here1] += left
            f1[off1 + size1 - 2 + k, here1] += right
        else:
            f1[off1 + 1 - k, here1] = left
            f1[off1 + size1 - 2 + k, here1] = right
    for k in range(2):
        left, right = arrived(base1 + (7 + k) * rows1, rows1)
        c1[off1 - 5 + (1 - k), here1] = left
        c1[off1 + size1 + 3 + k, here1] = right
    planes1 = size1 + 10
    for ref in (u1, w1):
        for at in range(planes1):
            ref[at, pl.ds(0, GUARD)] = zeros8
            ref[at, pl.ds(GUARD + rows1, GUARD)] = zeros8
    for at in range(planes1):
        c1[at, here1] = weight_of(c1[at, here1])
        u1[at, here1] = c1[at, here1] * f1[at, here1]
    for source, target, margin in ((u1, w1, 1), (w1, u1, 2), (u1, w1, 3)):
        for at in range(margin, planes1 - margin):
            center, total = around(source, at, GUARD, rows1, lane1, 64)
            value = 0.2 * center + c1[at, here1] * (total + f1[at, here1])
            if margin == 1:
                value = value + lift1[(at - 1) // 2]
            target[at, here1] = value

    size_x = f_in.shape[0]
    size_z = kept - 2 * KEEP
    short = kept // 4
    index = lanes_of(short) >> 1
    for x in range(-2, size1 + 2):
        for part in range(2):
            source = w1[x + off1, pl.ds(GUARD + (4 if part == 0 else 8), short)]
            tile = take_lanes(source, index + 64 * part)
            lift0[x + 2, pl.ds(part * 2 * short, short, stride=2), :] = tile
            lift0[x + 2, pl.ds(part * 2 * short + 1, short, stride=2), :] = tile

    off = 3
    last = size_x + off - 1
    here = pl.ds(GUARD, kept)
    for ref in (ua, ub):
        for at in range(size_x + 6):
            ref[at, pl.ds(0, GUARD)] = zeros8
            ref[at, pl.ds(GUARD + kept, GUARD)] = zeros8
    reach = {}
    for k in range(5):
        left, right = arrived(k * kept, kept)
        reach[1 - k] = left
        reach[size_x - 2 + k] = right
    for x in range(-3, size_x + 3):
        value = lift0[(x + 4) // 2]
        if -2 <= x <= size_x + 1:
            value = value + v_in[x + 2]
        if x in reach:
            value = value + reach[x]
        ua[x + off, here] = value
    half = kept // 2
    parts = [(GUARD, half), (GUARD + half, half)]
    laneh = lanes_of(half)
    for x in range(-2, size_x + 2):
        for start, rows in parts:
            g[x + 2, pl.ds(start, rows)] = weight_of(c_in[x + 2, pl.ds(start - GUARD, rows)])

    def source_of(x, start, rows):
        at = pl.ds(start - GUARD, rows)
        if 0 <= x < size_x:
            return f_in[x, at]
        k = -1 - x if x < 0 else x - size_x
        left, right = arrived((5 + k) * kept + start - GUARD, rows)
        return left if x < 0 else right

    for source, target, margin in ((ua, ub, 1), (ub, ua, 2)):
        for at in range(margin, size_x + 6 - margin):
            for start, rows in parts:
                center, total = around(source, at, start, rows, laneh, LANES)
                total = total + source_of(at - off, start, rows)
                target[at, pl.ds(start, rows)] = 0.2 * center + g[at - 1, pl.ds(start, rows)] * total
    lane_z = lanes_of(size_z)
    own = GUARD + KEEP
    for x in range(size_x):
        center, total = around(ua, x + off, own, size_z, lane_z, LANES)
        total = total + f_in[x, pl.ds(KEEP, size_z)]
        pressure[x] = center.T
        residual[x] = (total - (6.0 + c_in[x + 2, pl.ds(KEEP, size_z)]) * center).T


def pairs_of(count):
    even = [(i, i ^ 1) for i in range(count)]
    odd = [(i, ((i - 1) ^ 1) + 1) for i in range(1, count - 1)]
    return even, odd


def local(nx, nz, right_side, reaction, initial, coarse_inverse):
    size_x, _, size_z = right_side.shape
    brick = (size_x, size_z, LANES)
    slab = (3, size_x, DEEP, LANES)
    f, c, v, mza, mzb = call(
        turn_kernel, "turn", (brick, brick, brick, slab, slab), (right_side, reaction, initial)
    )
    even_z, odd_z = pairs_of(nz)
    za = lax.ppermute(mza, ("gy", "gc"), even_z)
    zb = lax.ppermute(mzb, ("gy", "gc"), odd_z)

    wide = size_z + 2 * DEEP
    deep = wide + 2 * GUARD
    rows1 = size_z // 4 + 2 * GUARD
    size1, size2 = size_x // 2, size_x // 4
    message = (2 * wide + 2 * rows1, LANES)
    mxa, mxb = call(
        coefficient_kernel, "coefficients", (message, message), (c, za, zb), [(size_x, deep, LANES)]
    )
    even_x, odd_x = pairs_of(nx)
    xa = lax.ppermute(mxa, "gx", even_x)
    xb = lax.ppermute(mxb, "gx", odd_x)

    kept = size_z + 2 * KEEP
    margin = (7 * kept + 9 * rows1, LANES)
    field = (size_x + 8, deep, LANES)
    field1 = (size1 + 10, rows1 + 2 * GUARD, LANES)
    chunk, v, f, c, f1, c1, mua, mub = call(
        down_kernel, "down",
        (
            (2 * size2 + 4, 8, LANES),
            (size_x + 4, kept, LANES),
            (size_x, kept, LANES),
            (size_x + 4, kept, LANES),
            (size1 + 4, rows1, LANES),
            (size1 + 6, rows1, LANES),
            margin,
            margin,
        ),
        (f, c, v, za, zb, xa, xb),
        [field, field, field, field, (size_x, deep, LANES), field1, field1, field1, field1],
    )
    ua = lax.ppermute(mua, "gx", even_x)
    ub = lax.ppermute(mub, "gx", odd_x)

    copies = jnp.broadcast_to(chunk, (nx * nz // 2, *chunk.shape))
    own = lax.all_to_all(copies, ("gx", "gy"), 0, 0, tiled=True)
    other = lax.ppermute(own, "gc", [(0, 1), (1, 0)])

    grid2 = (size2 * nx + 8, nz + 2, 8, LANES)
    grid3 = (2 * nx + 8, nz + 2, 8, LANES)
    rows = coarse_inverse.shape[0]
    window2, window3, e = call(
        functools.partial(coarse_kernel, nx, nz), "coarse",
        ((3, size2 + 8, 3, 8, LANES), (3, 10, 3, 8, LANES), (nx * nz, rows)),
        (own, other, coarse_inverse),
        [*[grid2] * 5, *[grid3] * 5, (LANES, LANES), (COARSE**3 // LANES, LANES)],
    )
    e = lax.all_to_all(e, ("gx", "gy", "gc"), 0, 0, tiled=True).reshape(COARSE**3 // LANES, LANES)

    box2 = (size2 + 8, 5, 8, LANES)
    box3 = (10, 5, 8, LANES)
    box = (size_x + 6, kept + 2 * GUARD, LANES)
    return call(
        functools.partial(up_kernel, nx, nz), "up",
        ((size_x, LANES, size_z), (size_x, LANES, size_z)),
        (e, window2, window3, v, f, c, f1, c1, ua, ub),
        [
            grid3, box3, box3, (LANES, LANES), box2, box2,
            field1, field1, field1, field1, (size2 + 4, rows1, LANES),
            box, box, box, (size1 + 4, kept, LANES),
        ],
        results=True,
    )


def solution(mesh):
    nx, nz = mesh.shape["gx"], mesh.shape["gz"]
    fine = Mesh(mesh.devices.reshape(nx, nz // 2, 2), ("gx", "gy", "gc"))
    brick = P("gx", None, ("gy", "gc"))
    return jax.shard_map(
        lambda *args: tuple(local(nx, nz, *args)),
        mesh=fine,
        in_specs=(brick, brick, brick, P(("gx", "gy", "gc"), None)),
        out_specs=(brick, brick),
        check_vma=False,
    )
```

```python
import functools
import math

import jax
import jax.numpy as jnp
from jax import lax
from jax.experimental import pallas as pl
from jax.experimental.pallas import tpu as pltpu
from jax.sharding import Mesh
from jax.sharding import PartitionSpec as P

COARSE = 16
RELAX_WEIGHT = 0.8
F32 = jnp.float32
LANES = 128
DEEP = 16
KEEP = 8
GUARD = 8
MIB = 1 << 20


def lanes_of(rows):
    return lax.broadcasted_iota(jnp.int32, (rows, LANES), 1)


def subs_of(rows):
    return lax.broadcasted_iota(jnp.int32, (rows, LANES), 0)


def take_lanes(values, index):
    return jnp.take_along_axis(values, index, axis=1, mode="promise_in_bounds")


def beside_lanes(values, lane, width, step):
    place = lane & (width - 1)
    low = jnp.where(place >= step, pltpu.roll(values, step, 1), 0.0)
    high = jnp.where(place < width - step, pltpu.roll(values, LANES - step, 1), 0.0)
    return low + high


def weight_of(c):
    return jnp.where(c > 0.0, RELAX_WEIGHT / (6.0 + c), 0.0)


def around(ref, at, start, rows, lane, width, lower=True, upper=True):
    center = ref[at, pl.ds(start, rows)]
    total = ref[at, pl.ds(start - 1, rows)] + ref[at, pl.ds(start + 1, rows)]
    total = total + beside_lanes(center, lane, width, 1)
    if lower:
        total = total + ref[at - 1, pl.ds(start, rows)]
    if upper:
        total = total + ref[at + 1, pl.ds(start, rows)]
    return center, total


def halve_two(ref, planes, lane, first, rows):
    index = 2 * (lane & 63)

    def part(start):
        total = None
        for at in planes:
            for odd in (0, 1):
                piece = ref[at, pl.ds(start + odd, rows, stride=2), :]
                total = piece if total is None else total + piece
        total = total + pltpu.roll(total, LANES - 1, 1)
        return take_lanes(total, index)

    return jnp.where(lane < 64, part(first), part(first + 64))


def halve_four(ref, planes, lane8, first):
    total = None
    for at in planes:
        for odd in (0, 1):
            piece = ref[at, pl.ds(first + odd, 16, stride=2), :]
            total = piece if total is None else total + piece
    total = total + pltpu.roll(total, LANES - 1, 1)
    index = (lane8 & 64) + 2 * (lane8 & 31)
    return jnp.where((lane8 & 32) == 0, take_lanes(total[:8], index), take_lanes(total[8:], index))


def around_tile(ref, x, t, step, lane, sub):
    center = ref[x, t]
    total = ref[x - 1, t] + ref[x + 1, t] + beside_lanes(center, lane, 32, step)
    after = pltpu.roll(jnp.where(lane < 32, ref[x, t + 1], center), LANES - 32, 1)
    total = total + pltpu.roll(jnp.where(sub < step, after, center), 8 - step, 0)
    before = pltpu.roll(jnp.where(lane >= 96, ref[x, t - 1], center), 32, 1)
    total = total + pltpu.roll(jnp.where(sub >= 8 - step, before, center), step, 0)
    return center, total


def pair_sums(values, lane, sub):
    partner = jnp.where((lane & 1) == 0, pltpu.roll(values, LANES - 1, 1), pltpu.roll(values, 1, 1))
    values = values + partner
    partner = jnp.where((sub & 1) == 0, pltpu.roll(values, 7, 0), pltpu.roll(values, 1, 0))
    return values + partner


def halve_tiles(ref, planes, lane, sub, beyond):
    def edge(start):
        total = None
        for at in planes:
            for odd in (0, 1):
                piece = ref[at, pl.ds(start + odd, 4, stride=2), :]
                total = piece if total is None else total + piece
        return total

    past = jnp.concatenate([edge(beyond), edge(GUARD)], axis=0)
    past = past + pltpu.roll(past, LANES - 1, 1)
    past = take_lanes(past, jnp.where(sub < 4, 64, 0) + 2 * (lane & 31))
    kept = ((sub < 4) & (lane < 32)) | ((sub >= 4) & (lane >= 96))
    return halve_four(ref, planes, lane, 2 * GUARD), jnp.where(kept, past, 0.0)


def put_tiles(target, at, own, past, lane):
    target[at, 2] = own
    target[at, 1] = jnp.where(lane >= 96, past, 0.0)
    target[at, 3] = jnp.where(lane < 32, past, 0.0)


def call(kernel, name, outs, args, scratch=(), results=None):
    limit = sum(4 * math.prod(s) for s in scratch) + 6 * MIB
    args = [pltpu.with_memory_space_constraint(a, pltpu.VMEM) for a in args]
    shapes = [
        jax.ShapeDtypeStruct(s, F32) if results else pltpu.VMEM(s, F32) for s in outs
    ]
    return pl.pallas_call(
        kernel,
        out_shape=shapes,
        in_specs=[pl.BlockSpec(memory_space=pltpu.VMEM)] * len(args),
        out_specs=[pl.BlockSpec(memory_space=pltpu.VMEM)] * len(outs),
        scratch_shapes=[pltpu.VMEM(s, F32) for s in scratch],
        compiler_params=pltpu.CompilerParams(vmem_limit_bytes=limit),
        name=name,
    )(*args)


def turn_kernel(f_in, c_in, v_in, f_out, c_out, v_out, to_a, to_b):
    odd = lax.axis_index("gc")
    size_x, _, size_z = f_in.shape
    far = size_z - DEEP
    start_a = pl.multiple_of((1 - odd) * far, DEEP)
    start_b = pl.multiple_of(odd * far, DEEP)
    for which, (source, target) in enumerate(((f_in, f_out), (c_in, c_out), (v_in, v_out))):
        for x in range(size_x):
            target[x] = source[x].T
        to_a[which] = target[:, pl.ds(start_a, DEEP), :]
        to_b[which] = target[:, pl.ds(start_b, DEEP), :]


def fill_rows(target, at, own, low, high):
    rows = own.shape[0]
    target[at, pl.ds(GUARD, DEEP)] = low
    target[at, pl.ds(GUARD + DEEP, rows)] = own
    target[at, pl.ds(GUARD + DEEP + rows, DEEP)] = high


def coefficient_kernel(c_in, za, zb, to_a, to_b, padded, c1):
    odd_z = lax.axis_index("gc") == 1
    even_x = lax.axis_index("gx") % 2 == 0
    size_x, size_z, _ = c_in.shape
    wide = pl.ds(GUARD, size_z + 2 * DEEP)
    rows1 = size_z // 4 + 2 * GUARD
    here1 = pl.ds(GUARD, rows1)
    lane, lane8, sub8 = lanes_of(rows1), lanes_of(8), subs_of(8)
    for x in range(size_x):
        low = jnp.where(odd_z, za[1, x], zb[1, x])
        high = jnp.where(odd_z, zb[1, x], za[1, x])
        fill_rows(padded, x, c_in[x], low, high)
    for x in range(1, 7):
        c1[x, here1] = 0.125 * halve_two(padded, (2 * x, 2 * x + 1), lane, GUARD, rows1)
    sides = []
    for order, order1 in ((range(size_x), range(8)), (range(size_x - 1, -1, -1), range(7, -1, -1))):
        tiles = []
        for k in (2, 4):
            tiles += [0.125 * tile for tile in halve_tiles(c1, order1[k : k + 2], lane8, sub8, rows1)]
        sides.append(
            [padded[order[0], wide], padded[order[1], wide], c1[order1[1], here1], c1[order1[2], here1], *tiles]
        )
    start = 0
    for left, right in zip(*sides, strict=True):
        rows = pl.ds(start, left.shape[0])
        to_a[rows] = jnp.where(even_x, right, left)
        to_b[rows] = jnp.where(even_x, left, right)
        start += left.shape[0]


def down_kernel(
    f_in, c_in, v_in, za, zb, xa, xb,
    chunk, near_a, near_b, to_a, to_b, v_out, f_out, c_out, f1_out, c1_out, v1_out, v2, f2, c2,
    va, vb, c, g, f, f1, c1, u1, w1, u2, r2,
):
    odd_z = lax.axis_index("gc") == 1
    even_x = lax.axis_index("gx") % 2 == 0
    size_x, size_z, _ = f_in.shape
    wide = size_z + 2 * DEEP
    half = wide // 2
    parts = [(GUARD, half), (GUARD + half, half)]
    off = 4
    last = size_x + off - 1
    lane = lanes_of(half)
    zeros8 = jnp.zeros((GUARD, LANES), F32)

    for which, (source, target, shift) in enumerate(((f_in, f, 0), (c_in, c, off), (v_in, va, off))):
        for x in range(size_x):
            low = jnp.where(odd_z, za[which, x], zb[which, x])
            high = jnp.where(odd_z, zb[which, x], za[which, x])
            fill_rows(target, x + shift, source[x], low, high)
    for ref in (va, vb):
        for at in range(2, size_x + 6):
            ref[at, pl.ds(0, GUARD)] = zeros8
            ref[at, pl.ds(GUARD + wide, GUARD)] = zeros8
    for k in range(2):
        rows = pl.ds(k * wide, wide)
        c[off - 1 - k, pl.ds(GUARD, wide)] = jnp.where(even_x, xb[rows], xa[rows])
        c[last + 1 + k, pl.ds(GUARD, wide)] = jnp.where(even_x, xa[rows], xb[rows])
    for at in range(off - 2, last + 3):
        for start, rows in parts:
            g[at, pl.ds(start, rows)] = weight_of(c[at, pl.ds(start, rows)])

    for at in range(off - 1, last + 2):
        for start, rows in parts:
            here = pl.ds(start, rows)
            if at < off:
                vb[at, here] = g[at, here] * va[off, here]
            elif at > last:
                vb[at, here] = g[at, here] * va[last, here]
            else:
                center, total = around(va, at, start, rows, lane, LANES, at > off, at < last)
                vb[at, here] = 0.2 * center + g[at, here] * (total + f[at - off, here])
    for at in range(off - 2, last + 3):
        for start, rows in parts:
            here = pl.ds(start, rows)
            if at == off - 2:
                va[at, here] = g[at, here] * vb[at + 1, here]
            elif at == last + 2:
                va[at, here] = g[at, here] * vb[at - 1, here]
            else:
                center, total = around(vb, at, start, rows, lane, LANES, at > off - 1, at < last + 1)
                if off <= at <= last:
                    total = total + f[at - off, here]
                va[at, here] = 0.2 * center + g[at, here] * total
    for at in range(off - 3, last + 4):
        for start, rows in parts:
            here = pl.ds(start, rows)
            if at == off - 3:
                vb[at, here] = va[at + 1, here]
            elif at == last + 3:
                vb[at, here] = va[at - 1, here]
            else:
                center, total = around(va, at, start, rows, lane, LANES, at > off - 2, at < last + 2)
                if off <= at <= last:
                    total = total + f[at - off, here]
                vb[at, here] = total - (6.0 + c[at, here]) * center

    rows1 = size_z // 4 + 2 * GUARD
    size1 = size_x // 2
    off1 = 5
    here1 = pl.ds(GUARD, rows1)
    lane1 = lanes_of(rows1)
    for x in range(-2, size1 + 2):
        planes = [at for at in (2 * x + off, 2 * x + off + 1) if off - 3 <= at <= last + 3]
        f1[x + off1, here1] = 0.5 * halve_two(vb, planes, lane1, GUARD, rows1)
    for x in range(-1, size1 + 1):
        c1[x + off1, here1] = 0.125 * halve_two(c, (2 * x + off, 2 * x + off + 1), lane1, GUARD, rows1)
    for k in range(2):
        rows = pl.ds(2 * wide + k * rows1, rows1)
        c1[off1 - 2 - k, here1] = jnp.where(even_x, xb[rows], xa[rows])
        c1[off1 + size1 + 1 + k, here1] = jnp.where(even_x, xa[rows], xb[rows])
    low1, high1 = off1 - 2, off1 + size1 + 1
    for at in range(low1 - 1, high1 + 2):
        for ref in (u1, w1):
            ref[at, pl.ds(0, GUARD)] = zeros8
            ref[at, pl.ds(GUARD + rows1, GUARD)] = zeros8
    for at in range(low1, high1 + 1):
        u1[at, here1] = weight_of(c1[at, here1]) * f1[at, here1]
    for at in range(low1 - 1, high1 + 2):
        weight = weight_of(c1[at, here1])
        if at == low1 - 1:
            w1[at, here1] = weight * u1[at + 1, here1]
        elif at == high1 + 1:
            w1[at, here1] = weight * u1[at - 1, here1]
        else:
            center, total = around(u1, at, GUARD, rows1, lane1, 64, at > low1, at < high1)
            w1[at, here1] = 0.2 * center + weight * (total + f1[at, here1])
    for at in range(low1 - 2, high1 + 3):
        if at == low1 - 2:
            u1[at, here1] = w1[at + 1, here1]
        elif at == high1 + 2:
            u1[at, here1] = w1[at - 1, here1]
        else:
            center, total = around(w1, at, GUARD, rows1, lane1, 64, at > low1 - 1, at < high1 + 1)
            if low1 <= at <= high1:
                total = total + f1[at, here1]
            u1[at, here1] = total - (6.0 + c1[at, here1]) * center

    size2 = size_x // 4
    off2 = 5
    low2, high2 = off2 - 2, off2 + size2 + 1
    lane8, sub8 = lanes_of(8), subs_of(8)
    for ref in (v2, f2, c2, u2):
        ref[...] = jnp.zeros(ref.shape, F32)
    for x in range(-2, size2 + 2):
        own, past = halve_tiles(u1, (2 * x + off1, 2 * x + off1 + 1), lane8, sub8, rows1)
        put_tiles(f2, x + off2, 0.5 * own, 0.5 * past, lane8)
    for x in range(-1, size2 + 1):
        own, past = halve_tiles(c1, (2 * x + off1, 2 * x + off1 + 1), lane8, sub8, rows1)
        put_tiles(c2, x + off2, 0.125 * own, 0.125 * past, lane8)
    for k in range(2):
        own, past = (pl.ds(2 * wide + 2 * rows1 + 8 * (2 * k + j), 8) for j in (0, 1))
        put_tiles(
            c2, low2 - k, jnp.where(even_x, xb[own], xa[own]), jnp.where(even_x, xb[past], xa[past]), lane8
        )
        put_tiles(
            c2, high2 + k, jnp.where(even_x, xa[own], xb[own]), jnp.where(even_x, xa[past], xb[past]), lane8
        )
    for at in range(low2, high2 + 1):
        for t in (1, 2, 3):
            u2[at, t] = weight_of(c2[at, t]) * f2[at, t]
    for at in range(low2 - 1, high2 + 2):
        for t in (1, 2, 3):
            center, total = around_tile(u2, at, t, 1, lane8, sub8)
            v2[at, t] = 0.2 * center + weight_of(c2[at, t]) * (total + f2[at, t])
    for at in range(low2 - 2, high2 + 3):
        center, total = around_tile(v2, at, 2, 1, lane8, sub8)
        r2[at] = f2[at, 2] + total - (6.0 + c2[at, 2]) * center

    planes = [0.5 * pair_sums(r2[2 * k + 1] + r2[2 * k + 2], lane8, sub8) for k in range(size2 // 2 + 4)]
    planes += [
        0.125 * pair_sums(c2[off2 + 2 * k, 2] + c2[off2 + 2 * k + 1, 2], lane8, sub8) for k in range(size2 // 2)
    ]
    planes = [take_lanes(plane, 2 * (lane8 & 63)) for plane in planes]
    for k in range(2):
        even, odd = (
            jnp.where(lane8 < 64, planes[4 * k + j], planes[4 * k + j + 1]) for j in (0, 2)
        )
        tile = jnp.where((sub8 & 1) == 0, even, odd)
        for at in range(chunk.shape[0]):
            chunk[at, k] = tile

    pairs = [(v2, 2, off2 - k, off2 + size2 - 1 + k) for k in (1, 2, 3)]
    pairs += [(f2, 2, off2 - k, off2 + size2 - 1 + k) for k in (1, 2)]
    pairs += [(f1, here1, off1 + k, off1 + size1 - 1 - k) for k in (-2, -1, 0, 1, 2)]
    pairs += [(w1, here1, off1 + k, off1 + size1 - 1 - k) for k in (2, 3)]
    start = 0
    for ref, rows, at_left, at_right in pairs:
        left, right = ref[at_left, rows], ref[at_right, rows]
        target = pl.ds(start, left.shape[0])
        near_a[target] = jnp.where(even_x, right, left)
        near_b[target] = jnp.where(even_x, left, right)
        start += left.shape[0]

    inner = pl.ds(GUARD + DEEP - KEEP, size_z + 2 * KEEP)
    v_out[...] = va[pl.ds(off - 2, size_x + 4), inner]
    c_out[...] = c[pl.ds(off - 2, size_x + 4), inner]
    f_out[...] = f[:, inner]
    f1_out[...] = f1[pl.ds(off1 - 2, size1 + 4), here1]
    c1_out[...] = c1[pl.ds(off1 - 3, size1 + 6), here1]
    v1_out[0] = w1[off1 - 3, here1]
    v1_out[1] = w1[off1 + size1 + 2, here1]

    kept = size_z + 2 * KEEP
    lane = lanes_of(kept)
    first = GUARD + DEEP - KEEP
    sides = []
    for edge, inward in ((off, 1), (last, -1)):
        second = edge + inward
        center, total = around(va, second, first, kept, lane, LANES)
        swept = 0.2 * center + g[second, inner] * (total + f[second - off, inner])
        source = f[edge - off, inner]
        sides.append(
            (va[edge - 2 * inward, inner], va[edge - inward, inner], va[edge, inner], source + center, source + swept)
        )
    for k, (left, right) in enumerate(zip(*sides, strict=True)):
        rows = pl.ds(k * kept, kept)
        to_a[rows] = jnp.where(even_x, right, left)
        to_b[rows] = jnp.where(even_x, left, right)


def hold_kernel(a, b, _, out_a, out_b):
    out_a[...] = a[...]
    out_b[...] = b[...]


def complete_kernel(v2, f2, near_a, near_b, to_a, to_b, own, out_a, out_b):
    even_x = lax.axis_index("gx") % 2 == 0
    size2 = own.shape[0] // 2
    planes = [ref[5 + x, 2] for ref in (v2, f2) for x in range(size2)]
    for k, (base, step) in enumerate(((0, 0), (0, 1), (0, 2), (size2, 0), (size2, 1))):
        rows = pl.ds(8 * k, 8)
        left = jnp.where(even_x, near_b[rows], near_a[rows])
        right = jnp.where(even_x, near_a[rows], near_b[rows])
        planes[base + step] = planes[base + step] + left
        planes[base + size2 - 1 - step] = planes[base + size2 - 1 - step] + right
    for k, plane in enumerate(planes):
        own[k] = plane
    out_a[...] = to_a[...]
    out_b[...] = to_b[...]


def past_tiles(za, zb, k, odd_z, lane):
    below = jnp.where(odd_z, za[k], zb[k])
    above = jnp.where(odd_z, zb[k], za[k])
    return jnp.where(lane >= 96, below, jnp.where(lane < 32, above, 0.0))


def side_kernel(own, za, zb, to_a, to_b):
    odd_z = lax.axis_index("gc") == 1
    even_x = lax.axis_index("gx") % 2 == 0
    size2 = own.shape[0] // 2
    lane = lanes_of(8)
    tiles = [(own[k], past_tiles(za, zb, k, odd_z, lane)) for k in range(2 * size2)]
    at = 0
    for base, count in ((0, size2), (size2, size2 - 1)):
        for k in range(count):
            for left, right in zip(tiles[base + k], tiles[base + size2 - 1 - k], strict=True):
                to_a[at] = jnp.where(even_x, right, left)
                to_b[at] = jnp.where(even_x, left, right)
                at += 1


def loop(count, body):
    if count <= 16:
        for i in range(count):
            body(i)
    else:
        lax.fori_loop(0, count, lambda i, _: (body(i), None)[1], None)


def coarse_kernel(
    nx, nz, own, other, inverse, _,
    window3, e_out,
    v3, f3, g3, c3, u3, turned, flat,
):
    core = lax.axis_index("gc")
    ny = nz // 2
    lane, sub = lanes_of(8), subs_of(8)
    for ref in (v3, f3, g3, u3):
        ref[...] = jnp.zeros(ref.shape, F32)

    def collect(at):
        for y in range(ny):
            for source, t in ((own, 1 + 2 * y + core), (other, 2 + 2 * y - core)):
                planes = []
                for k in range(2):
                    tile = source[at * ny + y, k]
                    even = jnp.where((sub & 1) == 0, tile, pltpu.roll(tile, 1, 0))
                    odd = jnp.where((sub & 1) == 1, tile, pltpu.roll(tile, 7, 0))
                    planes += [take_lanes(part, (lane >> 1) + 64 * j) for part in (even, odd) for j in (0, 1)]
                for k in range(6):
                    f3[2 * at + 2 + k, t] += planes[k]
                for k in range(2):
                    c3[2 * at + 4 + k, t] = planes[6 + k]

    loop(nx, collect)

    def third(at):
        for k in range(2):
            x = 4 + 2 * at + k
            for t in range(1, nz + 1):
                g3[x, t] = RELAX_WEIGHT / (6.0 + c3[x, t])
                u3[x, t] = g3[x, t] * f3[x, t]

    loop(nx, third)

    def fourth(at):
        for k in range(2):
            x = 4 + 2 * at + k
            for t in range(1, nz + 1):
                center, total = around_tile(u3, x, t, 2, lane, sub)
                v3[x, t] = 0.2 * center + g3[x, t] * (total + f3[x, t])

    loop(nx, fourth)

    step_x = 2 * nx // COARSE
    group = nz // 4

    for t in range(1, nz + 1):
        rows = []
        for xc in range(COARSE):
            total = 0.0
            for k in range(step_x):
                x = 4 + xc * step_x + k
                center, beside = around_tile(v3, x, t, 2, lane, sub)
                total += f3[x, t] + beside - (6.0 + c3[x, t]) * center
            rows.append(jnp.sum(total, axis=0, keepdims=True))
        block = 0.125 * jnp.concatenate(rows, axis=0)
        spread = block
        for k in range(1, group):
            spread = spread + pltpu.roll(block, LANES - 32 * k, 1)
        tall = jnp.concatenate([spread, jnp.zeros((LANES - COARSE, LANES), F32)], axis=0)
        turned[...] = tall.T
        line = jnp.zeros((8, LANES), F32)
        for k in range(8):
            piece = pltpu.roll(turned[pl.ds(2 * k, 8, stride=16), :], 16 * k, 1) if k else turned[pl.ds(0, 8, stride=16), :]
            line = jnp.where((lane >= 16 * k) & (lane < 16 * k + 16), piece, line)
        count = 4 // group
        for q in range(count):
            at = 2 * ((t - 1) * count + q)
            flat[at : at + 2] = line[2 * group * q : 2 * group * q + 2]

    at_x = lax.axis_index("gx")
    at_z = 2 * lax.axis_index("gy") + core
    for k, ref in enumerate((v3, f3, g3)):
        for t in range(3):
            window3[k, :, t] = ref[pl.ds(2 * at_x, 10), at_z + t]

    total = None
    for t in range(inverse.shape[1] // LANES):
        piece = inverse[:, t * LANES : (t + 1) * LANES] * flat[t : t + 1]
        total = piece if total is None else total + piece
    column = jnp.sum(total, axis=1, keepdims=True)
    copies = e_out.shape[0]
    width = -(-copies // LANES) * LANES
    e_out[...] = jnp.broadcast_to(column, (inverse.shape[0], width)).T[:copies]


def top_kernel(nx, nz, e, window3, u3, lifted3, w3, turned):
    at_x = lax.axis_index("gx")
    at_z = 2 * lax.axis_index("gy") + lax.axis_index("gc")
    lane, sub = lanes_of(8), subs_of(8)
    step_x = 2 * nx // COARSE
    group = nz // 4

    for ref in (lifted3, u3, w3):
        ref[...] = jnp.zeros(ref.shape, F32)
    for t in range(1, nz + 1):
        pieces = []
        for q in range(4):
            at = 2 * (((t - 1) * 4 + q) // group)
            pieces.append(e[at : at + 2])
        rows = jnp.concatenate(pieces, axis=0)
        for k in range(8):
            piece = pltpu.roll(rows, LANES - 16 * k, 1) if k else rows
            turned[pl.ds(2 * k, 8, stride=16), :] = piece
            turned[pl.ds(2 * k + 1, 8, stride=16), :] = piece
        lifted = turned[...].T
        for xc in range(COARSE):
            tile = jnp.broadcast_to(lifted[xc : xc + 1], (8, LANES))
            for k in range(step_x):
                lifted3[4 + xc * step_x + k, t] = tile
    for x in range(10):
        for t in range(3):
            u3[x, t + 1] = window3[0, x, t] + lifted3[2 * at_x + x, at_z + t]
    for source, target, margin in ((u3, w3, 1), (w3, u3, 2)):
        for x in range(margin, 10 - margin):
            for t in range(3):
                center, total = around_tile(source, x, t + 1, 2, lane, sub)
                target[x, t + 1] = 0.2 * center + window3[2, x, t] * (total + window3[1, x, t])


def up_kernel(
    nx, nz, u3, own2, za, zb, sides_a, sides_b, c2, v_in, f_in, c_in, f1_in, c1_in, v1_in, near_a, near_b, xa, xb,
    pressure, residual,
    u2, w2, f2, f1, c1, u1, w1, lift1, ua, ub, g, lift0,
):
    even_x = lax.axis_index("gx") % 2 == 0
    lane, sub = lanes_of(8), subs_of(8)
    zeros8 = jnp.zeros((GUARD, LANES), F32)
    for ref in (u2, w2, f2):
        ref[...] = jnp.zeros(ref.shape, F32)

    odd_z = lax.axis_index("gc") == 1
    size2 = own2.shape[0] // 2
    planes2 = size2 + 8
    for k in range(2 * size2):
        target = u2 if k < size2 else f2
        put_tiles(target, 4 + k % size2, own2[k], past_tiles(za, zb, k, odd_z, lane), lane)
    at = 0
    for target, count in ((u2, size2), (f2, size2 - 1)):
        for k in range(count):
            left = [jnp.where(even_x, sides_b[at + j], sides_a[at + j]) for j in (0, 1)]
            right = [jnp.where(even_x, sides_a[at + j], sides_b[at + j]) for j in (0, 1)]
            put_tiles(target, 3 - k, *left, lane)
            put_tiles(target, 4 + size2 + k, *right, lane)
            at += 2
    for x in range(planes2):
        for t in (1, 2, 3):
            u2[x, t] += u3[2 + x // 2, t]
    for source, target, margin in ((u2, w2, 1), (w2, u2, 2)):
        for x in range(margin, planes2 - margin):
            for t in (1, 2, 3):
                center, total = around_tile(source, x, t, 1, lane, sub)
                target[x, t] = 0.2 * center + weight_of(c2[x + 1, t]) * (total + f2[x, t])

    rows1 = f1_in.shape[1]
    size1 = 2 * size2
    off1 = 4
    here1 = pl.ds(GUARD, rows1)
    lane1 = lanes_of(rows1)
    side = lane >> 6
    fine = (lane & 63) >> 1
    for x in range(2, planes2 - 2):
        below, middle, above = u2[x, 1], u2[x, 2], u2[x, 3]
        index = [(((2 * side + q) & 3) << 5) + fine for q in (-1, 0, 1, 2)]
        tiles = [
            jnp.where(side == 0, take_lanes(below, index[0]), take_lanes(middle, index[0]))[4:],
            take_lanes(middle, index[1]),
            take_lanes(middle, index[2]),
            jnp.where(side == 0, take_lanes(middle, index[3]), take_lanes(above, index[3]))[:4],
        ]
        start = 0
        for tile in tiles:
            count = tile.shape[0]
            lift1[x - 2, pl.ds(start, count, stride=2), :] = tile
            lift1[x - 2, pl.ds(start + 1, count, stride=2), :] = tile
            start += 2 * count

    kept = v_in.shape[1]

    def arrived(start, rows, a=xa, b=xb):
        a, b = a[pl.ds(start, rows)], b[pl.ds(start, rows)]
        return jnp.where(even_x, b, a), jnp.where(even_x, a, b)

    for x in range(-2, size1 + 2):
        f1[x + off1, here1] = f1_in[x + 2]
    for x in range(-3, size1 + 3):
        c1[x + off1, here1] = weight_of(c1_in[x + 3])
    base1 = 40
    for k in range(7):
        left, right = arrived(base1 + k * rows1, rows1, near_a, near_b)
        if k < 4:
            f1[off1 + 1 - k, here1] += left
            f1[off1 + size1 - 2 + k, here1] += right
        elif k == 4:
            f1[off1 - 3, here1] = left
            f1[off1 + size1 + 2, here1] = right
        else:
            w1[off1 + 2 - k, here1] = left + v1_in[0] if k == 5 else left
            w1[off1 + size1 - 3 + k, here1] = right + v1_in[1] if k == 5 else right
    planes1 = size1 + 8
    for ref in (u1, w1):
        for at in range(planes1):
            ref[at, pl.ds(0, GUARD)] = zeros8
            ref[at, pl.ds(GUARD + rows1, GUARD)] = zeros8
    for at in range(1, planes1 - 1):
        u1[at, here1] = c1[at, here1] * f1[at, here1]
    for at in range(planes1):
        value = w1[at, here1]
        if 2 <= at < planes1 - 2:
            center, total = around(u1, at, GUARD, rows1, lane1, 64)
            value = 0.2 * center + c1[at, here1] * (total + f1[at, here1])
        w1[at, here1] = value + lift1[at // 2]
    for source, target, margin in ((w1, u1, 1), (u1, w1, 2)):
        for at in range(margin, planes1 - margin):
            center, total = around(source, at, GUARD, rows1, lane1, 64)
            target[at, here1] = 0.2 * center + c1[at, here1] * (total + f1[at, here1])

    size_x = f_in.shape[0]
    size_z = kept - 2 * KEEP
    short = kept // 4
    index = lanes_of(short) >> 1
    for x in range(-2, size1 + 2):
        for part in range(2):
            source = w1[x + off1, pl.ds(GUARD + (4 if part == 0 else 8), short)]
            tile = take_lanes(source, index + 64 * part)
            lift0[x + 2, pl.ds(part * 2 * short, short, stride=2), :] = tile
            lift0[x + 2, pl.ds(part * 2 * short + 1, short, stride=2), :] = tile

    off = 3
    last = size_x + off - 1
    here = pl.ds(GUARD, kept)
    for ref in (ua, ub):
        for at in range(size_x + 6):
            ref[at, pl.ds(0, GUARD)] = zeros8
            ref[at, pl.ds(GUARD + kept, GUARD)] = zeros8
    for x in range(-3, size_x + 3):
        value = lift0[(x + 4) // 2]
        if -2 <= x <= size_x + 1:
            value = value + v_in[x + 2]
        ua[x + off, here] = value
    edges = ua[off - 1, here], ua[last + 1, here]
    for k in range(3):
        left, right = arrived(k * kept, kept)
        ua[off + 1 - k, here] += left
        ua[last - 1 + k, here] += right
    half = kept // 2
    parts = [(GUARD, half), (GUARD + half, half)]
    laneh = lanes_of(half)
    for x in range(-2, size_x + 2):
        for start, rows in parts:
            g[x + 2, pl.ds(start, rows)] = weight_of(c_in[x + 2, pl.ds(start - GUARD, rows)])

    def source_of(x, start, rows, sweep):
        if 0 <= x < size_x:
            return f_in[x, pl.ds(start - GUARD, rows)]
        return arrived((3 + sweep) * kept + start - GUARD, rows)[0 if x < 0 else 1]

    for at, edge, outward in ((1, edges[0], -1), (size_x + 4, edges[1], 1)):
        for start, rows in parts:
            center, total = around(ua, at, start, rows, laneh, LANES, outward < 0, outward > 0)
            total = total + edge[start - GUARD : start - GUARD + rows]
            ub[at, pl.ds(start, rows)] = 0.2 * center + g[at - 1, pl.ds(start, rows)] * total
    for source, target in ((ua, ub), (ub, ua)):
        for at in range(2, size_x + 4):
            for start, rows in parts:
                center, total = around(source, at, start, rows, laneh, LANES)
                total = total + source_of(at - off, start, rows, 0 if source is ua else 1)
                target[at, pl.ds(start, rows)] = 0.2 * center + g[at - 1, pl.ds(start, rows)] * total
    lane_z = lanes_of(size_z)
    own = GUARD + KEEP
    for x in range(size_x):
        center, total = around(ua, x + off, own, size_z, lane_z, LANES)
        total = total + f_in[x, pl.ds(KEEP, size_z)]
        pressure[x] = center.T
        residual[x] = (total - (6.0 + c_in[x + 2, pl.ds(KEEP, size_z)]) * center).T


def pairs_of(count):
    even = [(i, i ^ 1) for i in range(count)]
    odd = [(i, ((i - 1) ^ 1) + 1) for i in range(1, count - 1)]
    return even, odd


def local(nx, nz, right_side, reaction, initial, coarse_inverse):
    size_x, _, size_z = right_side.shape
    brick = (size_x, size_z, LANES)
    slab = (3, size_x, DEEP, LANES)
    f, c, v, mza, mzb = call(
        turn_kernel, "turn", (brick, brick, brick, slab, slab), (right_side, reaction, initial)
    )
    even_z, odd_z = pairs_of(nz)
    za = lax.ppermute(mza, ("gy", "gc"), even_z)
    zb = lax.ppermute(mzb, ("gy", "gc"), odd_z)

    wide = size_z + 2 * DEEP
    deep = wide + 2 * GUARD
    rows1 = size_z // 4 + 2 * GUARD
    size1, size2 = size_x // 2, size_x // 4
    box2 = (size2 + 10, 5, 8, LANES)
    near = (40 + 7 * rows1, LANES)
    message = (2 * wide + 2 * rows1 + 32, LANES)
    mxa, mxb = call(
        coefficient_kernel, "coefficients", (message, message), (c, za, zb),
        [(size_x, deep, LANES), (size1, rows1 + 2 * GUARD, LANES)],
    )
    even_x, odd_x = pairs_of(nx)
    xa = lax.ppermute(mxa, "gx", even_x)
    xb = lax.ppermute(mxb, "gx", odd_x)

    kept = size_z + 2 * KEEP
    margin = (5 * kept, LANES)
    field = (size_x + 8, deep, LANES)
    field1 = (size1 + 10, rows1 + 2 * GUARD, LANES)
    chunk, mna, mnb, mua, mub, v, f, c, f1, c1, v1, v2, f2, c2 = call(
        down_kernel, "down",
        (
            (nx * nz // 2, 2, 8, LANES),
            near,
            near,
            margin,
            margin,
            (size_x + 4, kept, LANES),
            (size_x, kept, LANES),
            (size_x + 4, kept, LANES),
            (size1 + 4, rows1, LANES),
            (size1 + 6, rows1, LANES),
            (2, rows1, LANES),
            box2,
            box2,
            box2,
        ),
        (f, c, v, za, zb, xa, xb),
        [field, field, field, field, (size_x, deep, LANES), field1, field1, field1, field1, box2, (size2 + 10, 8, LANES)],
    )
    own = lax.all_to_all(chunk, ("gx", "gy"), 0, 0, tiled=True)
    mna, mnb = call(hold_kernel, "hold", (near, near), (mna, mnb, own))
    other = lax.ppermute(own, "gc", [(0, 1), (1, 0)])
    na = lax.ppermute(mna, "gx", even_x)
    nb = lax.ppermute(mnb, "gx", odd_x)

    own2, mua, mub = call(
        complete_kernel, "complete", ((2 * size2, 8, LANES), margin, margin), (v2, f2, na, nb, mua, mub)
    )
    ua = lax.ppermute(mua, "gx", even_x)
    ub = lax.ppermute(mub, "gx", odd_x)
    z2a = lax.ppermute(own2, ("gy", "gc"), even_z)
    z2b = lax.ppermute(own2, ("gy", "gc"), odd_z)
    sides = (4 * size2 - 2, 8, LANES)
    msa, msb = call(side_kernel, "sides", (sides, sides), (own2, z2a, z2b))
    sa = lax.ppermute(msa, "gx", even_x)
    sb = lax.ppermute(msb, "gx", odd_x)

    grid3 = (2 * nx + 8, nz + 2, 8, LANES)
    rows = coarse_inverse.shape[0]
    window3, e = call(
        functools.partial(coarse_kernel, nx, nz), "coarse",
        ((3, 10, 3, 8, LANES), (nx * nz, rows)),
        (own, other, coarse_inverse, msa),
        [*[grid3] * 5, (LANES, LANES), (COARSE**3 // LANES, LANES)],
    )
    e = lax.all_to_all(e, ("gx", "gy", "gc"), 0, 0, tiled=True).reshape(COARSE**3 // LANES, LANES)

    near2 = (size2 + 8, 5, 8, LANES)
    box3 = (10, 5, 8, LANES)
    (u3,) = call(
        functools.partial(top_kernel, nx, nz), "top", (box3,), (e, window3), [grid3, box3, (LANES, LANES)]
    )
    box = (size_x + 6, kept + 2 * GUARD, LANES)
    return call(
        functools.partial(up_kernel, nx, nz), "up",
        ((size_x, LANES, size_z), (size_x, LANES, size_z)),
        (u3, own2, z2a, z2b, sa, sb, c2, v, f, c, f1, c1, v1, na, nb, ua, ub),
        [
            near2, near2, near2,
            field1, field1, field1, field1, (size2 + 4, rows1, LANES),
            box, box, box, (size1 + 4, kept, LANES),
        ],
        results=True,
    )


def solution(mesh):
    nx, nz = mesh.shape["gx"], mesh.shape["gz"]
    fine = Mesh(mesh.devices.reshape(nx, nz // 2, 2), ("gx", "gy", "gc"))
    brick = P("gx", None, ("gy", "gc"))
    return jax.shard_map(
        lambda *args: tuple(local(nx, nz, *args)),
        mesh=fine,
        in_specs=(brick, brick, brick, P(("gx", "gy", "gc"), None)),
        out_specs=(brick, brick),
        check_vma=False,
    )
```

```python
import functools
import math

import jax
import jax.numpy as jnp
from jax import lax
from jax.experimental import pallas as pl
from jax.experimental.pallas import tpu as pltpu
from jax.sharding import Mesh
from jax.sharding import PartitionSpec as P

COARSE = 16
RELAX_WEIGHT = 0.8
F32 = jnp.float32
LANES = 128
DEEP = 16
KEEP = 8
SENT = 4
GUARD = 8
MIB = 1 << 20


def lanes_of(rows):
    return lax.broadcasted_iota(jnp.int32, (rows, LANES), 1)


def subs_of(rows):
    return lax.broadcasted_iota(jnp.int32, (rows, LANES), 0)


def take_lanes(values, index):
    return jnp.take_along_axis(values, index, axis=1, mode="promise_in_bounds")


def beside_lanes(values, lane, width, step):
    place = lane & (width - 1)
    low = jnp.where(place >= step, pltpu.roll(values, step, 1), 0.0)
    high = jnp.where(place < width - step, pltpu.roll(values, LANES - step, 1), 0.0)
    return low + high


def weight_of(c):
    return jnp.where(c > 0.0, RELAX_WEIGHT / (6.0 + c), 0.0)


def around(ref, at, start, rows, lane, width, lower=True, upper=True):
    center = ref[at, pl.ds(start, rows)]
    total = ref[at, pl.ds(start - 1, rows)] + ref[at, pl.ds(start + 1, rows)]
    total = total + beside_lanes(center, lane, width, 1)
    if lower:
        total = total + ref[at - 1, pl.ds(start, rows)]
    if upper:
        total = total + ref[at + 1, pl.ds(start, rows)]
    return center, total


def halve_two(ref, planes, lane, first, rows):
    index = 2 * (lane & 63)

    def part(start):
        total = None
        for at in planes:
            for odd in (0, 1):
                piece = ref[at, pl.ds(start + odd, rows, stride=2), :]
                total = piece if total is None else total + piece
        total = total + pltpu.roll(total, LANES - 1, 1)
        return take_lanes(total, index)

    return jnp.where(lane < 64, part(first), part(first + 64))


def halve_four(ref, planes, lane8, first):
    total = None
    for at in planes:
        for odd in (0, 1):
            piece = ref[at, pl.ds(first + odd, 16, stride=2), :]
            total = piece if total is None else total + piece
    total = total + pltpu.roll(total, LANES - 1, 1)
    index = (lane8 & 64) + 2 * (lane8 & 31)
    return jnp.where((lane8 & 32) == 0, take_lanes(total[:8], index), take_lanes(total[8:], index))


def around_tile(ref, x, t, step, lane, sub):
    center = ref[x, t]
    total = ref[x - 1, t] + ref[x + 1, t] + beside_lanes(center, lane, 32, step)
    after = pltpu.roll(jnp.where(lane < 32, ref[x, t + 1], center), LANES - 32, 1)
    total = total + pltpu.roll(jnp.where(sub < step, after, center), 8 - step, 0)
    before = pltpu.roll(jnp.where(lane >= 96, ref[x, t - 1], center), 32, 1)
    total = total + pltpu.roll(jnp.where(sub >= 8 - step, before, center), step, 0)
    return center, total


def pair_sums(values, lane, sub):
    partner = jnp.where((lane & 1) == 0, pltpu.roll(values, LANES - 1, 1), pltpu.roll(values, 1, 1))
    values = values + partner
    partner = jnp.where((sub & 1) == 0, pltpu.roll(values, 7, 0), pltpu.roll(values, 1, 0))
    return values + partner


def halve_tiles(ref, planes, lane, sub, beyond):
    def edge(start):
        total = None
        for at in planes:
            for odd in (0, 1):
                piece = ref[at, pl.ds(start + odd, 4, stride=2), :]
                total = piece if total is None else total + piece
        return total

    past = jnp.concatenate([edge(beyond), edge(GUARD)], axis=0)
    past = past + pltpu.roll(past, LANES - 1, 1)
    past = take_lanes(past, jnp.where(sub < 4, 64, 0) + 2 * (lane & 31))
    kept = ((sub < 4) & (lane < 32)) | ((sub >= 4) & (lane >= 96))
    return halve_four(ref, planes, lane, 2 * GUARD), jnp.where(kept, past, 0.0)


def put_tiles(target, at, own, past, lane):
    target[at, 2] = own
    target[at, 1] = jnp.where(lane >= 96, past, 0.0)
    target[at, 3] = jnp.where(lane < 32, past, 0.0)


def call(kernel, name, outs, args, scratch=(), far_args=(), far_outs=(), copies=0, results=False, micros=1):
    limit = sum(4 * math.prod(s) for s in scratch) + 6 * MIB
    spaces_in = [pltpu.HBM if k in far_args else pltpu.VMEM for k in range(len(args))]
    spaces_out = [pltpu.HBM if k in far_outs else pltpu.VMEM for k in range(len(outs))]
    args = [pltpu.with_memory_space_constraint(a, space) for a, space in zip(args, spaces_in, strict=True)]
    return pl.pallas_call(
        kernel,
        out_shape=[
            jax.ShapeDtypeStruct(s, F32) if results else space(s, F32)
            for s, space in zip(outs, spaces_out, strict=True)
        ],
        in_specs=[pl.BlockSpec(memory_space=space) for space in spaces_in],
        out_specs=[pl.BlockSpec(memory_space=space) for space in spaces_out],
        scratch_shapes=[pltpu.VMEM(s, F32) for s in scratch] + [pltpu.SemaphoreType.DMA((copies,))] * (copies > 0),
        compiler_params=pltpu.CompilerParams(vmem_limit_bytes=limit),
        cost_estimate=pl.CostEstimate(flops=0, bytes_accessed=3_000_000 * micros, transcendentals=0),
        name=name,
    )(*args)


def edge_rows(source, to_a, to_b):
    odd = lax.axis_index("gc")
    far = source.shape[1] - DEEP
    to_a[...] = source[:, pl.ds(pl.multiple_of((1 - odd) * far, DEEP), DEEP), :]
    to_b[...] = source[:, pl.ds(pl.multiple_of(odd * far, DEEP), DEEP), :]


def turn_kernel(*refs):
    *refs, held, arrivals = refs
    count = (len(refs) - 2) // 2
    sources, targets, (to_a, to_b) = refs[:count], refs[count : 2 * count], refs[2 * count :]
    piece = targets[0].shape[0] // 4
    copies = []
    for which, source in enumerate(sources):
        for k in range(4):
            planes = pl.ds(k * piece, piece)
            copies.append(
                pltpu.make_async_copy(source.at[planes], held.at[which, planes], arrivals.at[4 * which + k])
            )
            copies[-1].start()
    for which, target in enumerate(targets):
        for k in range(4):
            copies[4 * which + k].wait()
            for x in range(k * piece, (k + 1) * piece):
                target[x] = held[which, x].T
        edge_rows(target, to_a.at[which], to_b.at[which])


def turn_again_kernel(v_in, _, v_out, to_a, to_b):
    for x in range(v_out.shape[0]):
        v_out[x] = v_in[x].T
    edge_rows(v_out, to_a, to_b)


def fill_rows(target, at, own, low, high):
    rows = own.shape[0]
    target[at, pl.ds(GUARD, DEEP)] = low
    target[at, pl.ds(GUARD + DEEP, rows)] = own
    target[at, pl.ds(GUARD + DEEP + rows, DEEP)] = high


def coefficient_kernel(c_in, za, zb, to_a, to_b, padded, c1):
    odd_z = lax.axis_index("gc") == 1
    even_x = lax.axis_index("gx") % 2 == 0
    size_x, size_z, _ = c_in.shape
    wide = pl.ds(GUARD, size_z + 2 * DEEP)
    rows1 = size_z // 4 + 2 * GUARD
    here1 = pl.ds(GUARD, rows1)
    lane, lane8, sub8 = lanes_of(rows1), lanes_of(8), subs_of(8)
    for x in range(size_x):
        low = jnp.where(odd_z, za[0, x], zb[0, x])
        high = jnp.where(odd_z, zb[0, x], za[0, x])
        fill_rows(padded, x, c_in[x], low, high)
    for x in range(size_x // 2):
        c1[x, here1] = 0.125 * halve_two(padded, (2 * x, 2 * x + 1), lane, GUARD, rows1)
    sides = []
    for order, order1 in ((range(size_x), range(8)), (range(size_x - 1, -1, -1), range(7, -1, -1))):
        tiles = []
        for k in (2, 4):
            tiles += [0.125 * tile for tile in halve_tiles(c1, order1[k : k + 2], lane8, sub8, rows1)]
        sides.append(
            [padded[order[0], wide], padded[order[1], wide], c1[order1[1], here1], c1[order1[2], here1], *tiles]
        )
    start = 0
    for left, right in zip(*sides, strict=True):
        rows = pl.ds(start, left.shape[0])
        to_a[rows] = jnp.where(even_x, right, left)
        to_b[rows] = jnp.where(even_x, left, right)
        start += left.shape[0]


def inner_kernel(
    f_in, v_in, c, za, zb, ya, yb,
    f, v2, edges, f1, to_a, to_b, later_a, later_b, f_far, c_far,
    va, vb, g, r, arrivals,
):
    odd_z = lax.axis_index("gc") == 1
    even_x = lax.axis_index("gx") % 2 == 0
    size_x, size_z, _ = f_in.shape
    wide = size_z + 2 * DEEP
    half = wide // 2
    parts = [(GUARD, half), (GUARD + half, half)]
    last = size_x - 1
    lane = lanes_of(half)
    zeros8 = jnp.zeros((GUARD, LANES), F32)

    kept = pl.ds(GUARD + DEEP - KEEP, size_z + 2 * KEEP)
    copies = [pltpu.make_async_copy(c.at[:, kept], c_far, arrivals.at[0])]
    copies[0].start()
    for source, target, a, b in ((f_in, f, za.at[1], zb.at[1]), (v_in, va, ya, yb)):
        for x in range(size_x):
            low = jnp.where(odd_z, a[x], b[x])
            high = jnp.where(odd_z, b[x], a[x])
            fill_rows(target, x, source[x], low, high)
        if target is f:
            copies.append(pltpu.make_async_copy(f.at[:, kept], f_far, arrivals.at[1]))
            copies[1].start()
    for ref in (va, vb, v2):
        for x in range(size_x):
            ref[x, pl.ds(0, GUARD)] = zeros8
            ref[x, pl.ds(GUARD + wide, GUARD)] = zeros8
    for x in range(size_x):
        for start, rows in parts:
            here = pl.ds(start, rows)
            g[x, here] = weight_of(c[x, here])
    for source, target in ((va, vb), (vb, v2)):
        for x in range(size_x):
            for start, rows in parts:
                here = pl.ds(start, rows)
                center, total = around(source, x, start, rows, lane, LANES, x > 0, x < last)
                target[x, here] = 0.2 * center + g[x, here] * (total + f[x, here])
    for x in range(2, last - 1):
        for start, rows in parts:
            here = pl.ds(start, rows)
            center, total = around(v2, x, start, rows, lane, LANES)
            r[x, here] = total + f[x, here] - (6.0 + c[x, here]) * center
    rows1 = size_z // 4 + 2 * GUARD
    lane1 = lanes_of(rows1)
    for x in range(1, size_x // 2 - 1):
        f1[x - 1] = 0.5 * halve_two(r, (2 * x, 2 * x + 1), lane1, GUARD, rows1)
    edges[0], edges[1], edges[2], edges[3] = va[0], va[last], vb[0], vb[last]

    sent = size_z + 2 * SENT
    first = GUARD + DEEP - SENT
    here = pl.ds(first, sent)
    lane = lanes_of(sent)
    sides = []
    for edge, second in ((0, 1), (last, last - 1)):
        center, total = around(v2, second, first, sent, lane, LANES, second != 1, second == 1)
        swept = 0.2 * center + g[second, here] * (total + f[second, here])
        source = f[edge, here]
        sides.append((va[edge, here], vb[edge, here], source + vb[second, here], source + center, source + swept))
    for k, (left, right) in enumerate(zip(*sides, strict=True)):
        a, b, rows = (to_a, to_b, pl.ds(k * sent, sent)) if k < 3 else (later_a, later_b, pl.ds((k - 3) * sent, sent))
        a[rows] = jnp.where(even_x, right, left)
        b[rows] = jnp.where(even_x, left, right)
    for copy in copies:
        copy.wait()


def outer_kernel(
    f, c, v2_in, edges, f1_in, c1_in, xa, xb,
    chunk, near_a, near_b, to_a, to_b, v_far, sides_far, f1_far, c1_far, v1_out, level2, c2_out,
    v, c_out, v1, r, f1, c1, u1, w1, u2, r2, v2, f2, c2, arrivals,
):
    even_x = lax.axis_index("gx") % 2 == 0
    size_x = f.shape[0]
    size_z = f.shape[1] - 2 * DEEP - 2 * GUARD
    wide = size_z + 2 * DEEP
    half = wide // 2
    parts = [(GUARD, half), (GUARD + half, half)]
    lane = lanes_of(half)
    zeros8 = jnp.zeros((GUARD, LANES), F32)

    copies = []

    def keep(source, target):
        copies.append(pltpu.make_async_copy(source, target, arrivals.at[len(copies)]))
        copies[-1].start()

    for x in range(size_x):
        v[x + 2] = v2_in[x]
    for ref, planes in ((v, (0, 1, size_x + 2, size_x + 3)), (v1, (0, 1))):
        for at in planes:
            ref[at, pl.ds(0, GUARD)] = zeros8
            ref[at, pl.ds(GUARD + wide, GUARD)] = zeros8
    for k in range(2):
        rows, here = pl.ds(k * wide, wide), pl.ds(GUARD, wide)
        c_out[1 - k, here] = jnp.where(even_x, xb[rows], xa[rows])
        c_out[2 + k, here] = jnp.where(even_x, xa[rows], xb[rows])
    last = size_x - 1
    for side, (edge, inward) in enumerate(((0, 1), (last, -1))):
        at = edge + 2
        beside, past = (1, 0) if side == 0 else (2, 3)
        for start, rows in parts:
            here = pl.ds(start, rows)
            v1[side, here] = weight_of(c_out[beside, here]) * edges[side, here]
        for start, rows in parts:
            here = pl.ds(start, rows)
            center, total = around(v1, side, start, rows, lane, LANES, False, False)
            v[at - inward, here] = 0.2 * center + weight_of(c_out[beside, here]) * (total + edges[2 + side, here])
            v[at - 2 * inward, here] = weight_of(c_out[past, here]) * center
            v[at, here] += weight_of(c[edge, here]) * center
        base = 0 if side == 0 else 11
        for start, rows in parts:
            here = pl.ds(start, rows)
            r[base + inward, here] = v[at - 2 * inward, here]
            for k in range(-2, 2):
                plane = at + k * inward
                center, total = around(
                    v, plane, start, rows, lane, LANES, not (side == 0 and k == -2), not (side == 1 and k == -2)
                )
                if k >= 0:
                    total = total + f[plane - 2, here]
                    weight = 6.0 + c[plane - 2, here]
                else:
                    weight = 6.0 + c_out[beside if k == -1 else past, here]
                r[base + (4 + k) * inward, here] = total - weight * center

    kept = pl.ds(GUARD + DEEP - KEEP, size_z + 2 * KEEP)
    keep(v.at[:, kept], v_far)
    keep(c_out.at[:, kept], sides_far)

    rows1 = size_z // 4 + 2 * GUARD
    size1 = size_x // 2
    off1 = 5
    here1 = pl.ds(GUARD, rows1)
    lane1 = lanes_of(rows1)
    for x in range(1, size1 - 1):
        f1[x + off1, here1] = f1_in[x - 1]
    for x, planes in (
        (-2, (1,)), (-1, (2, 3)), (0, (4, 5)), (size1 - 1, (6, 7)), (size1, (8, 9)), (size1 + 1, (10,))
    ):
        f1[x + off1, here1] = 0.5 * halve_two(r, planes, lane1, GUARD, rows1)
    for x in range(size1):
        c1[x + off1, here1] = c1_in[x, here1]
    c1[off1 - 1, here1] = 0.125 * halve_two(c_out, (0, 1), lane1, GUARD, rows1)
    c1[off1 + size1, here1] = 0.125 * halve_two(c_out, (2, 3), lane1, GUARD, rows1)
    for k in range(2):
        rows = pl.ds(2 * wide + k * rows1, rows1)
        c1[off1 - 2 - k, here1] = jnp.where(even_x, xb[rows], xa[rows])
        c1[off1 + size1 + 1 + k, here1] = jnp.where(even_x, xa[rows], xb[rows])
    low1, high1 = off1 - 2, off1 + size1 + 1
    keep(f1.at[pl.ds(off1 - 2, size1 + 4), here1], f1_far)
    keep(c1.at[pl.ds(off1 - 3, size1 + 6), here1], c1_far)
    for at in range(low1 - 1, high1 + 2):
        for ref in (u1, w1):
            ref[at, pl.ds(0, GUARD)] = zeros8
            ref[at, pl.ds(GUARD + rows1, GUARD)] = zeros8
    for at in range(low1, high1 + 1):
        u1[at, here1] = weight_of(c1[at, here1]) * f1[at, here1]
    for at in range(low1 - 1, high1 + 2):
        weight = weight_of(c1[at, here1])
        if at == low1 - 1:
            w1[at, here1] = weight * u1[at + 1, here1]
        elif at == high1 + 1:
            w1[at, here1] = weight * u1[at - 1, here1]
        else:
            center, total = around(u1, at, GUARD, rows1, lane1, 64, at > low1, at < high1)
            w1[at, here1] = 0.2 * center + weight * (total + f1[at, here1])
    for at in range(low1 - 2, high1 + 3):
        if at == low1 - 2:
            u1[at, here1] = w1[at + 1, here1]
        elif at == high1 + 2:
            u1[at, here1] = w1[at - 1, here1]
        else:
            center, total = around(w1, at, GUARD, rows1, lane1, 64, at > low1 - 1, at < high1 + 1)
            if low1 <= at <= high1:
                total = total + f1[at, here1]
            u1[at, here1] = total - (6.0 + c1[at, here1]) * center

    size2 = size_x // 4
    off2 = 5
    low2, high2 = off2 - 2, off2 + size2 + 1
    lane8, sub8 = lanes_of(8), subs_of(8)
    for ref in (v2, f2, c2, u2):
        ref[...] = jnp.zeros(ref.shape, F32)
    for x in range(-2, size2 + 2):
        own, past = halve_tiles(u1, (2 * x + off1, 2 * x + off1 + 1), lane8, sub8, rows1)
        put_tiles(f2, x + off2, 0.5 * own, 0.5 * past, lane8)
    for x in range(-1, size2 + 1):
        own, past = halve_tiles(c1, (2 * x + off1, 2 * x + off1 + 1), lane8, sub8, rows1)
        put_tiles(c2, x + off2, 0.125 * own, 0.125 * past, lane8)
    for k in range(2):
        own, past = (pl.ds(2 * wide + 2 * rows1 + 8 * (2 * k + j), 8) for j in (0, 1))
        put_tiles(
            c2, low2 - k, jnp.where(even_x, xb[own], xa[own]), jnp.where(even_x, xb[past], xa[past]), lane8
        )
        put_tiles(
            c2, high2 + k, jnp.where(even_x, xa[own], xb[own]), jnp.where(even_x, xa[past], xb[past]), lane8
        )
    for at in range(low2, high2 + 1):
        for t in (1, 2, 3):
            u2[at, t] = weight_of(c2[at, t]) * f2[at, t]
    for at in range(low2 - 1, high2 + 2):
        for t in (1, 2, 3):
            center, total = around_tile(u2, at, t, 1, lane8, sub8)
            v2[at, t] = 0.2 * center + weight_of(c2[at, t]) * (total + f2[at, t])
    for at in range(low2 - 2, high2 + 3):
        center, total = around_tile(v2, at, 2, 1, lane8, sub8)
        r2[at] = f2[at, 2] + total - (6.0 + c2[at, 2]) * center

    planes = [0.5 * pair_sums(r2[2 * k + 1] + r2[2 * k + 2], lane8, sub8) for k in range(size2 // 2 + 4)]
    planes += [
        0.125 * pair_sums(c2[off2 + 2 * k, 2] + c2[off2 + 2 * k + 1, 2], lane8, sub8) for k in range(size2 // 2)
    ]
    planes = [take_lanes(plane, 2 * (lane8 & 63)) for plane in planes]
    for k in range(2):
        even, odd = (
            jnp.where(lane8 < 64, planes[4 * k + j], planes[4 * k + j + 1]) for j in (0, 2)
        )
        tile = jnp.where((sub8 & 1) == 0, even, odd)
        for at in range(chunk.shape[0]):
            chunk[at, k] = tile

    pairs = [(v2, 2, off2 - k, off2 + size2 - 1 + k) for k in (1, 2, 3)]
    pairs += [(f2, 2, off2 - k, off2 + size2 - 1 + k) for k in (1, 2)]
    pairs += [(f1, here1, off1 + k, off1 + size1 - 1 - k) for k in (-2, -1, 0, 1, 2)]
    pairs += [(w1, here1, off1 + k, off1 + size1 - 1 - k) for k in (2, 3)]
    for k, (ref, rows, at_left, at_right) in enumerate(pairs):
        left, right = ref[at_left, rows], ref[at_right, rows]
        a, b, at = (near_a, near_b, 8 * k) if k < 5 else (to_a, to_b, (k - 5) * rows1)
        target = pl.ds(at, left.shape[0])
        a[target] = jnp.where(even_x, right, left)
        b[target] = jnp.where(even_x, left, right)

    for at in range(size2 + 6):
        level2[at] = v2[at + 2, 2]
    for at in range(size2 + 4):
        level2[size2 + 6 + at] = f2[at + 3, 2]
    c2_out[...] = c2[pl.ds(2, size2 + 6), pl.ds(1, 3)]
    v1_out[0] = w1[off1 - 3, here1]
    v1_out[1] = w1[off1 + size1 + 2, here1]
    for copy in copies:
        copy.wait()


def meet_kernel(level2, xa, xb, level1_a, level1_b, later_a, later_b, _, __, ___, own, to_a, to_b):
    even_x = lax.axis_index("gx") % 2 == 0
    size2 = own.shape[0] // 2
    planes = [level2[3 + x] for x in range(size2)] + [level2[size2 + 8 + x] for x in range(size2)]
    for k, (base, step) in enumerate(((0, 0), (0, 1), (0, 2), (size2, 0), (size2, 1))):
        rows = pl.ds(8 * k, 8)
        left = jnp.where(even_x, xb[rows], xa[rows])
        right = jnp.where(even_x, xa[rows], xb[rows])
        planes[base + step] = planes[base + step] + left
        planes[base + size2 - 1 - step] = planes[base + size2 - 1 - step] + right
    for k, plane in enumerate(planes):
        own[k] = plane
    size = level1_a.shape[0]
    for first, second, target in ((level1_a, later_a, to_a), (level1_b, later_b, to_b)):
        target[pl.ds(0, size)] = first[...]
        target[pl.ds(size, second.shape[0])] = second[...]


def past_tiles(za, zb, k, odd_z, lane):
    below = jnp.where(odd_z, za[k], zb[k])
    above = jnp.where(odd_z, zb[k], za[k])
    return jnp.where(lane >= 96, below, jnp.where(lane < 32, above, 0.0))


def side_kernel(own, za, zb, to_a, to_b):
    odd_z = lax.axis_index("gc") == 1
    even_x = lax.axis_index("gx") % 2 == 0
    size2 = own.shape[0] // 2
    lane = lanes_of(8)
    tiles = [(own[k], past_tiles(za, zb, k, odd_z, lane)) for k in range(2 * size2)]
    at = 0
    for base, count in ((0, size2), (size2, size2 - 1)):
        for k in range(count):
            for left, right in zip(tiles[base + k], tiles[base + size2 - 1 - k], strict=True):
                to_a[at] = jnp.where(even_x, right, left)
                to_b[at] = jnp.where(even_x, left, right)
                at += 1


def loop(count, body):
    if count <= 16:
        for i in range(count):
            body(i)
    else:
        lax.fori_loop(0, count, lambda i, _: (body(i), None)[1], None)


def coarse_kernel(
    nx, nz, own, other, inverse_far, _,
    window3, e_out,
    v3, f3, g3, c3, u3, turned, flat, inverse, arrivals,
):
    core = lax.axis_index("gc")
    ny = nz // 2
    lane, sub = lanes_of(8), subs_of(8)
    copies = []
    piece = inverse.shape[0] // 4
    for k in range(4):
        rows = pl.ds(k * piece, piece)
        copies.append(pltpu.make_async_copy(inverse_far.at[rows], inverse.at[rows], arrivals.at[k]))
        copies[k].start()
    for ref in (v3, f3, g3, u3):
        ref[...] = jnp.zeros(ref.shape, F32)

    def collect(at):
        for y in range(ny):
            for source, t in ((own, 1 + 2 * y + core), (other, 2 + 2 * y - core)):
                planes = []
                for k in range(2):
                    tile = source[at * ny + y, k]
                    even = jnp.where((sub & 1) == 0, tile, pltpu.roll(tile, 1, 0))
                    odd = jnp.where((sub & 1) == 1, tile, pltpu.roll(tile, 7, 0))
                    planes += [take_lanes(part, (lane >> 1) + 64 * j) for part in (even, odd) for j in (0, 1)]
                for k in range(6):
                    f3[2 * at + 2 + k, t] += planes[k]
                for k in range(2):
                    c3[2 * at + 4 + k, t] = planes[6 + k]

    loop(nx, collect)

    def third(at):
        for k in range(2):
            x = 4 + 2 * at + k
            for t in range(1, nz + 1):
                g3[x, t] = RELAX_WEIGHT / (6.0 + c3[x, t])
                u3[x, t] = g3[x, t] * f3[x, t]

    loop(nx, third)

    def fourth(at):
        for k in range(2):
            x = 4 + 2 * at + k
            for t in range(1, nz + 1):
                center, total = around_tile(u3, x, t, 2, lane, sub)
                v3[x, t] = 0.2 * center + g3[x, t] * (total + f3[x, t])

    loop(nx, fourth)

    step_x = 2 * nx // COARSE
    group = nz // 4

    for t in range(1, nz + 1):
        rows = []
        for xc in range(COARSE):
            total = 0.0
            for k in range(step_x):
                x = 4 + xc * step_x + k
                center, beside = around_tile(v3, x, t, 2, lane, sub)
                total += f3[x, t] + beside - (6.0 + c3[x, t]) * center
            rows.append(jnp.sum(total, axis=0, keepdims=True))
        block = 0.125 * jnp.concatenate(rows, axis=0)
        spread = block
        for k in range(1, group):
            spread = spread + pltpu.roll(block, LANES - 32 * k, 1)
        tall = jnp.concatenate([spread, jnp.zeros((LANES - COARSE, LANES), F32)], axis=0)
        turned[...] = tall.T
        line = jnp.zeros((8, LANES), F32)
        for k in range(8):
            piece = pltpu.roll(turned[pl.ds(2 * k, 8, stride=16), :], 16 * k, 1) if k else turned[pl.ds(0, 8, stride=16), :]
            line = jnp.where((lane >= 16 * k) & (lane < 16 * k + 16), piece, line)
        count = 4 // group
        for q in range(count):
            at = 2 * ((t - 1) * count + q)
            flat[at : at + 2] = line[2 * group * q : 2 * group * q + 2]

    at_x = lax.axis_index("gx")
    at_z = 2 * lax.axis_index("gy") + core
    for k, ref in enumerate((v3, f3, g3)):
        for t in range(3):
            window3[k, :, t] = ref[pl.ds(2 * at_x, 10), at_z + t]

    for copy in copies:
        copy.wait()
    total = None
    for t in range(inverse.shape[1] // LANES):
        piece = inverse[:, t * LANES : (t + 1) * LANES] * flat[t : t + 1]
        total = piece if total is None else total + piece
    column = jnp.sum(total, axis=1, keepdims=True)
    copies = e_out.shape[0]
    width = -(-copies // LANES) * LANES
    e_out[...] = jnp.broadcast_to(column, (inverse.shape[0], width)).T[:copies]


def top_level(nx, nz, e, window3, u3, lifted3, w3, turned):
    at_x = lax.axis_index("gx")
    at_z = 2 * lax.axis_index("gy") + lax.axis_index("gc")
    lane, sub = lanes_of(8), subs_of(8)
    step_x = 2 * nx // COARSE
    group = nz // 4

    for ref in (lifted3, u3, w3):
        ref[...] = jnp.zeros(ref.shape, F32)
    for t in range(1, nz + 1):
        pieces = []
        for q in range(4):
            at = 2 * (((t - 1) * 4 + q) // group)
            pieces.append(e[at : at + 2])
        rows = jnp.concatenate(pieces, axis=0)
        for k in range(8):
            piece = pltpu.roll(rows, LANES - 16 * k, 1) if k else rows
            turned[pl.ds(2 * k, 8, stride=16), :] = piece
            turned[pl.ds(2 * k + 1, 8, stride=16), :] = piece
        lifted = turned[...].T
        for xc in range(COARSE):
            tile = jnp.broadcast_to(lifted[xc : xc + 1], (8, LANES))
            for k in range(step_x):
                lifted3[4 + xc * step_x + k, t] = tile
    for x in range(10):
        for t in range(3):
            u3[x, t + 1] = window3[0, x, t] + lifted3[2 * at_x + x, at_z + t]
    for source, target, margin in ((u3, w3, 1), (w3, u3, 2)):
        for x in range(margin, 10 - margin):
            for t in range(3):
                center, total = around_tile(source, x, t + 1, 2, lane, sub)
                target[x, t + 1] = 0.2 * center + window3[2, x, t] * (total + window3[1, x, t])


def up_kernel(
    nx, nz, e, window3, own2, za, zb, sides_a, sides_b, c2, v_far, f_far, c_far, sides_far, f1_far, c1_far, v1_in, xa, xb, later_a, later_b,
    pressure, residual,
    u3, lifted3, w3, turned, u2, w2, f2, f1, c1, u1, w1, lift1, ua, ub, g, lift0, before_in, after_in, sources, v_in, f_in, c_in, c_sides, f1_in, c1_in, arrivals,
):
    even_x = lax.axis_index("gx") % 2 == 0
    lane, sub = lanes_of(8), subs_of(8)
    zeros8 = jnp.zeros((GUARD, LANES), F32)
    pairs = (f1_far, f1_in), (c1_far, c1_in), (sides_far, c_sides), (c_far, c_in), (v_far, v_in), (f_far, f_in)
    copies = [pltpu.make_async_copy(*pair, arrivals.at[k]) for k, pair in enumerate(pairs)]
    for copy in copies:
        copy.start()
    for ref in (u2, w2, f2):
        ref[...] = jnp.zeros(ref.shape, F32)

    top_level(nx, nz, e, window3, u3, lifted3, w3, turned)

    odd_z = lax.axis_index("gc") == 1
    size2 = own2.shape[0] // 2
    planes2 = size2 + 8
    for k in range(2 * size2):
        target = u2 if k < size2 else f2
        put_tiles(target, 4 + k % size2, own2[k], past_tiles(za, zb, k, odd_z, lane), lane)
    at = 0
    for target, count in ((u2, size2), (f2, size2 - 1)):
        for k in range(count):
            left = [jnp.where(even_x, sides_b[at + j], sides_a[at + j]) for j in (0, 1)]
            right = [jnp.where(even_x, sides_a[at + j], sides_b[at + j]) for j in (0, 1)]
            put_tiles(target, 3 - k, *left, lane)
            put_tiles(target, 4 + size2 + k, *right, lane)
            at += 2
    for x in range(planes2):
        for t in (1, 2, 3):
            u2[x, t] += u3[2 + x // 2, t]
    for source, target, margin in ((u2, w2, 1), (w2, u2, 2)):
        for x in range(margin, planes2 - margin):
            for t in (1, 2, 3):
                center, total = around_tile(source, x, t, 1, lane, sub)
                target[x, t] = 0.2 * center + weight_of(c2[x - 1, t - 1]) * (total + f2[x, t])

    rows1 = f1_in.shape[1]
    size1 = 2 * size2
    off1 = 4
    here1 = pl.ds(GUARD, rows1)
    lane1 = lanes_of(rows1)
    side = lane >> 6
    fine = (lane & 63) >> 1
    for x in range(2, planes2 - 2):
        below, middle, above = u2[x, 1], u2[x, 2], u2[x, 3]
        index = [(((2 * side + q) & 3) << 5) + fine for q in (-1, 0, 1, 2)]
        tiles = [
            jnp.where(side == 0, take_lanes(below, index[0]), take_lanes(middle, index[0]))[4:],
            take_lanes(middle, index[1]),
            take_lanes(middle, index[2]),
            jnp.where(side == 0, take_lanes(middle, index[3]), take_lanes(above, index[3]))[:4],
        ]
        start = 0
        for tile in tiles:
            count = tile.shape[0]
            lift1[x - 2, pl.ds(start, count, stride=2), :] = tile
            lift1[x - 2, pl.ds(start + 1, count, stride=2), :] = tile
            start += 2 * count

    kept = v_in.shape[1]

    def arrived(start, rows, a=xa, b=xb):
        a, b = a[pl.ds(start, rows)], b[pl.ds(start, rows)]
        return jnp.where(even_x, b, a), jnp.where(even_x, a, b)

    copies[0].wait()
    copies[1].wait()
    for x in range(-2, size1 + 2):
        f1[x + off1, here1] = f1_in[x + 2]
    for x in range(-3, size1 + 3):
        c1[x + off1, here1] = weight_of(c1_in[x + 3])
    for k in range(7):
        left, right = arrived(k * rows1, rows1, later_a, later_b)
        if k < 4:
            f1[off1 + 1 - k, here1] += left
            f1[off1 + size1 - 2 + k, here1] += right
        elif k == 4:
            f1[off1 - 3, here1] = left
            f1[off1 + size1 + 2, here1] = right
        else:
            w1[off1 + 2 - k, here1] = left + v1_in[0] if k == 5 else left
            w1[off1 + size1 - 3 + k, here1] = right + v1_in[1] if k == 5 else right
    planes1 = size1 + 8
    for ref in (u1, w1):
        for at in range(planes1):
            ref[at, pl.ds(0, GUARD)] = zeros8
            ref[at, pl.ds(GUARD + rows1, GUARD)] = zeros8
    for at in range(1, planes1 - 1):
        u1[at, here1] = c1[at, here1] * f1[at, here1]
    for at in range(planes1):
        value = w1[at, here1]
        if 2 <= at < planes1 - 2:
            center, total = around(u1, at, GUARD, rows1, lane1, 64)
            value = 0.2 * center + c1[at, here1] * (total + f1[at, here1])
        w1[at, here1] = value + lift1[at // 2]
    for source, target, margin in ((w1, u1, 1), (u1, w1, 2)):
        for at in range(margin, planes1 - margin):
            center, total = around(source, at, GUARD, rows1, lane1, 64)
            target[at, here1] = 0.2 * center + c1[at, here1] * (total + f1[at, here1])

    size_x = f_in.shape[0]
    size_z = kept - 2 * KEEP
    short = kept // 4
    index = lanes_of(short) >> 1
    for x in range(-2, size1 + 2):
        for part in range(2):
            source = w1[x + off1, pl.ds(GUARD + (4 if part == 0 else 8), short)]
            tile = take_lanes(source, index + 64 * part)
            lift0[x + 2, pl.ds(part * 2 * short, short, stride=2), :] = tile
            lift0[x + 2, pl.ds(part * 2 * short + 1, short, stride=2), :] = tile

    off = 3
    last = size_x + off - 1
    here = pl.ds(GUARD, kept)
    for ref in (ua, ub):
        for at in range(size_x + 6):
            ref[at, pl.ds(0, GUARD)] = zeros8
            ref[at, pl.ds(GUARD + kept, GUARD)] = zeros8
    for copy in copies[2:]:
        copy.wait()
    shift = -GUARD
    for x in range(-3, size_x + 3):
        value = lift0[(x + 4) // 2]
        if -2 <= x <= size_x + 1:
            value = value + v_in[x + 2, pl.ds(GUARD + shift, kept)]
        ua[x + off, here] = value
    half = kept // 2
    parts = [(GUARD, half), (GUARD + half, half)]
    laneh = lanes_of(half)
    beyond = {-2: 0, -1: 1, size_x: 2, size_x + 1: 3}
    for x in range(-2, size_x + 2):
        for start, rows in parts:
            at = pl.ds(start + shift, rows)
            g[x + 2, pl.ds(start, rows)] = weight_of(c_sides[beyond[x], at] if x in beyond else c_in[x, at])

    sent = size_z + 2 * SENT
    begin = GUARD + KEEP - SENT
    taken = pl.ds(begin, sent)
    lane_s = lanes_of(sent)
    for ref in (before_in, after_in, sources):
        ref[...] = jnp.zeros(ref.shape, F32)
    messages = [arrived(k * sent, sent) for k in range(3)]
    messages += [arrived(7 * rows1 + k * sent, sent, later_a, later_b) for k in range(2)]
    for side, (edge, inward) in enumerate(((off, 1), (last, -1))):
        before, after, source0, source1, source2 = (message[side] for message in messages)
        before_in[side, taken] = g[edge - 1, taken] * before
        after_in[side, taken] = after
        sources[side, taken] = source1
        sources[2 + side, taken] = source2
        center, total = around(before_in, side, begin, sent, lane_s, LANES, False, False)
        ua[edge, taken] += 0.2 * center + g[edge - 1, taken] * (total + after)
        ua[edge + inward, taken] += g[edge + inward - 1, taken] * center
        _, total = around(after_in, side, begin, sent, lane_s, LANES, False, False)
        ua[edge - inward, taken] += 0.2 * after + g[edge - inward - 1, taken] * (total + source0 + center)

    for sweep, (origin, target) in enumerate(((ua, ub), (ub, ua))):
        for at in range(1 + sweep, size_x + 5 - sweep):
            for start, rows in parts:
                center, total = around(origin, at, start, rows, laneh, LANES)
                x = at - off
                if 0 <= x < size_x:
                    total = total + f_in[x, pl.ds(start + shift, rows)]
                elif x in (-1, size_x):
                    total = total + sources[2 * sweep + (x > 0), pl.ds(start, rows)]
                target[at, pl.ds(start, rows)] = 0.2 * center + g[at - 1, pl.ds(start, rows)] * total
    lane_z = lanes_of(size_z)
    own = GUARD + KEEP
    for x in range(size_x):
        center, total = around(ua, x + off, own, size_z, lane_z, LANES)
        mine = pl.ds(own + shift, size_z)
        total = total + f_in[x, mine]
        pressure[x] = center.T
        residual[x] = (total - (6.0 + c_in[x, mine]) * center).T


def pairs_of(count):
    even = [(i, i ^ 1) for i in range(count)]
    odd = [(i, ((i - 1) ^ 1) + 1) for i in range(1, count - 1)]
    return even, odd


def gather(copies, axes):
    always = lax.optimization_barrier(jnp.int32(1)) > 0
    return lax.cond(always, lambda x: lax.all_to_all(x, axes, 0, 0, tiled=True), lambda x: x, copies)


def local(nx, nz, right_side, reaction, initial, coarse_inverse):
    size_x, _, size_z = right_side.shape
    size1, size2 = size_x // 2, size_x // 4
    wide, kept, sent = (size_z + 2 * rows for rows in (DEEP, KEEP, SENT))
    deep = wide + 2 * GUARD
    rows1 = size_z // 4 + 2 * GUARD
    brick = (size_x, size_z, LANES)
    padded = (size_x, deep, LANES)
    padded1 = (size1, rows1 + 2 * GUARD, LANES)
    slab = (size_x, DEEP, LANES)
    c, f, mza, mzb = call(
        turn_kernel, "turn", (brick, brick, (2, *slab), (2, *slab)), (reaction, right_side),
        [(2, *right_side.shape)], far_args=(0, 1), copies=8,
    )
    even_z, odd_z = pairs_of(nz)
    za = lax.ppermute(mza, ("gy", "gc"), even_z)
    zb = lax.ppermute(mzb, ("gy", "gc"), odd_z)
    v, mya, myb = call(turn_again_kernel, "turn_again", (brick, slab, slab), (initial, mza))
    ya = lax.ppermute(mya, ("gy", "gc"), even_z)
    yb = lax.ppermute(myb, ("gy", "gc"), odd_z)

    message = (2 * wide + 2 * rows1 + 32, LANES)
    mxa, mxb, c, c1 = call(
        coefficient_kernel, "coefficients", (message, message, padded, padded1), (c, za, zb)
    )
    even_x, odd_x = pairs_of(nx)
    xa = lax.ppermute(mxa, "gx", even_x)
    xb = lax.ppermute(mxb, "gx", odd_x)

    margin, later = (3 * sent, LANES), (2 * sent, LANES)
    held = (size_x, kept, LANES)
    f, v, edges, f1, mua, mub, mla, mlb, f_far, c_far = call(
        inner_kernel, "inner",
        (padded, padded, (4, deep, LANES), (size1 - 2, rows1, LANES), margin, margin, later, later, held, held),
        (f, v, c, za, zb, ya, yb),
        [padded] * 4, far_outs=(8, 9), copies=2,
    )
    ua = lax.ppermute(mua, "gx", even_x)
    ub = lax.ppermute(mub, "gx", odd_x)

    box2 = (size2 + 10, 5, 8, LANES)
    near, level1 = (40, LANES), (7 * rows1, LANES)
    sides0, sides1 = (4, deep, LANES), (2, rows1, LANES)
    parts1 = (size1 + 4, rows1, LANES), (size1 + 6, rows1, LANES)
    field0 = (size_x + 4, deep, LANES)
    field1 = (size1 + 10, rows1 + 2 * GUARD, LANES)
    chunk, mna, mnb, m1a, m1b, v, c_sides, f1, c1, v1, level2, c2 = call(
        outer_kernel, "outer",
        (
            (nx * nz // 2, 2, 8, LANES), near, near, level1, level1,
            (size_x + 4, kept, LANES), (4, kept, LANES), *parts1, sides1, (2 * size2 + 10, 8, LANES), (size2 + 6, 3, 8, LANES),
        ),
        (f, c, v, edges, f1, c1, xa, xb),
        [
            field0, sides0, (2, deep, LANES), (12, deep, LANES), field1, field1, field1, field1,
            box2, (size2 + 10, 8, LANES), box2, box2, box2,
        ],
        far_outs=range(5, 9), copies=4,
    )
    na = lax.ppermute(mna, "gx", even_x)
    nb = lax.ppermute(mnb, "gx", odd_x)
    own = gather(chunk, ("gx", "gy"))
    both = (7 * rows1 + 2 * sent, LANES)
    own2, mla, mlb = call(
        meet_kernel, "meet", ((2 * size2, 8, LANES), both, both), (level2, na, nb, m1a, m1b, mla, mlb, ua, ub, own)
    )
    la = lax.ppermute(mla, "gx", even_x)
    lb = lax.ppermute(mlb, "gx", odd_x)
    other = lax.ppermute(own, "gc", [(0, 1), (1, 0)])
    z2a = lax.ppermute(own2, ("gy", "gc"), even_z)
    z2b = lax.ppermute(own2, ("gy", "gc"), odd_z)
    sides = (4 * size2 - 2, 8, LANES)
    msa, msb = call(side_kernel, "sides", (sides, sides), (own2, z2a, z2b))
    sa = lax.ppermute(msa, "gx", even_x)
    sb = lax.ppermute(msb, "gx", odd_x)

    grid3 = (2 * nx + 8, nz + 2, 8, LANES)
    rows = coarse_inverse.shape[0]
    window3, e = call(
        functools.partial(coarse_kernel, nx, nz), "coarse",
        ((3, 10, 3, 8, LANES), (nx * nz, rows)),
        (own, other, coarse_inverse, msa),
        [*[grid3] * 5, (LANES, LANES), (COARSE**3 // LANES, LANES), coarse_inverse.shape],
        far_args=(2,), copies=4,
    )
    e = gather(e, ("gx", "gy", "gc")).reshape(COARSE**3 // LANES, LANES)

    near2 = (size2 + 8, 5, 8, LANES)
    box3 = (10, 5, 8, LANES)
    box = (size_x + 6, kept + 2 * GUARD, LANES)
    return call(
        functools.partial(up_kernel, nx, nz), "up",
        ((size_x, LANES, size_z), (size_x, LANES, size_z)),
        (e, window3, own2, z2a, z2b, sa, sb, c2, v, f_far, c_far, c_sides, f1, c1, v1, ua, ub, la, lb),
        [
            box3, grid3, box3, (LANES, LANES), near2, near2, near2,
            field1, field1, field1, field1, (size2 + 4, rows1, LANES),
            box, box, box, (size1 + 4, kept, LANES), *[(2, kept + 2 * GUARD, LANES)] * 2, (4, kept + 2 * GUARD, LANES),
            (size_x + 4, kept, LANES), held, held, (4, kept, LANES), *parts1,
        ],
        far_args=range(8, 14), copies=6, results=True,
    )


def solution(mesh):
    nx, nz = mesh.shape["gx"], mesh.shape["gz"]
    fine = Mesh(mesh.devices.reshape(nx, nz // 2, 2), ("gx", "gy", "gc"))
    brick = P("gx", None, ("gy", "gc"))
    return jax.shard_map(
        lambda *args: tuple(local(nx, nz, *args)),
        mesh=fine,
        in_specs=(brick, brick, brick, P(("gx", "gy", "gc"), None)),
        out_specs=(brick, brick),
        check_vma=False,
    )
```

```python
import functools
import math

import jax
import jax.numpy as jnp
from jax import lax
from jax.experimental import pallas as pl
from jax.experimental.pallas import tpu as pltpu
from jax.sharding import Mesh
from jax.sharding import PartitionSpec as P

COARSE = 16
RELAX_WEIGHT = 0.8
F32 = jnp.float32
LANES = 128
DEEP = 16
KEEP = 8
SENT = 4
GUARD = 8
EARLY = 2
MIB = 1 << 20


def lanes_of(rows):
    return lax.broadcasted_iota(jnp.int32, (rows, LANES), 1)


def subs_of(rows):
    return lax.broadcasted_iota(jnp.int32, (rows, LANES), 0)


def take_lanes(values, index):
    return jnp.take_along_axis(values, index, axis=1, mode="promise_in_bounds")


def beside_lanes(values, lane, width, step):
    place = lane & (width - 1)
    low = jnp.where(place >= step, pltpu.roll(values, step, 1), 0.0)
    high = jnp.where(place < width - step, pltpu.roll(values, LANES - step, 1), 0.0)
    return low + high


def weight_of(c):
    return jnp.where(c > 0.0, RELAX_WEIGHT / (6.0 + c), 0.0)


def around(ref, at, start, rows, lane, width, lower=True, upper=True):
    center = ref[at, pl.ds(start, rows)]
    total = ref[at, pl.ds(start - 1, rows)] + ref[at, pl.ds(start + 1, rows)]
    total = total + beside_lanes(center, lane, width, 1)
    if lower:
        total = total + ref[at - 1, pl.ds(start, rows)]
    if upper:
        total = total + ref[at + 1, pl.ds(start, rows)]
    return center, total


def halve_two(ref, planes, lane, first, rows):
    index = 2 * (lane & 63)

    def part(start):
        total = None
        for at in planes:
            for odd in (0, 1):
                piece = ref[at, pl.ds(start + odd, rows, stride=2), :]
                total = piece if total is None else total + piece
        total = total + pltpu.roll(total, LANES - 1, 1)
        return take_lanes(total, index)

    return jnp.where(lane < 64, part(first), part(first + 64))


def halve_four(ref, planes, lane8, first):
    total = None
    for at in planes:
        for odd in (0, 1):
            piece = ref[at, pl.ds(first + odd, 16, stride=2), :]
            total = piece if total is None else total + piece
    total = total + pltpu.roll(total, LANES - 1, 1)
    index = (lane8 & 64) + 2 * (lane8 & 31)
    return jnp.where((lane8 & 32) == 0, take_lanes(total[:8], index), take_lanes(total[8:], index))


def around_tile(ref, x, t, step, lane, sub):
    center = ref[x, t]
    total = ref[x - 1, t] + ref[x + 1, t] + beside_lanes(center, lane, 32, step)
    after = pltpu.roll(jnp.where(lane < 32, ref[x, t + 1], center), LANES - 32, 1)
    total = total + pltpu.roll(jnp.where(sub < step, after, center), 8 - step, 0)
    before = pltpu.roll(jnp.where(lane >= 96, ref[x, t - 1], center), 32, 1)
    total = total + pltpu.roll(jnp.where(sub >= 8 - step, before, center), step, 0)
    return center, total


def pair_sums(values, lane, sub):
    partner = jnp.where((lane & 1) == 0, pltpu.roll(values, LANES - 1, 1), pltpu.roll(values, 1, 1))
    values = values + partner
    partner = jnp.where((sub & 1) == 0, pltpu.roll(values, 7, 0), pltpu.roll(values, 1, 0))
    return values + partner


def halve_tiles(ref, planes, lane, sub, beyond):
    def edge(start):
        total = None
        for at in planes:
            for odd in (0, 1):
                piece = ref[at, pl.ds(start + odd, 4, stride=2), :]
                total = piece if total is None else total + piece
        return total

    past = jnp.concatenate([edge(beyond), edge(GUARD)], axis=0)
    past = past + pltpu.roll(past, LANES - 1, 1)
    past = take_lanes(past, jnp.where(sub < 4, 64, 0) + 2 * (lane & 31))
    kept = ((sub < 4) & (lane < 32)) | ((sub >= 4) & (lane >= 96))
    return halve_four(ref, planes, lane, 2 * GUARD), jnp.where(kept, past, 0.0)


def put_tiles(target, at, own, past, lane):
    target[at, 2] = own
    target[at, 1] = jnp.where(lane >= 96, past, 0.0)
    target[at, 3] = jnp.where(lane < 32, past, 0.0)


def call(kernel, name, outs, args, scratch=(), far_args=(), far_outs=(), copies=0, results=False, micros=1):
    limit = sum(4 * math.prod(s) for s in scratch) + 6 * MIB
    spaces_in = [pltpu.HBM if k in far_args else pltpu.VMEM for k in range(len(args))]
    spaces_out = [pltpu.HBM if k in far_outs else pltpu.VMEM for k in range(len(outs))]
    spaces_in = [pltpu.SMEM if a.dtype == jnp.int32 else space for a, space in zip(args, spaces_in, strict=True)]
    args = [
        a if space == pltpu.SMEM else pltpu.with_memory_space_constraint(a, space)
        for a, space in zip(args, spaces_in, strict=True)
    ]
    return pl.pallas_call(
        kernel,
        out_shape=[
            jax.ShapeDtypeStruct(s, F32) if results else space(s, F32)
            for s, space in zip(outs, spaces_out, strict=True)
        ],
        in_specs=[pl.BlockSpec(memory_space=space) for space in spaces_in],
        out_specs=[pl.BlockSpec(memory_space=space) for space in spaces_out],
        scratch_shapes=[pltpu.VMEM(s, F32) for s in scratch] + [pltpu.SemaphoreType.DMA((copies,))] * (copies > 0),
        compiler_params=pltpu.CompilerParams(vmem_limit_bytes=limit),
        cost_estimate=pl.CostEstimate(flops=0, bytes_accessed=3_000_000 * micros, transcendentals=0),
        name=name,
    )(*args)


def edge_rows(source, to_a, to_b):
    odd = lax.axis_index("gc")
    far = source.shape[1] - DEEP
    to_a[...] = source[:, pl.ds(pl.multiple_of((1 - odd) * far, DEEP), DEEP), :]
    to_b[...] = source[:, pl.ds(pl.multiple_of(odd * far, DEEP), DEEP), :]


def turn_kernel(*refs):
    *refs, held, arrivals = refs
    count = (len(refs) - 3) // 2
    sources, targets, (to_a, to_b) = refs[:count], refs[count + 1 : 2 * count + 1], refs[2 * count + 1 :]
    piece = targets[0].shape[0] // 4
    copies = []
    for which, source in enumerate(sources):
        for k in range(4):
            planes = pl.ds(k * piece, piece)
            copies.append(
                pltpu.make_async_copy(source.at[planes], held.at[which, planes], arrivals.at[4 * which + k])
            )
            copies[-1].start()
    for which, target in enumerate(targets):
        for k in range(4):
            copies[4 * which + k].wait()
            for x in range(k * piece, (k + 1) * piece):
                target[x] = held[which, x].T
        edge_rows(target, to_a.at[which], to_b.at[which])


def turn_again_kernel(v_in, _, v_out, to_a, to_b):
    for x in range(v_out.shape[0]):
        v_out[x] = v_in[x].T
    edge_rows(v_out, to_a, to_b)


def fill_rows(target, at, own, low, high):
    rows = own.shape[0]
    target[at, pl.ds(GUARD, DEEP)] = low
    target[at, pl.ds(GUARD + DEEP, rows)] = own
    target[at, pl.ds(GUARD + DEEP + rows, DEEP)] = high


def coefficient_kernel(c_in, za, zb, to_a, to_b, padded, c1):
    odd_z = lax.axis_index("gc") == 1
    even_x = lax.axis_index("gx") % 2 == 0
    size_x, size_z, _ = c_in.shape
    wide = pl.ds(GUARD, size_z + 2 * DEEP)
    rows1 = size_z // 4 + 2 * GUARD
    here1 = pl.ds(GUARD, rows1)
    lane, lane8, sub8 = lanes_of(rows1), lanes_of(8), subs_of(8)
    for x in range(size_x):
        low = jnp.where(odd_z, za[0, x], zb[0, x])
        high = jnp.where(odd_z, zb[0, x], za[0, x])
        fill_rows(padded, x, c_in[x], low, high)
    for x in range(size_x // 2):
        c1[x, here1] = 0.125 * halve_two(padded, (2 * x, 2 * x + 1), lane, GUARD, rows1)
    sides = []
    for order, order1 in ((range(size_x), range(8)), (range(size_x - 1, -1, -1), range(7, -1, -1))):
        tiles = []
        for k in (2, 4):
            tiles += [0.125 * tile for tile in halve_tiles(c1, order1[k : k + 2], lane8, sub8, rows1)]
        sides.append(
            [padded[order[0], wide], padded[order[1], wide], c1[order1[1], here1], c1[order1[2], here1], *tiles]
        )
    start = 0
    for left, right in zip(*sides, strict=True):
        rows = pl.ds(start, left.shape[0])
        to_a[rows] = jnp.where(even_x, right, left)
        to_b[rows] = jnp.where(even_x, left, right)
        start += left.shape[0]


def inner_kernel(
    f_in, v_in, c, za, zb, ya, yb,
    f, v2, edges, f1, to_a, to_b, later_a, later_b, f_ends, c_ends,
    va, vb, g, r,
):
    odd_z = lax.axis_index("gc") == 1
    even_x = lax.axis_index("gx") % 2 == 0
    size_x, size_z, _ = f_in.shape
    wide = size_z + 2 * DEEP
    half = wide // 2
    parts = [(GUARD, half), (GUARD + half, half)]
    last = size_x - 1
    lane = lanes_of(half)
    zeros8 = jnp.zeros((GUARD, LANES), F32)

    for source, target, a, b in ((f_in, f, za.at[1], zb.at[1]), (v_in, va, ya, yb)):
        for x in range(size_x):
            low = jnp.where(odd_z, a[x], b[x])
            high = jnp.where(odd_z, b[x], a[x])
            fill_rows(target, x, source[x], low, high)
    for ref in (va, vb, v2):
        for x in range(size_x):
            ref[x, pl.ds(0, GUARD)] = zeros8
            ref[x, pl.ds(GUARD + wide, GUARD)] = zeros8
    for x in range(size_x):
        for start, rows in parts:
            here = pl.ds(start, rows)
            g[x, here] = weight_of(c[x, here])
    for source, target in ((va, vb), (vb, v2)):
        for x in range(size_x):
            for start, rows in parts:
                here = pl.ds(start, rows)
                center, total = around(source, x, start, rows, lane, LANES, x > 0, x < last)
                target[x, here] = 0.2 * center + g[x, here] * (total + f[x, here])
    for x in range(2, last - 1):
        for start, rows in parts:
            here = pl.ds(start, rows)
            center, total = around(v2, x, start, rows, lane, LANES)
            r[x, here] = total + f[x, here] - (6.0 + c[x, here]) * center
    rows1 = size_z // 4 + 2 * GUARD
    lane1 = lanes_of(rows1)
    for x in range(1, size_x // 2 - 1):
        f1[x - 1] = 0.5 * halve_two(r, (2 * x, 2 * x + 1), lane1, GUARD, rows1)
    edges[0], edges[1], edges[2], edges[3] = va[0], va[last], vb[0], vb[last]

    sent = size_z + 2 * SENT
    first = GUARD + DEEP - SENT
    here = pl.ds(first, sent)
    lane = lanes_of(sent)
    sides = []
    for edge, second in ((0, 1), (last, last - 1)):
        center, total = around(v2, second, first, sent, lane, LANES, second != 1, second == 1)
        swept = 0.2 * center + g[second, here] * (total + f[second, here])
        source = f[edge, here]
        sides.append((va[edge, here], vb[edge, here], source + vb[second, here], source + center, source + swept))
    for k, (left, right) in enumerate(zip(*sides, strict=True)):
        a, b, rows = (to_a, to_b, pl.ds(k * sent, sent)) if k < EARLY else (later_a, later_b, pl.ds((k - EARLY) * sent, sent))
        a[rows] = jnp.where(even_x, right, left)
        b[rows] = jnp.where(even_x, left, right)
    for source, target in ((f, f_ends), (c, c_ends)):
        target[:, pl.ds(0, KEEP)] = source[:, pl.ds(GUARD + DEEP - KEEP, KEEP)]
        target[:, pl.ds(KEEP, KEEP)] = source[:, pl.ds(GUARD + DEEP + size_z, KEEP)]


def outer_kernel(
    f, c, v2_in, edges, f1_in, c1_in, xa, xb,
    chunk, near_a, near_b, to_a, to_b, v_far, sides_far, f1_far, c1_far, v1_out, level2, c2_out,
    v, c_out, v1, r, f1, c1, u1, w1, u2, r2, v2, f2, c2, arrivals,
):
    even_x = lax.axis_index("gx") % 2 == 0
    size_x = f.shape[0]
    size_z = f.shape[1] - 2 * DEEP - 2 * GUARD
    wide = size_z + 2 * DEEP
    half = wide // 2
    parts = [(GUARD, half), (GUARD + half, half)]
    lane = lanes_of(half)
    zeros8 = jnp.zeros((GUARD, LANES), F32)

    copies = []

    def keep(source, target):
        copies.append(pltpu.make_async_copy(source, target, arrivals.at[len(copies)]))
        copies[-1].start()

    kept = pl.ds(GUARD + DEEP - KEEP, size_z + 2 * KEEP)
    keep(v2_in.at[pl.ds(1, size_x - 2), kept], v_far.at[pl.ds(3, size_x - 2)])

    for x in range(size_x):
        v[x + 2] = v2_in[x]
    for ref, planes in ((v, (0, 1, size_x + 2, size_x + 3)), (v1, (0, 1))):
        for at in planes:
            ref[at, pl.ds(0, GUARD)] = zeros8
            ref[at, pl.ds(GUARD + wide, GUARD)] = zeros8
    for k in range(2):
        rows, here = pl.ds(k * wide, wide), pl.ds(GUARD, wide)
        c_out[1 - k, here] = jnp.where(even_x, xb[rows], xa[rows])
        c_out[2 + k, here] = jnp.where(even_x, xa[rows], xb[rows])
    last = size_x - 1
    for side, (edge, inward) in enumerate(((0, 1), (last, -1))):
        at = edge + 2
        beside, past = (1, 0) if side == 0 else (2, 3)
        for start, rows in parts:
            here = pl.ds(start, rows)
            v1[side, here] = weight_of(c_out[beside, here]) * edges[side, here]
        for start, rows in parts:
            here = pl.ds(start, rows)
            center, total = around(v1, side, start, rows, lane, LANES, False, False)
            v[at - inward, here] = 0.2 * center + weight_of(c_out[beside, here]) * (total + edges[2 + side, here])
            v[at - 2 * inward, here] = weight_of(c_out[past, here]) * center
            v[at, here] += weight_of(c[edge, here]) * center
        base = 0 if side == 0 else 11
        for start, rows in parts:
            here = pl.ds(start, rows)
            r[base + inward, here] = v[at - 2 * inward, here]
            for k in range(-2, 2):
                plane = at + k * inward
                center, total = around(
                    v, plane, start, rows, lane, LANES, not (side == 0 and k == -2), not (side == 1 and k == -2)
                )
                if k >= 0:
                    total = total + f[plane - 2, here]
                    weight = 6.0 + c[plane - 2, here]
                else:
                    weight = 6.0 + c_out[beside if k == -1 else past, here]
                r[base + (4 + k) * inward, here] = total - weight * center

    for at in (0, size_x + 1):
        keep(v.at[pl.ds(at, 3), kept], v_far.at[pl.ds(at, 3)])
    keep(c_out.at[:, kept], sides_far)

    rows1 = size_z // 4 + 2 * GUARD
    size1 = size_x // 2
    off1 = 5
    here1 = pl.ds(GUARD, rows1)
    lane1 = lanes_of(rows1)
    for x in range(1, size1 - 1):
        f1[x + off1, here1] = f1_in[x - 1]
    for x, planes in (
        (-2, (1,)), (-1, (2, 3)), (0, (4, 5)), (size1 - 1, (6, 7)), (size1, (8, 9)), (size1 + 1, (10,))
    ):
        f1[x + off1, here1] = 0.5 * halve_two(r, planes, lane1, GUARD, rows1)
    for x in range(size1):
        c1[x + off1, here1] = c1_in[x, here1]
    c1[off1 - 1, here1] = 0.125 * halve_two(c_out, (0, 1), lane1, GUARD, rows1)
    c1[off1 + size1, here1] = 0.125 * halve_two(c_out, (2, 3), lane1, GUARD, rows1)
    for k in range(2):
        rows = pl.ds(2 * wide + k * rows1, rows1)
        c1[off1 - 2 - k, here1] = jnp.where(even_x, xb[rows], xa[rows])
        c1[off1 + size1 + 1 + k, here1] = jnp.where(even_x, xa[rows], xb[rows])
    low1, high1 = off1 - 2, off1 + size1 + 1
    keep(f1.at[pl.ds(off1 - 2, size1 + 4), here1], f1_far)
    keep(c1.at[pl.ds(off1 - 3, size1 + 6), here1], c1_far)
    for at in range(low1 - 1, high1 + 2):
        for ref in (u1, w1):
            ref[at, pl.ds(0, GUARD)] = zeros8
            ref[at, pl.ds(GUARD + rows1, GUARD)] = zeros8
    for at in range(low1, high1 + 1):
        u1[at, here1] = weight_of(c1[at, here1]) * f1[at, here1]
    for at in range(low1 - 1, high1 + 2):
        weight = weight_of(c1[at, here1])
        if at == low1 - 1:
            w1[at, here1] = weight * u1[at + 1, here1]
        elif at == high1 + 1:
            w1[at, here1] = weight * u1[at - 1, here1]
        else:
            center, total = around(u1, at, GUARD, rows1, lane1, 64, at > low1, at < high1)
            w1[at, here1] = 0.2 * center + weight * (total + f1[at, here1])
    for at in range(low1 - 2, high1 + 3):
        if at == low1 - 2:
            u1[at, here1] = w1[at + 1, here1]
        elif at == high1 + 2:
            u1[at, here1] = w1[at - 1, here1]
        else:
            center, total = around(w1, at, GUARD, rows1, lane1, 64, at > low1 - 1, at < high1 + 1)
            if low1 <= at <= high1:
                total = total + f1[at, here1]
            u1[at, here1] = total - (6.0 + c1[at, here1]) * center

    size2 = size_x // 4
    off2 = 5
    low2, high2 = off2 - 2, off2 + size2 + 1
    lane8, sub8 = lanes_of(8), subs_of(8)
    for ref in (v2, f2, c2, u2):
        ref[...] = jnp.zeros(ref.shape, F32)
    for x in range(-2, size2 + 2):
        own, past = halve_tiles(u1, (2 * x + off1, 2 * x + off1 + 1), lane8, sub8, rows1)
        put_tiles(f2, x + off2, 0.5 * own, 0.5 * past, lane8)
    for x in range(-1, size2 + 1):
        own, past = halve_tiles(c1, (2 * x + off1, 2 * x + off1 + 1), lane8, sub8, rows1)
        put_tiles(c2, x + off2, 0.125 * own, 0.125 * past, lane8)
    for k in range(2):
        own, past = (pl.ds(2 * wide + 2 * rows1 + 8 * (2 * k + j), 8) for j in (0, 1))
        put_tiles(
            c2, low2 - k, jnp.where(even_x, xb[own], xa[own]), jnp.where(even_x, xb[past], xa[past]), lane8
        )
        put_tiles(
            c2, high2 + k, jnp.where(even_x, xa[own], xb[own]), jnp.where(even_x, xa[past], xb[past]), lane8
        )
    for at in range(low2, high2 + 1):
        for t in (1, 2, 3):
            u2[at, t] = weight_of(c2[at, t]) * f2[at, t]
    for at in range(low2 - 1, high2 + 2):
        for t in (1, 2, 3):
            center, total = around_tile(u2, at, t, 1, lane8, sub8)
            v2[at, t] = 0.2 * center + weight_of(c2[at, t]) * (total + f2[at, t])
    for at in range(low2 - 2, high2 + 3):
        center, total = around_tile(v2, at, 2, 1, lane8, sub8)
        r2[at] = f2[at, 2] + total - (6.0 + c2[at, 2]) * center

    planes = [0.5 * pair_sums(r2[2 * k + 1] + r2[2 * k + 2], lane8, sub8) for k in range(size2 // 2 + 4)]
    planes += [
        0.125 * pair_sums(c2[off2 + 2 * k, 2] + c2[off2 + 2 * k + 1, 2], lane8, sub8) for k in range(size2 // 2)
    ]
    planes = [take_lanes(plane, 2 * (lane8 & 63)) for plane in planes]
    for k in range(2):
        even, odd = (
            jnp.where(lane8 < 64, planes[4 * k + j], planes[4 * k + j + 1]) for j in (0, 2)
        )
        tile = jnp.where((sub8 & 1) == 0, even, odd)
        for at in range(chunk.shape[0]):
            chunk[at, k] = tile

    pairs = [(v2, 2, off2 - k, off2 + size2 - 1 + k) for k in (1, 2, 3)]
    pairs += [(f2, 2, off2 - k, off2 + size2 - 1 + k) for k in (1, 2)]
    pairs += [(f1, here1, off1 + k, off1 + size1 - 1 - k) for k in (-2, -1, 0, 1, 2)]
    pairs += [(w1, here1, off1 + k, off1 + size1 - 1 - k) for k in (2, 3)]
    for k, (ref, rows, at_left, at_right) in enumerate(pairs):
        left, right = ref[at_left, rows], ref[at_right, rows]
        a, b, at = (near_a, near_b, 8 * k) if k < 5 else (to_a, to_b, (k - 5) * rows1)
        target = pl.ds(at, left.shape[0])
        a[target] = jnp.where(even_x, right, left)
        b[target] = jnp.where(even_x, left, right)

    for at in range(size2 + 6):
        level2[at] = v2[at + 2, 2]
    for at in range(size2 + 4):
        level2[size2 + 6 + at] = f2[at + 3, 2]
    c2_out[...] = c2[pl.ds(2, size2 + 6), pl.ds(1, 3)]
    v1_out[0] = w1[off1 - 3, here1]
    v1_out[1] = w1[off1 + size1 + 2, here1]
    for copy in copies:
        copy.wait()


def meet_kernel(level2, xa, xb, level1_a, level1_b, later_a, later_b, _, __, ___, own, to_a, to_b):
    even_x = lax.axis_index("gx") % 2 == 0
    size2 = own.shape[0] // 2
    planes = [level2[3 + x] for x in range(size2)] + [level2[size2 + 8 + x] for x in range(size2)]
    for k, (base, step) in enumerate(((0, 0), (0, 1), (0, 2), (size2, 0), (size2, 1))):
        rows = pl.ds(8 * k, 8)
        left = jnp.where(even_x, xb[rows], xa[rows])
        right = jnp.where(even_x, xa[rows], xb[rows])
        planes[base + step] = planes[base + step] + left
        planes[base + size2 - 1 - step] = planes[base + size2 - 1 - step] + right
    for k, plane in enumerate(planes):
        own[k] = plane
    size = level1_a.shape[0]
    for first, second, target in ((level1_a, later_a, to_a), (level1_b, later_b, to_b)):
        target[pl.ds(0, size)] = first[...]
        target[pl.ds(size, second.shape[0])] = second[...]


def follow_kernel(values, _, out):
    out[...] = values[...]


def past_tiles(za, zb, k, odd_z, lane):
    below = jnp.where(odd_z, za[k], zb[k])
    above = jnp.where(odd_z, zb[k], za[k])
    return jnp.where(lane >= 96, below, jnp.where(lane < 32, above, 0.0))


def side_kernel(own, za, zb, _, to_a, to_b):
    odd_z = lax.axis_index("gc") == 1
    even_x = lax.axis_index("gx") % 2 == 0
    size2 = own.shape[0] // 2
    lane = lanes_of(8)
    tiles = [(own[k], past_tiles(za, zb, k, odd_z, lane)) for k in range(2 * size2)]
    at = 0
    for base, count in ((0, size2), (size2, size2 - 1)):
        for k in range(count):
            for left, right in zip(tiles[base + k], tiles[base + size2 - 1 - k], strict=True):
                to_a[at] = jnp.where(even_x, right, left)
                to_b[at] = jnp.where(even_x, left, right)
                at += 1


def loop(count, body):
    if count <= 16:
        for i in range(count):
            body(i)
    else:
        lax.fori_loop(0, count, lambda i, _: (body(i), None)[1], None)


def coarse_kernel(
    nx, nz, own, other, inverse_far,
    window3, e_out,
    v3, f3, g3, c3, u3, turned, flat, inverse, arrivals,
):
    core = lax.axis_index("gc")
    ny = nz // 2
    lane, sub = lanes_of(8), subs_of(8)
    copies = []
    piece = inverse.shape[0] // 4
    for k in range(4):
        rows = pl.ds(k * piece, piece)
        copies.append(pltpu.make_async_copy(inverse_far.at[rows], inverse.at[rows], arrivals.at[k]))
        copies[k].start()
    for ref in (v3, f3, g3, u3):
        ref[...] = jnp.zeros(ref.shape, F32)

    def collect(at):
        for y in range(ny):
            for source, t in ((own, 1 + 2 * y + core), (other, 2 + 2 * y - core)):
                planes = []
                for k in range(2):
                    tile = source[at * ny + y, k]
                    even = jnp.where((sub & 1) == 0, tile, pltpu.roll(tile, 1, 0))
                    odd = jnp.where((sub & 1) == 1, tile, pltpu.roll(tile, 7, 0))
                    planes += [take_lanes(part, (lane >> 1) + 64 * j) for part in (even, odd) for j in (0, 1)]
                for k in range(6):
                    f3[2 * at + 2 + k, t] += planes[k]
                for k in range(2):
                    c3[2 * at + 4 + k, t] = planes[6 + k]

    loop(nx, collect)

    def third(at):
        for k in range(2):
            x = 4 + 2 * at + k
            for t in range(1, nz + 1):
                g3[x, t] = RELAX_WEIGHT / (6.0 + c3[x, t])
                u3[x, t] = g3[x, t] * f3[x, t]

    loop(nx, third)

    def fourth(at):
        for k in range(2):
            x = 4 + 2 * at + k
            for t in range(1, nz + 1):
                center, total = around_tile(u3, x, t, 2, lane, sub)
                v3[x, t] = 0.2 * center + g3[x, t] * (total + f3[x, t])

    loop(nx, fourth)

    step_x = 2 * nx // COARSE
    group = nz // 4

    for t in range(1, nz + 1):
        rows = []
        for xc in range(COARSE):
            total = 0.0
            for k in range(step_x):
                x = 4 + xc * step_x + k
                center, beside = around_tile(v3, x, t, 2, lane, sub)
                total += f3[x, t] + beside - (6.0 + c3[x, t]) * center
            rows.append(jnp.sum(total, axis=0, keepdims=True))
        block = 0.125 * jnp.concatenate(rows, axis=0)
        spread = block
        for k in range(1, group):
            spread = spread + pltpu.roll(block, LANES - 32 * k, 1)
        tall = jnp.concatenate([spread, jnp.zeros((LANES - COARSE, LANES), F32)], axis=0)
        turned[...] = tall.T
        line = jnp.zeros((8, LANES), F32)
        for k in range(8):
            piece = pltpu.roll(turned[pl.ds(2 * k, 8, stride=16), :], 16 * k, 1) if k else turned[pl.ds(0, 8, stride=16), :]
            line = jnp.where((lane >= 16 * k) & (lane < 16 * k + 16), piece, line)
        count = 4 // group
        for q in range(count):
            at = 2 * ((t - 1) * count + q)
            flat[at : at + 2] = line[2 * group * q : 2 * group * q + 2]

    at_x = lax.axis_index("gx")
    at_z = 2 * lax.axis_index("gy") + core
    for k, ref in enumerate((v3, f3, g3)):
        for t in range(3):
            window3[k, :, t] = ref[pl.ds(2 * at_x, 10), at_z + t]

    for copy in copies:
        copy.wait()
    total = None
    for t in range(inverse.shape[1] // LANES):
        piece = inverse[:, t * LANES : (t + 1) * LANES] * flat[t : t + 1]
        total = piece if total is None else total + piece
    column = jnp.sum(total, axis=1, keepdims=True)
    copies = e_out.shape[0]
    width = -(-copies // LANES) * LANES
    e_out[...] = jnp.broadcast_to(column, (inverse.shape[0], width)).T[:copies]


def top_level(nx, nz, e, window3, u3, lifted3, w3, turned):
    at_x = lax.axis_index("gx")
    at_z = 2 * lax.axis_index("gy") + lax.axis_index("gc")
    lane, sub = lanes_of(8), subs_of(8)
    step_x = 2 * nx // COARSE
    group = nz // 4

    for ref in (lifted3, u3, w3):
        ref[...] = jnp.zeros(ref.shape, F32)
    for t in range(1, nz + 1):
        pieces = []
        for q in range(4):
            at = 2 * (((t - 1) * 4 + q) // group)
            pieces.append(e[at : at + 2])
        rows = jnp.concatenate(pieces, axis=0)
        for k in range(8):
            piece = pltpu.roll(rows, LANES - 16 * k, 1) if k else rows
            turned[pl.ds(2 * k, 8, stride=16), :] = piece
            turned[pl.ds(2 * k + 1, 8, stride=16), :] = piece
        lifted = turned[...].T
        for xc in range(COARSE):
            tile = jnp.broadcast_to(lifted[xc : xc + 1], (8, LANES))
            for k in range(step_x):
                lifted3[4 + xc * step_x + k, t] = tile
    for x in range(10):
        for t in range(3):
            u3[x, t + 1] = window3[0, x, t] + lifted3[2 * at_x + x, at_z + t]
    for source, target, margin in ((u3, w3, 1), (w3, u3, 2)):
        for x in range(margin, 10 - margin):
            for t in range(3):
                center, total = around_tile(source, x, t + 1, 2, lane, sub)
                target[x, t + 1] = 0.2 * center + window3[2, x, t] * (total + window3[1, x, t])


def up_kernel(
    nx, nz, e, window3, own2, za, zb, sides_a, sides_b, c2, v_far, f_far, c_far, sides_far, f1_far, c1_far, f_ends, c_ends, v1_in, xa, xb, later_a, later_b,
    pressure_far, residual_far,
    u3, lifted3, w3, turned, u2, w2, f2, f1, c1, u1, w1, lift1, ua, ub, g, lift0, before_in, after_in, sources, v_in, f_in, c_in, f_held, c_held, c_sides, f1_in, c1_in, pressure, residual, arrivals,
):
    even_x = lax.axis_index("gx") % 2 == 0
    lane, sub = lanes_of(8), subs_of(8)
    zeros8 = jnp.zeros((GUARD, LANES), F32)
    pairs = (f1_far, f1_in), (c1_far, c1_in), (sides_far, c_sides), (v_far, v_in), (c_far, c_held), (f_far, f_held)
    copies = [pltpu.make_async_copy(*pair, arrivals.at[k]) for k, pair in enumerate(pairs)]
    for copy in copies:
        copy.start()
    for ref in (u2, w2, f2):
        ref[...] = jnp.zeros(ref.shape, F32)

    top_level(nx, nz, e, window3, u3, lifted3, w3, turned)

    odd_z = lax.axis_index("gc") == 1
    size2 = own2.shape[0] // 2
    planes2 = size2 + 8
    for k in range(2 * size2):
        target = u2 if k < size2 else f2
        put_tiles(target, 4 + k % size2, own2[k], past_tiles(za, zb, k, odd_z, lane), lane)
    at = 0
    for target, count in ((u2, size2), (f2, size2 - 1)):
        for k in range(count):
            left = [jnp.where(even_x, sides_b[at + j], sides_a[at + j]) for j in (0, 1)]
            right = [jnp.where(even_x, sides_a[at + j], sides_b[at + j]) for j in (0, 1)]
            put_tiles(target, 3 - k, *left, lane)
            put_tiles(target, 4 + size2 + k, *right, lane)
            at += 2
    for x in range(planes2):
        for t in (1, 2, 3):
            u2[x, t] += u3[2 + x // 2, t]
    for source, target, margin in ((u2, w2, 1), (w2, u2, 2)):
        for x in range(margin, planes2 - margin):
            for t in (1, 2, 3):
                center, total = around_tile(source, x, t, 1, lane, sub)
                target[x, t] = 0.2 * center + weight_of(c2[x - 1, t - 1]) * (total + f2[x, t])

    rows1 = f1_in.shape[1]
    size1 = 2 * size2
    off1 = 4
    here1 = pl.ds(GUARD, rows1)
    lane1 = lanes_of(rows1)
    side = lane >> 6
    fine = (lane & 63) >> 1
    for x in range(2, planes2 - 2):
        below, middle, above = u2[x, 1], u2[x, 2], u2[x, 3]
        index = [(((2 * side + q) & 3) << 5) + fine for q in (-1, 0, 1, 2)]
        tiles = [
            jnp.where(side == 0, take_lanes(below, index[0]), take_lanes(middle, index[0]))[4:],
            take_lanes(middle, index[1]),
            take_lanes(middle, index[2]),
            jnp.where(side == 0, take_lanes(middle, index[3]), take_lanes(above, index[3]))[:4],
        ]
        start = 0
        for tile in tiles:
            count = tile.shape[0]
            lift1[x - 2, pl.ds(start, count, stride=2), :] = tile
            lift1[x - 2, pl.ds(start + 1, count, stride=2), :] = tile
            start += 2 * count

    kept = v_in.shape[1]

    def arrived(start, rows, a=xa, b=xb):
        a, b = a[pl.ds(start, rows)], b[pl.ds(start, rows)]
        return jnp.where(even_x, b, a), jnp.where(even_x, a, b)

    copies[0].wait()
    copies[1].wait()
    for x in range(-2, size1 + 2):
        f1[x + off1, here1] = f1_in[x + 2]
    for x in range(-3, size1 + 3):
        c1[x + off1, here1] = weight_of(c1_in[x + 3])
    for k in range(7):
        left, right = arrived(k * rows1, rows1, later_a, later_b)
        if k < 4:
            f1[off1 + 1 - k, here1] += left
            f1[off1 + size1 - 2 + k, here1] += right
        elif k == 4:
            f1[off1 - 3, here1] = left
            f1[off1 + size1 + 2, here1] = right
        else:
            w1[off1 + 2 - k, here1] = left + v1_in[0] if k == 5 else left
            w1[off1 + size1 - 3 + k, here1] = right + v1_in[1] if k == 5 else right
    planes1 = size1 + 8
    for ref in (u1, w1):
        for at in range(planes1):
            ref[at, pl.ds(0, GUARD)] = zeros8
            ref[at, pl.ds(GUARD + rows1, GUARD)] = zeros8
    for at in range(1, planes1 - 1):
        u1[at, here1] = c1[at, here1] * f1[at, here1]
    for at in range(planes1):
        value = w1[at, here1]
        if 2 <= at < planes1 - 2:
            center, total = around(u1, at, GUARD, rows1, lane1, 64)
            value = 0.2 * center + c1[at, here1] * (total + f1[at, here1])
        w1[at, here1] = value + lift1[at // 2]
    for source, target, margin in ((w1, u1, 1), (u1, w1, 2)):
        for at in range(margin, planes1 - margin):
            center, total = around(source, at, GUARD, rows1, lane1, 64)
            target[at, here1] = 0.2 * center + c1[at, here1] * (total + f1[at, here1])

    size_x = f_in.shape[0]
    size_z = kept - 2 * KEEP
    short = kept // 4
    index = lanes_of(short) >> 1
    for x in range(-2, size1 + 2):
        for part in range(2):
            source = w1[x + off1, pl.ds(GUARD + (4 if part == 0 else 8), short)]
            tile = take_lanes(source, index + 64 * part)
            lift0[x + 2, pl.ds(part * 2 * short, short, stride=2), :] = tile
            lift0[x + 2, pl.ds(part * 2 * short + 1, short, stride=2), :] = tile

    off = 3
    last = size_x + off - 1
    here = pl.ds(GUARD, kept)
    for ref in (ua, ub):
        for at in range(size_x + 6):
            ref[at, pl.ds(0, GUARD)] = zeros8
            ref[at, pl.ds(GUARD + kept, GUARD)] = zeros8
    for copy in copies[2:]:
        copy.wait()
    for held, part, target in ((f_held, f_ends, f_in), (c_held, c_ends, c_in)):
        for x in range(size_x):
            target[x, pl.ds(KEEP, size_z)] = held[x].T
        target[:, pl.ds(0, KEEP)] = part[:, pl.ds(0, KEEP)]
        target[:, pl.ds(KEEP + size_z, KEEP)] = part[:, pl.ds(KEEP, KEEP)]
    shift = -GUARD
    for x in range(-3, size_x + 3):
        value = lift0[(x + 4) // 2]
        if -2 <= x <= size_x + 1:
            value = value + v_in[x + 2, pl.ds(GUARD + shift, kept)]
        ua[x + off, here] = value
    half = kept // 2
    parts = [(GUARD, half), (GUARD + half, half)]
    laneh = lanes_of(half)
    beyond = {-2: 0, -1: 1, size_x: 2, size_x + 1: 3}
    for x in range(-2, size_x + 2):
        for start, rows in parts:
            at = pl.ds(start + shift, rows)
            g[x + 2, pl.ds(start, rows)] = weight_of(c_sides[beyond[x], at] if x in beyond else c_in[x, at])

    sent = size_z + 2 * SENT
    begin = GUARD + KEEP - SENT
    taken = pl.ds(begin, sent)
    lane_s = lanes_of(sent)
    for ref in (before_in, after_in, sources):
        ref[...] = jnp.zeros(ref.shape, F32)
    messages = [arrived(k * sent, sent) for k in range(EARLY)]
    messages += [arrived(7 * rows1 + k * sent, sent, later_a, later_b) for k in range(5 - EARLY)]
    for side, (edge, inward) in enumerate(((off, 1), (last, -1))):
        before, after, source0, source1, source2 = (message[side] for message in messages)
        before_in[side, taken] = g[edge - 1, taken] * before
        after_in[side, taken] = after
        sources[side, taken] = source1
        sources[2 + side, taken] = source2
        center, total = around(before_in, side, begin, sent, lane_s, LANES, False, False)
        ua[edge, taken] += 0.2 * center + g[edge - 1, taken] * (total + after)
        ua[edge + inward, taken] += g[edge + inward - 1, taken] * center
        _, total = around(after_in, side, begin, sent, lane_s, LANES, False, False)
        ua[edge - inward, taken] += 0.2 * after + g[edge - inward - 1, taken] * (total + source0 + center)

    for sweep, (origin, target) in enumerate(((ua, ub), (ub, ua))):
        for at in range(1 + sweep, size_x + 5 - sweep):
            for start, rows in parts:
                center, total = around(origin, at, start, rows, laneh, LANES)
                x = at - off
                if 0 <= x < size_x:
                    total = total + f_in[x, pl.ds(start + shift, rows)]
                elif x in (-1, size_x):
                    total = total + sources[2 * sweep + (x > 0), pl.ds(start, rows)]
                target[at, pl.ds(start, rows)] = 0.2 * center + g[at - 1, pl.ds(start, rows)] * total
    lane_z = lanes_of(size_z)
    own = GUARD + KEEP
    piece = size_x // 4
    copies = []

    def leave(source, target, x):
        if (x + 1) % piece == 0:
            planes = pl.ds(x + 1 - piece, piece)
            copies.append(pltpu.make_async_copy(source.at[planes], target.at[planes], arrivals.at[len(copies)]))
            copies[-1].start()

    for x in range(size_x):
        pressure[x] = ua[x + off, pl.ds(own, size_z)].T
        leave(pressure, pressure_far, x)
    for x in range(size_x):
        center, total = around(ua, x + off, own, size_z, lane_z, LANES)
        mine = pl.ds(own + shift, size_z)
        total = total + f_in[x, mine]
        residual[x] = (total - (6.0 + c_in[x, mine]) * center).T
        leave(residual, residual_far, x)
    for copy in copies:
        copy.wait()


def pairs_of(count):
    even = [(i, i ^ 1) for i in range(count)]
    odd = [(i, ((i - 1) ^ 1) + 1) for i in range(1, count - 1)]
    return even, odd


def gather(copies, axes, always):
    return lax.cond(always, lambda x: lax.all_to_all(x, axes, 0, 0, tiled=True), lambda x: x, copies)


def local(nx, nz, right_side, reaction, initial, coarse_inverse):
    size_x, _, size_z = right_side.shape
    size1, size2 = size_x // 2, size_x // 4
    wide, kept, sent = (size_z + 2 * rows for rows in (DEEP, KEEP, SENT))
    deep = wide + 2 * GUARD
    rows1 = size_z // 4 + 2 * GUARD
    brick = (size_x, size_z, LANES)
    padded = (size_x, deep, LANES)
    padded1 = (size1, rows1 + 2 * GUARD, LANES)
    slab = (size_x, DEEP, LANES)
    always = lax.optimization_barrier(jnp.int32(1)) > 0
    flag = always.astype(jnp.int32).reshape(1, 1)
    c, f, mza, mzb = call(
        turn_kernel, "turn", (brick, brick, (2, *slab), (2, *slab)), (reaction, right_side, flag),
        [(2, *right_side.shape)], far_args=(0, 1), copies=8,
    )
    even_z, odd_z = pairs_of(nz)
    za = lax.ppermute(mza, ("gy", "gc"), even_z)
    zb = lax.ppermute(mzb, ("gy", "gc"), odd_z)
    v, mya, myb = call(turn_again_kernel, "turn_again", (brick, slab, slab), (initial, mza))
    ya = lax.ppermute(mya, ("gy", "gc"), even_z)
    yb = lax.ppermute(myb, ("gy", "gc"), odd_z)

    message = (2 * wide + 2 * rows1 + 32, LANES)
    mxa, mxb, c, c1 = call(
        coefficient_kernel, "coefficients", (message, message, padded, padded1), (c, za, zb)
    )
    even_x, odd_x = pairs_of(nx)
    xa = lax.ppermute(mxa, "gx", even_x)
    xb = lax.ppermute(mxb, "gx", odd_x)

    margin, later = (EARLY * sent, LANES), ((5 - EARLY) * sent, LANES)
    held, ends = (size_x, kept, LANES), (size_x, 2 * KEEP, LANES)
    f, v, edges, f1, mua, mub, mla, mlb, f_ends, c_ends = call(
        inner_kernel, "inner",
        (padded, padded, (4, deep, LANES), (size1 - 2, rows1, LANES), margin, margin, later, later, ends, ends),
        (f, v, c, za, zb, ya, yb),
        [padded] * 4,
    )
    ua = lax.ppermute(mua, "gx", even_x)
    ub = lax.ppermute(mub, "gx", odd_x)

    box2 = (size2 + 10, 5, 8, LANES)
    near, level1 = (40, LANES), (7 * rows1, LANES)
    sides0, sides1 = (4, deep, LANES), (2, rows1, LANES)
    parts1 = (size1 + 4, rows1, LANES), (size1 + 6, rows1, LANES)
    field0 = (size_x + 4, deep, LANES)
    field1 = (size1 + 10, rows1 + 2 * GUARD, LANES)
    chunk, mna, mnb, m1a, m1b, v, c_sides, f1, c1, v1, level2, c2 = call(
        outer_kernel, "outer",
        (
            (nx * nz // 2, 2, 8, LANES), near, near, level1, level1,
            (size_x + 4, kept, LANES), (4, kept, LANES), *parts1, sides1, (2 * size2 + 10, 8, LANES), (size2 + 6, 3, 8, LANES),
        ),
        (f, c, v, edges, f1, c1, xa, xb),
        [
            field0, sides0, (2, deep, LANES), (12, deep, LANES), field1, field1, field1, field1,
            box2, (size2 + 10, 8, LANES), box2, box2, box2,
        ],
        far_outs=range(5, 9), copies=6,
    )
    na = lax.ppermute(mna, "gx", even_x)
    nb = lax.ppermute(mnb, "gx", odd_x)
    own = gather(chunk, ("gx", "gy"), always)
    both = (7 * rows1 + (5 - EARLY) * sent, LANES)
    own2, mla, mlb = call(
        meet_kernel, "meet", ((2 * size2, 8, LANES), both, both), (level2, na, nb, m1a, m1b, mla, mlb, ua, ub, own)
    )
    la = lax.ppermute(mla, "gx", even_x)
    lb = lax.ppermute(mlb, "gx", odd_x)
    other = lax.ppermute(own, "gc", [(0, 1), (1, 0)])
    z2a = lax.ppermute(own2, ("gy", "gc"), even_z)
    z2b = lax.ppermute(own2, ("gy", "gc"), odd_z)
    grid3 = (2 * nx + 8, nz + 2, 8, LANES)
    rows = coarse_inverse.shape[0]
    window3, e = call(
        functools.partial(coarse_kernel, nx, nz), "coarse",
        ((3, 10, 3, 8, LANES), (nx * nz, rows)),
        (own, other, coarse_inverse),
        [*[grid3] * 5, (LANES, LANES), (COARSE**3 // LANES, LANES), coarse_inverse.shape],
        far_args=(2,), copies=4,
    )
    sides = (4 * size2 - 2, 8, LANES)
    msa, msb = call(side_kernel, "sides", (sides, sides), (own2, z2a, z2b, e))
    sa = lax.ppermute(msa, "gx", even_x)
    sb = lax.ppermute(msb, "gx", odd_x)
    (e,) = call(follow_kernel, "follow", (e.shape,), (e, msa))
    e = gather(e, ("gx", "gy", "gc"), always).reshape(COARSE**3 // LANES, LANES)

    near2 = (size2 + 8, 5, 8, LANES)
    box3 = (10, 5, 8, LANES)
    box = (size_x + 6, kept + 2 * GUARD, LANES)
    return call(
        functools.partial(up_kernel, nx, nz), "up",
        ((size_x, LANES, size_z), (size_x, LANES, size_z)),
        (e, window3, own2, z2a, z2b, sa, sb, c2, v, right_side, reaction, c_sides, f1, c1, f_ends, c_ends, v1, ua, ub, la, lb),
        [
            box3, grid3, box3, (LANES, LANES), near2, near2, near2,
            field1, field1, field1, field1, (size2 + 4, rows1, LANES),
            box, box, box, (size1 + 4, kept, LANES), *[(2, kept + 2 * GUARD, LANES)] * 2, (4, kept + 2 * GUARD, LANES),
            (size_x + 4, kept, LANES), held, held, right_side.shape, right_side.shape, (4, kept, LANES), *parts1,
            right_side.shape, right_side.shape,
        ],
        far_args=range(8, 14), far_outs=(0, 1), copies=8, results=True,
    )


def solution(mesh):
    nx, nz = mesh.shape["gx"], mesh.shape["gz"]
    fine = Mesh(mesh.devices.reshape(nx, nz // 2, 2), ("gx", "gy", "gc"))
    brick = P("gx", None, ("gy", "gc"))
    return jax.shard_map(
        lambda *args: tuple(local(nx, nz, *args)),
        mesh=fine,
        in_specs=(brick, brick, brick, P(("gx", "gy", "gc"), None)),
        out_specs=(brick, brick),
        check_vma=False,
    )
```

```python
import functools
import math

import jax
import jax.numpy as jnp
from jax import lax
from jax.experimental import pallas as pl
from jax.experimental.pallas import tpu as pltpu
from jax.sharding import Mesh
from jax.sharding import PartitionSpec as P

COARSE = 16
RELAX_WEIGHT = 0.8
F32 = jnp.float32
LANES = 128
DEEP = 16
KEEP = 8
SENT = 4
GUARD = 8
EARLY = 2
MIB = 1 << 20


def lanes_of(rows):
    return lax.broadcasted_iota(jnp.int32, (rows, LANES), 1)


def subs_of(rows):
    return lax.broadcasted_iota(jnp.int32, (rows, LANES), 0)


def take_lanes(values, index):
    return jnp.take_along_axis(values, index, axis=1, mode="promise_in_bounds")


def beside_lanes(values, lane, width, step):
    place = lane & (width - 1)
    low = jnp.where(place >= step, pltpu.roll(values, step, 1), 0.0)
    high = jnp.where(place < width - step, pltpu.roll(values, LANES - step, 1), 0.0)
    return low + high


def weight_of(c):
    return jnp.where(c > 0.0, RELAX_WEIGHT / (6.0 + c), 0.0)


def around(ref, at, start, rows, lane, width, lower=True, upper=True):
    center = ref[at, pl.ds(start, rows)]
    total = ref[at, pl.ds(start - 1, rows)] + ref[at, pl.ds(start + 1, rows)]
    total = total + beside_lanes(center, lane, width, 1)
    if lower:
        total = total + ref[at - 1, pl.ds(start, rows)]
    if upper:
        total = total + ref[at + 1, pl.ds(start, rows)]
    return center, total


def halve_two(ref, planes, lane, first, rows):
    index = 2 * (lane & 63)

    def part(start):
        total = None
        for at in planes:
            for odd in (0, 1):
                piece = ref[at, pl.ds(start + odd, rows, stride=2), :]
                total = piece if total is None else total + piece
        total = total + pltpu.roll(total, LANES - 1, 1)
        return take_lanes(total, index)

    return jnp.where(lane < 64, part(first), part(first + 64))


def halve_four(ref, planes, lane8, first):
    total = None
    for at in planes:
        for odd in (0, 1):
            piece = ref[at, pl.ds(first + odd, 16, stride=2), :]
            total = piece if total is None else total + piece
    total = total + pltpu.roll(total, LANES - 1, 1)
    index = (lane8 & 64) + 2 * (lane8 & 31)
    return jnp.where((lane8 & 32) == 0, take_lanes(total[:8], index), take_lanes(total[8:], index))


def around_tile(ref, x, t, step, lane, sub):
    center = ref[x, t]
    total = ref[x - 1, t] + ref[x + 1, t] + beside_lanes(center, lane, 32, step)
    after = pltpu.roll(jnp.where(lane < 32, ref[x, t + 1], center), LANES - 32, 1)
    total = total + pltpu.roll(jnp.where(sub < step, after, center), 8 - step, 0)
    before = pltpu.roll(jnp.where(lane >= 96, ref[x, t - 1], center), 32, 1)
    total = total + pltpu.roll(jnp.where(sub >= 8 - step, before, center), step, 0)
    return center, total


def pair_sums(values, lane, sub):
    partner = jnp.where((lane & 1) == 0, pltpu.roll(values, LANES - 1, 1), pltpu.roll(values, 1, 1))
    values = values + partner
    partner = jnp.where((sub & 1) == 0, pltpu.roll(values, 7, 0), pltpu.roll(values, 1, 0))
    return values + partner


def halve_tiles(ref, planes, lane, sub, beyond):
    def edge(start):
        total = None
        for at in planes:
            for odd in (0, 1):
                piece = ref[at, pl.ds(start + odd, 4, stride=2), :]
                total = piece if total is None else total + piece
        return total

    past = jnp.concatenate([edge(beyond), edge(GUARD)], axis=0)
    past = past + pltpu.roll(past, LANES - 1, 1)
    past = take_lanes(past, jnp.where(sub < 4, 64, 0) + 2 * (lane & 31))
    kept = ((sub < 4) & (lane < 32)) | ((sub >= 4) & (lane >= 96))
    return halve_four(ref, planes, lane, 2 * GUARD), jnp.where(kept, past, 0.0)


def put_tiles(target, at, own, past, lane):
    target[at, 2] = own
    target[at, 1] = jnp.where(lane >= 96, past, 0.0)
    target[at, 3] = jnp.where(lane < 32, past, 0.0)


def call(kernel, name, outs, args, scratch=(), far_args=(), far_outs=(), copies=0, results=False, micros=1):
    limit = sum(4 * math.prod(s) for s in scratch) + 6 * MIB
    spaces_in = [pltpu.HBM if k in far_args else pltpu.VMEM for k in range(len(args))]
    spaces_out = [pltpu.HBM if k in far_outs else pltpu.VMEM for k in range(len(outs))]
    spaces_in = [pltpu.SMEM if a.dtype == jnp.int32 else space for a, space in zip(args, spaces_in, strict=True)]
    args = [
        a if space == pltpu.SMEM else pltpu.with_memory_space_constraint(a, space)
        for a, space in zip(args, spaces_in, strict=True)
    ]
    return pl.pallas_call(
        kernel,
        out_shape=[
            jax.ShapeDtypeStruct(s, F32) if results else space(s, F32)
            for s, space in zip(outs, spaces_out, strict=True)
        ],
        in_specs=[pl.BlockSpec(memory_space=space) for space in spaces_in],
        out_specs=[pl.BlockSpec(memory_space=space) for space in spaces_out],
        scratch_shapes=[pltpu.VMEM(s, F32) for s in scratch] + [pltpu.SemaphoreType.DMA((copies,))] * (copies > 0),
        compiler_params=pltpu.CompilerParams(vmem_limit_bytes=limit),
        cost_estimate=pl.CostEstimate(flops=0, bytes_accessed=3_000_000 * micros, transcendentals=0),
        name=name,
    )(*args)


def edge_rows(source, to_a, to_b):
    odd = lax.axis_index("gc")
    far = source.shape[1] - DEEP
    to_a[...] = source[:, pl.ds(pl.multiple_of((1 - odd) * far, DEEP), DEEP), :]
    to_b[...] = source[:, pl.ds(pl.multiple_of(odd * far, DEEP), DEEP), :]


def turn_kernel(*refs):
    *refs, held, arrivals = refs
    count = (len(refs) - 3) // 2
    sources, targets, (to_a, to_b) = refs[:count], refs[count + 1 : 2 * count + 1], refs[2 * count + 1 :]
    piece = targets[0].shape[0] // 4
    copies = []
    for which, source in enumerate(sources):
        for k in range(4):
            planes = pl.ds(k * piece, piece)
            copies.append(
                pltpu.make_async_copy(source.at[planes], held.at[which, planes], arrivals.at[4 * which + k])
            )
            copies[-1].start()
    for which, target in enumerate(targets):
        for k in range(4):
            copies[4 * which + k].wait()
            for x in range(k * piece, (k + 1) * piece):
                target[x] = held[which, x].T
        edge_rows(target, to_a.at[which], to_b.at[which])


def turn_again_kernel(v_in, _, v_out, to_a, to_b):
    for x in range(v_out.shape[0]):
        v_out[x] = v_in[x].T
    edge_rows(v_out, to_a, to_b)


def fill_rows(target, at, own, low, high):
    rows = own.shape[0]
    target[at, pl.ds(GUARD, DEEP)] = low
    target[at, pl.ds(GUARD + DEEP, rows)] = own
    target[at, pl.ds(GUARD + DEEP + rows, DEEP)] = high


def coefficient_kernel(c_in, za, zb, _, __, to_a, to_b, padded, c1):
    odd_z = lax.axis_index("gc") == 1
    even_x = lax.axis_index("gx") % 2 == 0
    size_x, size_z, _ = c_in.shape
    wide = pl.ds(GUARD, size_z + 2 * DEEP)
    rows1 = size_z // 4 + 2 * GUARD
    here1 = pl.ds(GUARD, rows1)
    lane, lane8, sub8 = lanes_of(rows1), lanes_of(8), subs_of(8)
    for x in range(size_x):
        low = jnp.where(odd_z, za[0, x], zb[0, x])
        high = jnp.where(odd_z, zb[0, x], za[0, x])
        fill_rows(padded, x, c_in[x], low, high)
    for x in range(size_x // 2):
        c1[x, here1] = 0.125 * halve_two(padded, (2 * x, 2 * x + 1), lane, GUARD, rows1)
    sides = []
    for order, order1 in ((range(size_x), range(8)), (range(size_x - 1, -1, -1), range(7, -1, -1))):
        tiles = []
        for k in (2, 4):
            tiles += [0.125 * tile for tile in halve_tiles(c1, order1[k : k + 2], lane8, sub8, rows1)]
        sides.append(
            [padded[order[0], wide], padded[order[1], wide], c1[order1[1], here1], c1[order1[2], here1], *tiles]
        )
    start = 0
    for left, right in zip(*sides, strict=True):
        rows = pl.ds(start, left.shape[0])
        to_a[rows] = jnp.where(even_x, right, left)
        to_b[rows] = jnp.where(even_x, left, right)
        start += left.shape[0]


def inner_kernel(
    f_in, v_in, c, za, zb, ya, yb,
    f, v2, edges, f1, to_a, to_b, later_a, later_b, f_ends, c_ends, v_far,
    va, vb, g, r, arrivals,
):
    odd_z = lax.axis_index("gc") == 1
    even_x = lax.axis_index("gx") % 2 == 0
    size_x, size_z, _ = f_in.shape
    wide = size_z + 2 * DEEP
    half = wide // 2
    parts = [(GUARD, half), (GUARD + half, half)]
    last = size_x - 1
    lane = lanes_of(half)
    zeros8 = jnp.zeros((GUARD, LANES), F32)

    for source, target, a, b in ((f_in, f, za.at[1], zb.at[1]), (v_in, va, ya, yb)):
        for x in range(size_x):
            low = jnp.where(odd_z, a[x], b[x])
            high = jnp.where(odd_z, b[x], a[x])
            fill_rows(target, x, source[x], low, high)
    for ref in (va, vb, v2):
        for x in range(size_x):
            ref[x, pl.ds(0, GUARD)] = zeros8
            ref[x, pl.ds(GUARD + wide, GUARD)] = zeros8
    for x in range(size_x):
        for start, rows in parts:
            here = pl.ds(start, rows)
            g[x, here] = weight_of(c[x, here])
    for source, target in ((va, vb), (vb, v2)):
        for x in range(size_x):
            for start, rows in parts:
                here = pl.ds(start, rows)
                center, total = around(source, x, start, rows, lane, LANES, x > 0, x < last)
                target[x, here] = 0.2 * center + g[x, here] * (total + f[x, here])
    copy = pltpu.make_async_copy(
        v2.at[pl.ds(1, size_x - 2), pl.ds(GUARD + DEEP - KEEP, size_z + 2 * KEEP)], v_far, arrivals.at[0]
    )
    copy.start()
    for x in range(2, last - 1):
        for start, rows in parts:
            here = pl.ds(start, rows)
            center, total = around(v2, x, start, rows, lane, LANES)
            r[x, here] = total + f[x, here] - (6.0 + c[x, here]) * center
    rows1 = size_z // 4 + 2 * GUARD
    lane1 = lanes_of(rows1)
    for x in range(1, size_x // 2 - 1):
        f1[x - 1] = 0.5 * halve_two(r, (2 * x, 2 * x + 1), lane1, GUARD, rows1)
    edges[0], edges[1], edges[2], edges[3] = va[0], va[last], vb[0], vb[last]

    sent = size_z + 2 * SENT
    first = GUARD + DEEP - SENT
    here = pl.ds(first, sent)
    lane = lanes_of(sent)
    sides = []
    for edge, second in ((0, 1), (last, last - 1)):
        center, total = around(v2, second, first, sent, lane, LANES, second != 1, second == 1)
        swept = 0.2 * center + g[second, here] * (total + f[second, here])
        source = f[edge, here]
        sides.append((va[edge, here], vb[edge, here], source + vb[second, here], source + center, source + swept))
    for k, (left, right) in enumerate(zip(*sides, strict=True)):
        a, b, rows = (to_a, to_b, pl.ds(k * sent, sent)) if k < EARLY else (later_a, later_b, pl.ds((k - EARLY) * sent, sent))
        a[rows] = jnp.where(even_x, right, left)
        b[rows] = jnp.where(even_x, left, right)
    for source, target in ((f, f_ends), (c, c_ends)):
        target[:, pl.ds(0, KEEP)] = source[:, pl.ds(GUARD + DEEP - KEEP, KEEP)]
        target[:, pl.ds(KEEP, KEEP)] = source[:, pl.ds(GUARD + DEEP + size_z, KEEP)]
    copy.wait()


def outer_kernel(
    f, c, v2_in, edges, f1_in, c1_in, early_a, early_b, xa, xb,
    chunk, near_a, near_b, to_a, to_b, v_far, sides_far, f1_far, c1_out, v1_out, level2, c2_out,
    v, c_out, v1, r, f1, c1, u1, w1, u2, r2, v2, f2, c2, arrivals,
):
    even_x = lax.axis_index("gx") % 2 == 0
    size_x = f.shape[0]
    size_z = f.shape[1] - 2 * DEEP - 2 * GUARD
    wide = size_z + 2 * DEEP
    half = wide // 2
    parts = [(GUARD, half), (GUARD + half, half)]
    lane = lanes_of(half)
    zeros8 = jnp.zeros((GUARD, LANES), F32)

    copies = []

    def keep(source, target):
        copies.append(pltpu.make_async_copy(source, target, arrivals.at[len(copies)]))
        copies[-1].start()

    kept = pl.ds(GUARD + DEEP - KEEP, size_z + 2 * KEEP)

    for x in (0, 1, 2, size_x - 3, size_x - 2, size_x - 1):
        v[x + 2] = v2_in[x]
    for ref, planes in ((v, (0, 1, size_x + 2, size_x + 3)), (v1, (0, 1))):
        for at in planes:
            ref[at, pl.ds(0, GUARD)] = zeros8
            ref[at, pl.ds(GUARD + wide, GUARD)] = zeros8
    for k in range(2):
        rows, here = pl.ds(k * wide, wide), pl.ds(GUARD, wide)
        c_out[1 - k, here] = jnp.where(even_x, xb[rows], xa[rows])
        c_out[2 + k, here] = jnp.where(even_x, xa[rows], xb[rows])
    last = size_x - 1
    for side, (edge, inward) in enumerate(((0, 1), (last, -1))):
        at = edge + 2
        beside, past = (1, 0) if side == 0 else (2, 3)
        for start, rows in parts:
            here = pl.ds(start, rows)
            v1[side, here] = weight_of(c_out[beside, here]) * edges[side, here]
        for start, rows in parts:
            here = pl.ds(start, rows)
            center, total = around(v1, side, start, rows, lane, LANES, False, False)
            v[at - inward, here] = 0.2 * center + weight_of(c_out[beside, here]) * (total + edges[2 + side, here])
            v[at - 2 * inward, here] = weight_of(c_out[past, here]) * center
            v[at, here] += weight_of(c[edge, here]) * center
        base = 0 if side == 0 else 11
        for start, rows in parts:
            here = pl.ds(start, rows)
            r[base + inward, here] = v[at - 2 * inward, here]
            for k in range(-2, 2):
                plane = at + k * inward
                center, total = around(
                    v, plane, start, rows, lane, LANES, not (side == 0 and k == -2), not (side == 1 and k == -2)
                )
                if k >= 0:
                    total = total + f[plane - 2, here]
                    weight = 6.0 + c[plane - 2, here]
                else:
                    weight = 6.0 + c_out[beside if k == -1 else past, here]
                r[base + (4 + k) * inward, here] = total - weight * center

    for k, at in enumerate((0, size_x + 1)):
        keep(v.at[pl.ds(at, 3), kept], v_far.at[pl.ds(3 * k, 3)])
    keep(c_out.at[:, kept], sides_far)

    rows1 = size_z // 4 + 2 * GUARD
    size1 = size_x // 2
    off1 = 5
    here1 = pl.ds(GUARD, rows1)
    lane1 = lanes_of(rows1)
    for x in range(1, size1 - 1):
        f1[x + off1, here1] = f1_in[x - 1]
    for x, planes in (
        (-2, (1,)), (-1, (2, 3)), (0, (4, 5)), (size1 - 1, (6, 7)), (size1, (8, 9)), (size1 + 1, (10,))
    ):
        f1[x + off1, here1] = 0.5 * halve_two(r, planes, lane1, GUARD, rows1)
    for x in range(size1):
        c1[x + off1, here1] = c1_in[x, here1]
    c1[off1 - 1, here1] = 0.125 * halve_two(c_out, (0, 1), lane1, GUARD, rows1)
    c1[off1 + size1, here1] = 0.125 * halve_two(c_out, (2, 3), lane1, GUARD, rows1)
    for k in range(2):
        rows = pl.ds(2 * wide + k * rows1, rows1)
        c1[off1 - 2 - k, here1] = jnp.where(even_x, xb[rows], xa[rows])
        c1[off1 + size1 + 1 + k, here1] = jnp.where(even_x, xa[rows], xb[rows])
    low1, high1 = off1 - 2, off1 + size1 + 1
    keep(f1.at[pl.ds(off1 - 2, size1 + 4), here1], f1_far)
    c1_out[...] = c1[pl.ds(off1 - 3, size1 + 6), here1]
    for at in range(low1 - 1, high1 + 2):
        for ref in (u1, w1):
            ref[at, pl.ds(0, GUARD)] = zeros8
            ref[at, pl.ds(GUARD + rows1, GUARD)] = zeros8
    for at in range(low1, high1 + 1):
        u1[at, here1] = weight_of(c1[at, here1]) * f1[at, here1]
    for at in range(low1 - 1, high1 + 2):
        weight = weight_of(c1[at, here1])
        if at == low1 - 1:
            w1[at, here1] = weight * u1[at + 1, here1]
        elif at == high1 + 1:
            w1[at, here1] = weight * u1[at - 1, here1]
        else:
            center, total = around(u1, at, GUARD, rows1, lane1, 64, at > low1, at < high1)
            w1[at, here1] = 0.2 * center + weight * (total + f1[at, here1])
    for at in range(low1 - 2, high1 + 3):
        if at == low1 - 2:
            u1[at, here1] = w1[at + 1, here1]
        elif at == high1 + 2:
            u1[at, here1] = w1[at - 1, here1]
        else:
            center, total = around(w1, at, GUARD, rows1, lane1, 64, at > low1 - 1, at < high1 + 1)
            if low1 <= at <= high1:
                total = total + f1[at, here1]
            u1[at, here1] = total - (6.0 + c1[at, here1]) * center

    size2 = size_x // 4
    off2 = 5
    low2, high2 = off2 - 2, off2 + size2 + 1
    lane8, sub8 = lanes_of(8), subs_of(8)
    for ref in (v2, f2, c2, u2):
        ref[...] = jnp.zeros(ref.shape, F32)
    for x in range(-2, size2 + 2):
        own, past = halve_tiles(u1, (2 * x + off1, 2 * x + off1 + 1), lane8, sub8, rows1)
        put_tiles(f2, x + off2, 0.5 * own, 0.5 * past, lane8)
    for x in range(-1, size2 + 1):
        own, past = halve_tiles(c1, (2 * x + off1, 2 * x + off1 + 1), lane8, sub8, rows1)
        put_tiles(c2, x + off2, 0.125 * own, 0.125 * past, lane8)
    for k in range(2):
        own, past = (pl.ds(2 * wide + 2 * rows1 + 8 * (2 * k + j), 8) for j in (0, 1))
        put_tiles(
            c2, low2 - k, jnp.where(even_x, xb[own], xa[own]), jnp.where(even_x, xb[past], xa[past]), lane8
        )
        put_tiles(
            c2, high2 + k, jnp.where(even_x, xa[own], xb[own]), jnp.where(even_x, xa[past], xb[past]), lane8
        )
    for at in range(low2, high2 + 1):
        for t in (1, 2, 3):
            u2[at, t] = weight_of(c2[at, t]) * f2[at, t]
    for at in range(low2 - 1, high2 + 2):
        for t in (1, 2, 3):
            center, total = around_tile(u2, at, t, 1, lane8, sub8)
            v2[at, t] = 0.2 * center + weight_of(c2[at, t]) * (total + f2[at, t])
    for at in range(low2 - 2, high2 + 3):
        center, total = around_tile(v2, at, 2, 1, lane8, sub8)
        r2[at] = f2[at, 2] + total - (6.0 + c2[at, 2]) * center

    planes = [0.5 * pair_sums(r2[2 * k + 1] + r2[2 * k + 2], lane8, sub8) for k in range(size2 // 2 + 4)]
    planes += [
        0.125 * pair_sums(c2[off2 + 2 * k, 2] + c2[off2 + 2 * k + 1, 2], lane8, sub8) for k in range(size2 // 2)
    ]
    planes = [take_lanes(plane, 2 * (lane8 & 63)) for plane in planes]
    for k in range(2):
        even, odd = (
            jnp.where(lane8 < 64, planes[4 * k + j], planes[4 * k + j + 1]) for j in (0, 2)
        )
        tile = jnp.where((sub8 & 1) == 0, even, odd)
        for at in range(chunk.shape[0]):
            chunk[at, k] = tile

    pairs = [(v2, 2, off2 - k, off2 + size2 - 1 + k) for k in (1, 2, 3)]
    pairs += [(f2, 2, off2 - k, off2 + size2 - 1 + k) for k in (1, 2)]
    pairs += [(f1, here1, off1 + k, off1 + size1 - 1 - k) for k in (-2, -1, 0, 1, 2)]
    pairs += [(w1, here1, off1 + k, off1 + size1 - 1 - k) for k in (2, 3)]
    for k, (ref, rows, at_left, at_right) in enumerate(pairs):
        left, right = ref[at_left, rows], ref[at_right, rows]
        a, b, at = (near_a, near_b, 8 * k) if k < 5 else (to_a, to_b, (k - 5) * rows1)
        target = pl.ds(at, left.shape[0])
        a[target] = jnp.where(even_x, right, left)
        b[target] = jnp.where(even_x, left, right)

    for early, near in ((early_a, near_a), (early_b, near_b)):
        near[pl.ds(40, early.shape[0])] = early[...]

    for at in range(size2 + 6):
        level2[at] = v2[at + 2, 2]
    for at in range(size2 + 4):
        level2[size2 + 6 + at] = f2[at + 3, 2]
    c2_out[...] = c2[pl.ds(2, size2 + 6), pl.ds(1, 3)]
    v1_out[0] = w1[off1 - 3, here1]
    v1_out[1] = w1[off1 + size1 + 2, here1]
    for copy in copies:
        copy.wait()


def meet_kernel(level2, xa, xb, level1_a, level1_b, later_a, later_b, _, own, to_a, to_b):
    even_x = lax.axis_index("gx") % 2 == 0
    size2 = own.shape[0] // 2
    planes = [level2[3 + x] for x in range(size2)] + [level2[size2 + 8 + x] for x in range(size2)]
    for k, (base, step) in enumerate(((0, 0), (0, 1), (0, 2), (size2, 0), (size2, 1))):
        rows = pl.ds(8 * k, 8)
        left = jnp.where(even_x, xb[rows], xa[rows])
        right = jnp.where(even_x, xa[rows], xb[rows])
        planes[base + step] = planes[base + step] + left
        planes[base + size2 - 1 - step] = planes[base + size2 - 1 - step] + right
    for k, plane in enumerate(planes):
        own[k] = plane
    size = level1_a.shape[0]
    for first, second, target in ((level1_a, later_a, to_a), (level1_b, later_b, to_b)):
        target[pl.ds(0, size)] = first[...]
        target[pl.ds(size, second.shape[0])] = second[...]


def follow_kernel(values, _, out):
    out[...] = values[...]


def past_tiles(za, zb, k, odd_z, lane):
    below = jnp.where(odd_z, za[k], zb[k])
    above = jnp.where(odd_z, zb[k], za[k])
    return jnp.where(lane >= 96, below, jnp.where(lane < 32, above, 0.0))


def side_kernel(own, za, zb, _, to_a, to_b):
    odd_z = lax.axis_index("gc") == 1
    even_x = lax.axis_index("gx") % 2 == 0
    size2 = own.shape[0] // 2
    lane = lanes_of(8)
    tiles = [(own[k], past_tiles(za, zb, k, odd_z, lane)) for k in range(2 * size2)]
    at = 0
    for base, count in ((0, size2), (size2, size2 - 1)):
        for k in range(count):
            for left, right in zip(tiles[base + k], tiles[base + size2 - 1 - k], strict=True):
                to_a[at] = jnp.where(even_x, right, left)
                to_b[at] = jnp.where(even_x, left, right)
                at += 1


def loop(count, body):
    if count <= 16:
        for i in range(count):
            body(i)
    else:
        lax.fori_loop(0, count, lambda i, _: (body(i), None)[1], None)


def coarse_kernel(
    nx, nz, own, other, inverse_far,
    window3, e_out,
    v3, f3, g3, c3, u3, turned, flat, inverse, arrivals,
):
    core = lax.axis_index("gc")
    ny = nz // 2
    lane, sub = lanes_of(8), subs_of(8)
    copies = []
    piece = inverse.shape[0] // 4
    for k in range(4):
        rows = pl.ds(k * piece, piece)
        copies.append(pltpu.make_async_copy(inverse_far.at[rows], inverse.at[rows], arrivals.at[k]))
        copies[k].start()
    for ref in (v3, f3, g3, u3):
        ref[...] = jnp.zeros(ref.shape, F32)

    def collect(at):
        for y in range(ny):
            for source, t in ((own, 1 + 2 * y + core), (other, 2 + 2 * y - core)):
                planes = []
                for k in range(2):
                    tile = source[at * ny + y, k]
                    even = jnp.where((sub & 1) == 0, tile, pltpu.roll(tile, 1, 0))
                    odd = jnp.where((sub & 1) == 1, tile, pltpu.roll(tile, 7, 0))
                    planes += [take_lanes(part, (lane >> 1) + 64 * j) for part in (even, odd) for j in (0, 1)]
                for k in range(6):
                    f3[2 * at + 2 + k, t] += planes[k]
                for k in range(2):
                    c3[2 * at + 4 + k, t] = planes[6 + k]

    loop(nx, collect)

    def third(at):
        for k in range(2):
            x = 4 + 2 * at + k
            for t in range(1, nz + 1):
                g3[x, t] = RELAX_WEIGHT / (6.0 + c3[x, t])
                u3[x, t] = g3[x, t] * f3[x, t]

    loop(nx, third)

    def fourth(at):
        for k in range(2):
            x = 4 + 2 * at + k
            for t in range(1, nz + 1):
                center, total = around_tile(u3, x, t, 2, lane, sub)
                v3[x, t] = 0.2 * center + g3[x, t] * (total + f3[x, t])

    loop(nx, fourth)

    step_x = 2 * nx // COARSE
    group = nz // 4

    for t in range(1, nz + 1):
        rows = []
        for xc in range(COARSE):
            total = 0.0
            for k in range(step_x):
                x = 4 + xc * step_x + k
                center, beside = around_tile(v3, x, t, 2, lane, sub)
                total += f3[x, t] + beside - (6.0 + c3[x, t]) * center
            rows.append(jnp.sum(total, axis=0, keepdims=True))
        block = 0.125 * jnp.concatenate(rows, axis=0)
        spread = block
        for k in range(1, group):
            spread = spread + pltpu.roll(block, LANES - 32 * k, 1)
        tall = jnp.concatenate([spread, jnp.zeros((LANES - COARSE, LANES), F32)], axis=0)
        turned[...] = tall.T
        line = jnp.zeros((8, LANES), F32)
        for k in range(8):
            piece = pltpu.roll(turned[pl.ds(2 * k, 8, stride=16), :], 16 * k, 1) if k else turned[pl.ds(0, 8, stride=16), :]
            line = jnp.where((lane >= 16 * k) & (lane < 16 * k + 16), piece, line)
        count = 4 // group
        for q in range(count):
            at = 2 * ((t - 1) * count + q)
            flat[at : at + 2] = line[2 * group * q : 2 * group * q + 2]

    at_x = lax.axis_index("gx")
    at_z = 2 * lax.axis_index("gy") + core
    for k, ref in enumerate((v3, f3, g3)):
        for t in range(3):
            window3[k, :, t] = ref[pl.ds(2 * at_x, 10), at_z + t]

    for copy in copies:
        copy.wait()
    total = None
    for t in range(inverse.shape[1] // LANES):
        piece = inverse[:, t * LANES : (t + 1) * LANES] * flat[t : t + 1]
        total = piece if total is None else total + piece
    column = jnp.sum(total, axis=1, keepdims=True)
    copies = e_out.shape[0]
    width = -(-copies // LANES) * LANES
    e_out[...] = jnp.broadcast_to(column, (inverse.shape[0], width)).T[:copies]


def top_level(nx, nz, e, window3, u3, lifted3, w3, turned):
    at_x = lax.axis_index("gx")
    at_z = 2 * lax.axis_index("gy") + lax.axis_index("gc")
    lane, sub = lanes_of(8), subs_of(8)
    step_x = 2 * nx // COARSE
    group = nz // 4

    for ref in (lifted3, u3, w3):
        ref[...] = jnp.zeros(ref.shape, F32)
    for t in range(1, nz + 1):
        pieces = []
        for q in range(4):
            at = 2 * (((t - 1) * 4 + q) // group)
            pieces.append(e[at : at + 2])
        rows = jnp.concatenate(pieces, axis=0)
        for k in range(8):
            piece = pltpu.roll(rows, LANES - 16 * k, 1) if k else rows
            turned[pl.ds(2 * k, 8, stride=16), :] = piece
            turned[pl.ds(2 * k + 1, 8, stride=16), :] = piece
        lifted = turned[...].T
        for xc in range(COARSE):
            tile = jnp.broadcast_to(lifted[xc : xc + 1], (8, LANES))
            for k in range(step_x):
                lifted3[4 + xc * step_x + k, t] = tile
    for x in range(10):
        for t in range(3):
            u3[x, t + 1] = window3[0, x, t] + lifted3[2 * at_x + x, at_z + t]
    for source, target, margin in ((u3, w3, 1), (w3, u3, 2)):
        for x in range(margin, 10 - margin):
            for t in range(3):
                center, total = around_tile(source, x, t + 1, 2, lane, sub)
                target[x, t + 1] = 0.2 * center + window3[2, x, t] * (total + window3[1, x, t])


def up_kernel(
    nx, nz, e, window3, own2, za, zb, sides_a, sides_b, c2, v_mid, v_edges, f_far, c_far, sides_far, f1_far, c1_in, f_ends, c_ends, v1_in, xa, xb, later_a, later_b,
    pressure_far, residual_far,
    u3, lifted3, w3, turned, u2, w2, f2, f1, c1, u1, w1, lift1, ua, ub, g, lift0, before_in, after_in, sources, v_in, f_in, c_in, f_held, c_held, c_sides, f1_in, pressure, residual, arrivals,
):
    even_x = lax.axis_index("gx") % 2 == 0
    lane, sub = lanes_of(8), subs_of(8)
    zeros8 = jnp.zeros((GUARD, LANES), F32)
    size_x = f_ends.shape[0]
    pairs = (
        (f1_far, f1_in), (sides_far, c_sides), (v_mid, v_in.at[pl.ds(3, size_x - 2)]),
        (v_edges.at[pl.ds(0, 3)], v_in.at[pl.ds(0, 3)]), (v_edges.at[pl.ds(3, 3)], v_in.at[pl.ds(size_x + 1, 3)]),
        (c_far, c_held), (f_far, f_held),
    )
    copies = [pltpu.make_async_copy(*pair, arrivals.at[k]) for k, pair in enumerate(pairs)]
    for copy in copies:
        copy.start()
    for ref in (u2, w2, f2):
        ref[...] = jnp.zeros(ref.shape, F32)

    top_level(nx, nz, e, window3, u3, lifted3, w3, turned)

    odd_z = lax.axis_index("gc") == 1
    size2 = own2.shape[0] // 2
    planes2 = size2 + 8
    for k in range(2 * size2):
        target = u2 if k < size2 else f2
        put_tiles(target, 4 + k % size2, own2[k], past_tiles(za, zb, k, odd_z, lane), lane)
    at = 0
    for target, count in ((u2, size2), (f2, size2 - 1)):
        for k in range(count):
            left = [jnp.where(even_x, sides_b[at + j], sides_a[at + j]) for j in (0, 1)]
            right = [jnp.where(even_x, sides_a[at + j], sides_b[at + j]) for j in (0, 1)]
            put_tiles(target, 3 - k, *left, lane)
            put_tiles(target, 4 + size2 + k, *right, lane)
            at += 2
    for x in range(planes2):
        for t in (1, 2, 3):
            u2[x, t] += u3[2 + x // 2, t]
    for source, target, margin in ((u2, w2, 1), (w2, u2, 2)):
        for x in range(margin, planes2 - margin):
            for t in (1, 2, 3):
                center, total = around_tile(source, x, t, 1, lane, sub)
                target[x, t] = 0.2 * center + weight_of(c2[x - 1, t - 1]) * (total + f2[x, t])

    rows1 = f1_in.shape[1]
    size1 = 2 * size2
    off1 = 4
    here1 = pl.ds(GUARD, rows1)
    lane1 = lanes_of(rows1)
    side = lane >> 6
    fine = (lane & 63) >> 1
    for x in range(2, planes2 - 2):
        below, middle, above = u2[x, 1], u2[x, 2], u2[x, 3]
        index = [(((2 * side + q) & 3) << 5) + fine for q in (-1, 0, 1, 2)]
        tiles = [
            jnp.where(side == 0, take_lanes(below, index[0]), take_lanes(middle, index[0]))[4:],
            take_lanes(middle, index[1]),
            take_lanes(middle, index[2]),
            jnp.where(side == 0, take_lanes(middle, index[3]), take_lanes(above, index[3]))[:4],
        ]
        start = 0
        for tile in tiles:
            count = tile.shape[0]
            lift1[x - 2, pl.ds(start, count, stride=2), :] = tile
            lift1[x - 2, pl.ds(start + 1, count, stride=2), :] = tile
            start += 2 * count

    kept = v_in.shape[1]

    def arrived(start, rows, a=xa, b=xb):
        a, b = a[pl.ds(start, rows)], b[pl.ds(start, rows)]
        return jnp.where(even_x, b, a), jnp.where(even_x, a, b)

    copies[0].wait()
    for x in range(-2, size1 + 2):
        f1[x + off1, here1] = f1_in[x + 2]
    for x in range(-3, size1 + 3):
        c1[x + off1, here1] = weight_of(c1_in[x + 3])
    for k in range(7):
        left, right = arrived(k * rows1, rows1, later_a, later_b)
        if k < 4:
            f1[off1 + 1 - k, here1] += left
            f1[off1 + size1 - 2 + k, here1] += right
        elif k == 4:
            f1[off1 - 3, here1] = left
            f1[off1 + size1 + 2, here1] = right
        else:
            w1[off1 + 2 - k, here1] = left + v1_in[0] if k == 5 else left
            w1[off1 + size1 - 3 + k, here1] = right + v1_in[1] if k == 5 else right
    planes1 = size1 + 8
    for ref in (u1, w1):
        for at in range(planes1):
            ref[at, pl.ds(0, GUARD)] = zeros8
            ref[at, pl.ds(GUARD + rows1, GUARD)] = zeros8
    for at in range(1, planes1 - 1):
        u1[at, here1] = c1[at, here1] * f1[at, here1]
    for at in range(planes1):
        value = w1[at, here1]
        if 2 <= at < planes1 - 2:
            center, total = around(u1, at, GUARD, rows1, lane1, 64)
            value = 0.2 * center + c1[at, here1] * (total + f1[at, here1])
        w1[at, here1] = value + lift1[at // 2]
    for source, target, margin in ((w1, u1, 1), (u1, w1, 2)):
        for at in range(margin, planes1 - margin):
            center, total = around(source, at, GUARD, rows1, lane1, 64)
            target[at, here1] = 0.2 * center + c1[at, here1] * (total + f1[at, here1])

    size_x = f_in.shape[0]
    size_z = kept - 2 * KEEP
    short = kept // 4
    index = lanes_of(short) >> 1
    for x in range(-2, size1 + 2):
        for part in range(2):
            source = w1[x + off1, pl.ds(GUARD + (4 if part == 0 else 8), short)]
            tile = take_lanes(source, index + 64 * part)
            lift0[x + 2, pl.ds(part * 2 * short, short, stride=2), :] = tile
            lift0[x + 2, pl.ds(part * 2 * short + 1, short, stride=2), :] = tile

    off = 3
    last = size_x + off - 1
    here = pl.ds(GUARD, kept)
    for ref in (ua, ub):
        for at in range(size_x + 6):
            ref[at, pl.ds(0, GUARD)] = zeros8
            ref[at, pl.ds(GUARD + kept, GUARD)] = zeros8
    for copy in copies[1:]:
        copy.wait()
    for held, part, target in ((f_held, f_ends, f_in), (c_held, c_ends, c_in)):
        for x in range(size_x):
            target[x, pl.ds(KEEP, size_z)] = held[x].T
        target[:, pl.ds(0, KEEP)] = part[:, pl.ds(0, KEEP)]
        target[:, pl.ds(KEEP + size_z, KEEP)] = part[:, pl.ds(KEEP, KEEP)]
    shift = -GUARD
    for x in range(-3, size_x + 3):
        value = lift0[(x + 4) // 2]
        if -2 <= x <= size_x + 1:
            value = value + v_in[x + 2, pl.ds(GUARD + shift, kept)]
        ua[x + off, here] = value
    half = kept // 2
    parts = [(GUARD, half), (GUARD + half, half)]
    laneh = lanes_of(half)
    beyond = {-2: 0, -1: 1, size_x: 2, size_x + 1: 3}
    for x in range(-2, size_x + 2):
        for start, rows in parts:
            at = pl.ds(start + shift, rows)
            g[x + 2, pl.ds(start, rows)] = weight_of(c_sides[beyond[x], at] if x in beyond else c_in[x, at])

    sent = size_z + 2 * SENT
    begin = GUARD + KEEP - SENT
    taken = pl.ds(begin, sent)
    lane_s = lanes_of(sent)
    for ref in (before_in, after_in, sources):
        ref[...] = jnp.zeros(ref.shape, F32)
    messages = [arrived(40 + k * sent, sent) for k in range(EARLY)]
    messages += [arrived(7 * rows1 + k * sent, sent, later_a, later_b) for k in range(5 - EARLY)]
    for side, (edge, inward) in enumerate(((off, 1), (last, -1))):
        before, after, source0, source1, source2 = (message[side] for message in messages)
        before_in[side, taken] = g[edge - 1, taken] * before
        after_in[side, taken] = after
        sources[side, taken] = source1
        sources[2 + side, taken] = source2
        center, total = around(before_in, side, begin, sent, lane_s, LANES, False, False)
        ua[edge, taken] += 0.2 * center + g[edge - 1, taken] * (total + after)
        ua[edge + inward, taken] += g[edge + inward - 1, taken] * center
        _, total = around(after_in, side, begin, sent, lane_s, LANES, False, False)
        ua[edge - inward, taken] += 0.2 * after + g[edge - inward - 1, taken] * (total + source0 + center)

    for sweep, (origin, target) in enumerate(((ua, ub), (ub, ua))):
        for at in range(1 + sweep, size_x + 5 - sweep):
            for start, rows in parts:
                center, total = around(origin, at, start, rows, laneh, LANES)
                x = at - off
                if 0 <= x < size_x:
                    total = total + f_in[x, pl.ds(start + shift, rows)]
                elif x in (-1, size_x):
                    total = total + sources[2 * sweep + (x > 0), pl.ds(start, rows)]
                target[at, pl.ds(start, rows)] = 0.2 * center + g[at - 1, pl.ds(start, rows)] * total
    lane_z = lanes_of(size_z)
    own = GUARD + KEEP
    piece = size_x // 4
    copies = []

    def leave(source, target, x):
        if (x + 1) % piece == 0:
            planes = pl.ds(x + 1 - piece, piece)
            copies.append(pltpu.make_async_copy(source.at[planes], target.at[planes], arrivals.at[len(copies)]))
            copies[-1].start()

    for x in range(size_x):
        pressure[x] = ua[x + off, pl.ds(own, size_z)].T
        leave(pressure, pressure_far, x)
    for x in range(size_x):
        center, total = around(ua, x + off, own, size_z, lane_z, LANES)
        mine = pl.ds(own + shift, size_z)
        total = total + f_in[x, mine]
        residual[x] = (total - (6.0 + c_in[x, mine]) * center).T
        leave(residual, residual_far, x)
    for copy in copies:
        copy.wait()


def pairs_of(count):
    even = [(i, i ^ 1) for i in range(count)]
    odd = [(i, ((i - 1) ^ 1) + 1) for i in range(1, count - 1)]
    return even, odd


def gather(copies, axes, always):
    return lax.cond(always, lambda x: lax.all_to_all(x, axes, 0, 0, tiled=True), lambda x: x, copies)


def local(nx, nz, right_side, reaction, initial, coarse_inverse):
    size_x, _, size_z = right_side.shape
    size1, size2 = size_x // 2, size_x // 4
    wide, kept, sent = (size_z + 2 * rows for rows in (DEEP, KEEP, SENT))
    deep = wide + 2 * GUARD
    rows1 = size_z // 4 + 2 * GUARD
    brick = (size_x, size_z, LANES)
    padded = (size_x, deep, LANES)
    padded1 = (size1, rows1 + 2 * GUARD, LANES)
    slab = (size_x, DEEP, LANES)
    always = lax.optimization_barrier(jnp.int32(1)) > 0
    flag = always.astype(jnp.int32).reshape(1, 1)
    c, f, mza, mzb = call(
        turn_kernel, "turn", (brick, brick, (2, *slab), (2, *slab)), (reaction, right_side, flag),
        [(2, *right_side.shape)], far_args=(0, 1), copies=8,
    )
    even_z, odd_z = pairs_of(nz)
    za = lax.ppermute(mza, ("gy", "gc"), even_z)
    zb = lax.ppermute(mzb, ("gy", "gc"), odd_z)
    v, mya, myb = call(turn_again_kernel, "turn_again", (brick, slab, slab), (initial, mza))
    ya = lax.ppermute(mya, ("gy", "gc"), even_z)
    yb = lax.ppermute(myb, ("gy", "gc"), odd_z)

    message = (2 * wide + 2 * rows1 + 32, LANES)
    mxa, mxb, c, c1 = call(
        coefficient_kernel, "coefficients", (message, message, padded, padded1), (c, za, zb, ya, yb)
    )
    even_x, odd_x = pairs_of(nx)
    xa = lax.ppermute(mxa, "gx", even_x)
    xb = lax.ppermute(mxb, "gx", odd_x)

    margin, later = (EARLY * sent, LANES), ((5 - EARLY) * sent, LANES)
    held, ends = (size_x, kept, LANES), (size_x, 2 * KEEP, LANES)
    f, v, edges, f1, mua, mub, mla, mlb, f_ends, c_ends, v_mid = call(
        inner_kernel, "inner",
        (padded, padded, (4, deep, LANES), (size1 - 2, rows1, LANES), margin, margin, later, later, ends, ends, (size_x - 2, kept, LANES)),
        (f, v, c, za, zb, ya, yb),
        [padded] * 4, far_outs=(10,), copies=1,
    )

    box2 = (size2 + 10, 5, 8, LANES)
    near, level1 = (40 + EARLY * sent, LANES), (7 * rows1, LANES)
    sides0, sides1 = (4, deep, LANES), (2, rows1, LANES)
    parts1 = (size1 + 4, rows1, LANES), (size1 + 6, rows1, LANES)
    field0 = (size_x + 4, deep, LANES)
    field1 = (size1 + 10, rows1 + 2 * GUARD, LANES)
    chunk, mna, mnb, m1a, m1b, v, c_sides, f1, c1, v1, level2, c2 = call(
        outer_kernel, "outer",
        (
            (nx * nz // 2, 2, 8, LANES), near, near, level1, level1,
            (6, kept, LANES), (4, kept, LANES), *parts1, sides1, (2 * size2 + 10, 8, LANES), (size2 + 6, 3, 8, LANES),
        ),
        (f, c, v, edges, f1, c1, mua, mub, xa, xb),
        [
            field0, sides0, (2, deep, LANES), (12, deep, LANES), field1, field1, field1, field1,
            box2, (size2 + 10, 8, LANES), box2, box2, box2,
        ],
        far_outs=range(5, 8), copies=4,
    )
    na = lax.ppermute(mna, "gx", even_x)
    nb = lax.ppermute(mnb, "gx", odd_x)
    own = gather(chunk, ("gx", "gy"), always)
    both = (7 * rows1 + (5 - EARLY) * sent, LANES)
    own2, mla, mlb = call(
        meet_kernel, "meet", ((2 * size2, 8, LANES), both, both), (level2, na, nb, m1a, m1b, mla, mlb, own)
    )
    la = lax.ppermute(mla, "gx", even_x)
    lb = lax.ppermute(mlb, "gx", odd_x)
    other = lax.ppermute(own, "gc", [(0, 1), (1, 0)])
    z2a = lax.ppermute(own2, ("gy", "gc"), even_z)
    z2b = lax.ppermute(own2, ("gy", "gc"), odd_z)
    grid3 = (2 * nx + 8, nz + 2, 8, LANES)
    rows = coarse_inverse.shape[0]
    window3, e = call(
        functools.partial(coarse_kernel, nx, nz), "coarse",
        ((3, 10, 3, 8, LANES), (nx * nz, rows)),
        (own, other, coarse_inverse),
        [*[grid3] * 5, (LANES, LANES), (COARSE**3 // LANES, LANES), coarse_inverse.shape],
        far_args=(2,), copies=4,
    )
    sides = (4 * size2 - 2, 8, LANES)
    msa, msb = call(side_kernel, "sides", (sides, sides), (own2, z2a, z2b, e))
    sa = lax.ppermute(msa, "gx", even_x)
    sb = lax.ppermute(msb, "gx", odd_x)
    (e,) = call(follow_kernel, "follow", (e.shape,), (e, msa))
    e = gather(e, ("gx", "gy", "gc"), always).reshape(COARSE**3 // LANES, LANES)

    near2 = (size2 + 8, 5, 8, LANES)
    box3 = (10, 5, 8, LANES)
    box = (size_x + 6, kept + 2 * GUARD, LANES)
    return call(
        functools.partial(up_kernel, nx, nz), "up",
        ((size_x, LANES, size_z), (size_x, LANES, size_z)),
        (e, window3, own2, z2a, z2b, sa, sb, c2, v_mid, v, right_side, reaction, c_sides, f1, c1, f_ends, c_ends, v1, na, nb, la, lb),
        [
            box3, grid3, box3, (LANES, LANES), near2, near2, near2,
            field1, field1, field1, field1, (size2 + 4, rows1, LANES),
            box, box, box, (size1 + 4, kept, LANES), *[(2, kept + 2 * GUARD, LANES)] * 2, (4, kept + 2 * GUARD, LANES),
            (size_x + 4, kept, LANES), held, held, right_side.shape, right_side.shape, (4, kept, LANES), parts1[0],
            right_side.shape, right_side.shape,
        ],
        far_args=range(8, 14), far_outs=(0, 1), copies=8, results=True,
    )


def solution(mesh):
    nx, nz = mesh.shape["gx"], mesh.shape["gz"]
    fine = Mesh(mesh.devices.reshape(nx, nz // 2, 2), ("gx", "gy", "gc"))
    brick = P("gx", None, ("gy", "gc"))
    return jax.shard_map(
        lambda *args: tuple(local(nx, nz, *args)),
        mesh=fine,
        in_specs=(brick, brick, brick, P(("gx", "gy", "gc"), None)),
        out_specs=(brick, brick),
        check_vma=False,
    )
```

```python
import functools
import math

import jax
import jax.numpy as jnp
from jax import lax
from jax.experimental import pallas as pl
from jax.experimental.pallas import tpu as pltpu
from jax.sharding import Mesh
from jax.sharding import PartitionSpec as P

COARSE = 16
RELAX_WEIGHT = 0.8
F32 = jnp.float32
LANES = 128
DEEP = 16
KEEP = 8
SENT = 4
GUARD = 8
EARLY = 2
MIB = 1 << 20


def lanes_of(rows):
    return lax.broadcasted_iota(jnp.int32, (rows, LANES), 1)


def subs_of(rows):
    return lax.broadcasted_iota(jnp.int32, (rows, LANES), 0)


def take_lanes(values, index):
    return jnp.take_along_axis(values, index, axis=1, mode="promise_in_bounds")


def beside_lanes(values, lane, width, step):
    place = lane & (width - 1)
    low = jnp.where(place >= step, pltpu.roll(values, step, 1), 0.0)
    high = jnp.where(place < width - step, pltpu.roll(values, LANES - step, 1), 0.0)
    return low + high


def weight_of(c):
    return jnp.where(c > 0.0, RELAX_WEIGHT / (6.0 + c), 0.0)


def around(ref, at, start, rows, lane, width, lower=True, upper=True):
    center = ref[at, pl.ds(start, rows)]
    total = ref[at, pl.ds(start - 1, rows)] + ref[at, pl.ds(start + 1, rows)]
    total = total + beside_lanes(center, lane, width, 1)
    if lower:
        total = total + ref[at - 1, pl.ds(start, rows)]
    if upper:
        total = total + ref[at + 1, pl.ds(start, rows)]
    return center, total


def halve_two(ref, planes, lane, first, rows):
    index = 2 * (lane & 63)

    def part(start):
        total = None
        for at in planes:
            for odd in (0, 1):
                piece = ref[at, pl.ds(start + odd, rows, stride=2), :]
                total = piece if total is None else total + piece
        total = total + pltpu.roll(total, LANES - 1, 1)
        return take_lanes(total, index)

    return jnp.where(lane < 64, part(first), part(first + 64))


def halve_four(ref, planes, lane8, first):
    total = None
    for at in planes:
        for odd in (0, 1):
            piece = ref[at, pl.ds(first + odd, 16, stride=2), :]
            total = piece if total is None else total + piece
    total = total + pltpu.roll(total, LANES - 1, 1)
    index = (lane8 & 64) + 2 * (lane8 & 31)
    return jnp.where((lane8 & 32) == 0, take_lanes(total[:8], index), take_lanes(total[8:], index))


def around_tile(ref, x, t, step, lane, sub):
    center = ref[x, t]
    total = ref[x - 1, t] + ref[x + 1, t] + beside_lanes(center, lane, 32, step)
    after = pltpu.roll(jnp.where(lane < 32, ref[x, t + 1], center), LANES - 32, 1)
    total = total + pltpu.roll(jnp.where(sub < step, after, center), 8 - step, 0)
    before = pltpu.roll(jnp.where(lane >= 96, ref[x, t - 1], center), 32, 1)
    total = total + pltpu.roll(jnp.where(sub >= 8 - step, before, center), step, 0)
    return center, total


def pair_sums(values, lane, sub):
    partner = jnp.where((lane & 1) == 0, pltpu.roll(values, LANES - 1, 1), pltpu.roll(values, 1, 1))
    values = values + partner
    partner = jnp.where((sub & 1) == 0, pltpu.roll(values, 7, 0), pltpu.roll(values, 1, 0))
    return values + partner


def halve_tiles(ref, planes, lane, sub, beyond):
    def edge(start):
        total = None
        for at in planes:
            for odd in (0, 1):
                piece = ref[at, pl.ds(start + odd, 4, stride=2), :]
                total = piece if total is None else total + piece
        return total

    past = jnp.concatenate([edge(beyond), edge(GUARD)], axis=0)
    past = past + pltpu.roll(past, LANES - 1, 1)
    past = take_lanes(past, jnp.where(sub < 4, 64, 0) + 2 * (lane & 31))
    kept = ((sub < 4) & (lane < 32)) | ((sub >= 4) & (lane >= 96))
    return halve_four(ref, planes, lane, 2 * GUARD), jnp.where(kept, past, 0.0)


def put_tiles(target, at, own, past, lane):
    target[at, 2] = own
    target[at, 1] = jnp.where(lane >= 96, past, 0.0)
    target[at, 3] = jnp.where(lane < 32, past, 0.0)


def call(kernel, name, outs, args, scratch=(), far_args=(), far_outs=(), copies=0, results=False, micros=1):
    limit = sum(4 * math.prod(s) for s in scratch) + 6 * MIB
    spaces_in = [pltpu.HBM if k in far_args else pltpu.VMEM for k in range(len(args))]
    spaces_out = [pltpu.HBM if k in far_outs else pltpu.VMEM for k in range(len(outs))]
    spaces_in = [pltpu.SMEM if a.dtype == jnp.int32 else space for a, space in zip(args, spaces_in, strict=True)]
    args = [
        a if space == pltpu.SMEM else pltpu.with_memory_space_constraint(a, space)
        for a, space in zip(args, spaces_in, strict=True)
    ]
    return pl.pallas_call(
        kernel,
        out_shape=[
            jax.ShapeDtypeStruct(s, F32) if results else space(s, F32)
            for s, space in zip(outs, spaces_out, strict=True)
        ],
        in_specs=[pl.BlockSpec(memory_space=space) for space in spaces_in],
        out_specs=[pl.BlockSpec(memory_space=space) for space in spaces_out],
        scratch_shapes=[pltpu.VMEM(s, F32) for s in scratch] + [pltpu.SemaphoreType.DMA((copies,))] * (copies > 0),
        compiler_params=pltpu.CompilerParams(vmem_limit_bytes=limit),
        cost_estimate=pl.CostEstimate(flops=0, bytes_accessed=3_000_000 * micros, transcendentals=0),
        name=name,
    )(*args)


def edge_rows(source, to_a, to_b):
    odd = lax.axis_index("gc")
    far = source.shape[1] - DEEP
    to_a[...] = source[:, pl.ds(pl.multiple_of((1 - odd) * far, DEEP), DEEP), :]
    to_b[...] = source[:, pl.ds(pl.multiple_of(odd * far, DEEP), DEEP), :]


def turn_kernel(*refs):
    *refs, held, arrivals = refs
    count = (len(refs) - 3) // 2
    sources, targets, (to_a, to_b) = refs[:count], refs[count + 1 : 2 * count + 1], refs[2 * count + 1 :]
    piece = targets[0].shape[0] // 4
    copies = []
    for which, source in enumerate(sources):
        for k in range(4):
            planes = pl.ds(k * piece, piece)
            copies.append(
                pltpu.make_async_copy(source.at[planes], held.at[which, planes], arrivals.at[4 * which + k])
            )
            copies[-1].start()
    for which, target in enumerate(targets):
        for k in range(4):
            copies[4 * which + k].wait()
            for x in range(k * piece, (k + 1) * piece):
                target[x] = held[which, x].T
        edge_rows(target, to_a.at[which], to_b.at[which])


def turn_again_kernel(v_in, _, v_out, to_a, to_b):
    for x in range(v_out.shape[0]):
        v_out[x] = v_in[x].T
    edge_rows(v_out, to_a, to_b)


def fill_rows(target, at, own, low, high):
    rows = own.shape[0]
    target[at, pl.ds(GUARD, DEEP)] = low
    target[at, pl.ds(GUARD + DEEP, rows)] = own
    target[at, pl.ds(GUARD + DEEP + rows, DEEP)] = high


def coefficient_kernel(c_in, za, zb, _, __, to_a, to_b, padded, c1):
    odd_z = lax.axis_index("gc") == 1
    even_x = lax.axis_index("gx") % 2 == 0
    size_x, size_z, _ = c_in.shape
    wide = pl.ds(GUARD, size_z + 2 * DEEP)
    rows1 = size_z // 4 + 2 * GUARD
    here1 = pl.ds(GUARD, rows1)
    lane, lane8, sub8 = lanes_of(rows1), lanes_of(8), subs_of(8)
    for x in range(size_x):
        low = jnp.where(odd_z, za[0, x], zb[0, x])
        high = jnp.where(odd_z, zb[0, x], za[0, x])
        fill_rows(padded, x, c_in[x], low, high)
    for x in range(size_x // 2):
        c1[x, here1] = 0.125 * halve_two(padded, (2 * x, 2 * x + 1), lane, GUARD, rows1)
    sides = []
    for order, order1 in ((range(size_x), range(8)), (range(size_x - 1, -1, -1), range(7, -1, -1))):
        tiles = []
        for k in (2, 4):
            tiles += [0.125 * tile for tile in halve_tiles(c1, order1[k : k + 2], lane8, sub8, rows1)]
        sides.append(
            [padded[order[0], wide], padded[order[1], wide], c1[order1[1], here1], c1[order1[2], here1], *tiles]
        )
    start = 0
    for left, right in zip(*sides, strict=True):
        rows = pl.ds(start, left.shape[0])
        to_a[rows] = jnp.where(even_x, right, left)
        to_b[rows] = jnp.where(even_x, left, right)
        start += left.shape[0]


def inner_kernel(
    f_in, v_in, c, za, zb, ya, yb,
    f, v2, edges, f1, to_a, to_b, later_a, later_b, f_ends, c_ends, v_far,
    va, vb, g, r, arrivals,
):
    odd_z = lax.axis_index("gc") == 1
    even_x = lax.axis_index("gx") % 2 == 0
    size_x, size_z, _ = f_in.shape
    wide = size_z + 2 * DEEP
    half = wide // 2
    parts = [(GUARD, half), (GUARD + half, half)]
    last = size_x - 1
    lane = lanes_of(half)
    zeros8 = jnp.zeros((GUARD, LANES), F32)

    for source, target, a, b in ((f_in, f, za.at[1], zb.at[1]), (v_in, va, ya, yb)):
        for x in range(size_x):
            low = jnp.where(odd_z, a[x], b[x])
            high = jnp.where(odd_z, b[x], a[x])
            fill_rows(target, x, source[x], low, high)
    for ref in (va, vb, v2):
        for x in range(size_x):
            ref[x, pl.ds(0, GUARD)] = zeros8
            ref[x, pl.ds(GUARD + wide, GUARD)] = zeros8
    for x in range(size_x):
        for start, rows in parts:
            here = pl.ds(start, rows)
            g[x, here] = weight_of(c[x, here])
    for source, target in ((va, vb), (vb, v2)):
        for x in range(size_x):
            for start, rows in parts:
                here = pl.ds(start, rows)
                center, total = around(source, x, start, rows, lane, LANES, x > 0, x < last)
                target[x, here] = 0.2 * center + g[x, here] * (total + f[x, here])
    copy = pltpu.make_async_copy(
        v2.at[pl.ds(1, size_x - 2), pl.ds(GUARD + DEEP - KEEP, size_z + 2 * KEEP)], v_far, arrivals.at[0]
    )
    copy.start()
    for x in range(2, last - 1):
        for start, rows in parts:
            here = pl.ds(start, rows)
            center, total = around(v2, x, start, rows, lane, LANES)
            r[x, here] = total + f[x, here] - (6.0 + c[x, here]) * center
    rows1 = size_z // 4 + 2 * GUARD
    lane1 = lanes_of(rows1)
    for x in range(1, size_x // 2 - 1):
        f1[x - 1] = 0.5 * halve_two(r, (2 * x, 2 * x + 1), lane1, GUARD, rows1)
    edges[0], edges[1], edges[2], edges[3] = va[0], va[last], vb[0], vb[last]

    sent = size_z + 2 * SENT
    first = GUARD + DEEP - SENT
    here = pl.ds(first, sent)
    lane = lanes_of(sent)
    sides = []
    for edge, second in ((0, 1), (last, last - 1)):
        center, total = around(v2, second, first, sent, lane, LANES, second != 1, second == 1)
        swept = 0.2 * center + g[second, here] * (total + f[second, here])
        source = f[edge, here]
        sides.append((va[edge, here], vb[edge, here], source + vb[second, here], source + center, source + swept))
    for k, (left, right) in enumerate(zip(*sides, strict=True)):
        a, b, rows = (to_a, to_b, pl.ds(k * sent, sent)) if k < EARLY else (later_a, later_b, pl.ds((k - EARLY) * sent, sent))
        a[rows] = jnp.where(even_x, right, left)
        b[rows] = jnp.where(even_x, left, right)
    for source, target in ((f, f_ends), (c, c_ends)):
        target[:, pl.ds(0, KEEP)] = source[:, pl.ds(GUARD + DEEP - KEEP, KEEP)]
        target[:, pl.ds(KEEP, KEEP)] = source[:, pl.ds(GUARD + DEEP + size_z, KEEP)]
    copy.wait()


def outer_kernel(
    f, c, v2_in, edges, f1_in, c1_in, early_a, early_b, xa, xb,
    chunk, near_a, near_b, to_a, to_b, v_far, sides_far, f1_far, c1_out, v1_out, level2, c2_out,
    v, c_out, v1, r, f1, c1, u1, w1, u2, r2, v2, f2, c2, arrivals,
):
    even_x = lax.axis_index("gx") % 2 == 0
    size_x = f.shape[0]
    size_z = f.shape[1] - 2 * DEEP - 2 * GUARD
    wide = size_z + 2 * DEEP
    half = wide // 2
    parts = [(GUARD, half), (GUARD + half, half)]
    lane = lanes_of(half)
    zeros8 = jnp.zeros((GUARD, LANES), F32)

    copies = []

    def keep(source, target):
        copies.append(pltpu.make_async_copy(source, target, arrivals.at[len(copies)]))
        copies[-1].start()

    kept = pl.ds(GUARD + DEEP - KEEP, size_z + 2 * KEEP)

    for x in (0, 1, 2, size_x - 3, size_x - 2, size_x - 1):
        v[x + 2] = v2_in[x]
    for ref, planes in ((v, (0, 1, size_x + 2, size_x + 3)), (v1, (0, 1))):
        for at in planes:
            ref[at, pl.ds(0, GUARD)] = zeros8
            ref[at, pl.ds(GUARD + wide, GUARD)] = zeros8
    for k in range(2):
        rows, here = pl.ds(k * wide, wide), pl.ds(GUARD, wide)
        c_out[1 - k, here] = jnp.where(even_x, xb[rows], xa[rows])
        c_out[2 + k, here] = jnp.where(even_x, xa[rows], xb[rows])
    last = size_x - 1
    for side, (edge, inward) in enumerate(((0, 1), (last, -1))):
        at = edge + 2
        beside, past = (1, 0) if side == 0 else (2, 3)
        for start, rows in parts:
            here = pl.ds(start, rows)
            v1[side, here] = weight_of(c_out[beside, here]) * edges[side, here]
        for start, rows in parts:
            here = pl.ds(start, rows)
            center, total = around(v1, side, start, rows, lane, LANES, False, False)
            v[at - inward, here] = 0.2 * center + weight_of(c_out[beside, here]) * (total + edges[2 + side, here])
            v[at - 2 * inward, here] = weight_of(c_out[past, here]) * center
            v[at, here] += weight_of(c[edge, here]) * center
        base = 0 if side == 0 else 11
        for start, rows in parts:
            here = pl.ds(start, rows)
            r[base + inward, here] = v[at - 2 * inward, here]
            for k in range(-2, 2):
                plane = at + k * inward
                center, total = around(
                    v, plane, start, rows, lane, LANES, not (side == 0 and k == -2), not (side == 1 and k == -2)
                )
                if k >= 0:
                    total = total + f[plane - 2, here]
                    weight = 6.0 + c[plane - 2, here]
                else:
                    weight = 6.0 + c_out[beside if k == -1 else past, here]
                r[base + (4 + k) * inward, here] = total - weight * center

    for k, at in enumerate((0, size_x + 1)):
        keep(v.at[pl.ds(at, 3), kept], v_far.at[pl.ds(3 * k, 3)])
    keep(c_out.at[:, kept], sides_far)

    rows1 = size_z // 4 + 2 * GUARD
    size1 = size_x // 2
    off1 = 5
    here1 = pl.ds(GUARD, rows1)
    lane1 = lanes_of(rows1)
    for x in range(1, size1 - 1):
        f1[x + off1, here1] = f1_in[x - 1]
    for x, planes in (
        (-2, (1,)), (-1, (2, 3)), (0, (4, 5)), (size1 - 1, (6, 7)), (size1, (8, 9)), (size1 + 1, (10,))
    ):
        f1[x + off1, here1] = 0.5 * halve_two(r, planes, lane1, GUARD, rows1)
    for x in range(size1):
        c1[x + off1, here1] = c1_in[x, here1]
    c1[off1 - 1, here1] = 0.125 * halve_two(c_out, (0, 1), lane1, GUARD, rows1)
    c1[off1 + size1, here1] = 0.125 * halve_two(c_out, (2, 3), lane1, GUARD, rows1)
    for k in range(2):
        rows = pl.ds(2 * wide + k * rows1, rows1)
        c1[off1 - 2 - k, here1] = jnp.where(even_x, xb[rows], xa[rows])
        c1[off1 + size1 + 1 + k, here1] = jnp.where(even_x, xa[rows], xb[rows])
    low1, high1 = off1 - 2, off1 + size1 + 1
    keep(f1.at[pl.ds(off1 - 2, size1 + 4), here1], f1_far)
    c1_out[...] = c1[pl.ds(off1 - 3, size1 + 6), here1]
    for at in range(low1 - 1, high1 + 2):
        for ref in (u1, w1):
            ref[at, pl.ds(0, GUARD)] = zeros8
            ref[at, pl.ds(GUARD + rows1, GUARD)] = zeros8
    for at in range(low1, high1 + 1):
        u1[at, here1] = weight_of(c1[at, here1]) * f1[at, here1]
    for at in range(low1 - 1, high1 + 2):
        weight = weight_of(c1[at, here1])
        if at == low1 - 1:
            w1[at, here1] = weight * u1[at + 1, here1]
        elif at == high1 + 1:
            w1[at, here1] = weight * u1[at - 1, here1]
        else:
            center, total = around(u1, at, GUARD, rows1, lane1, 64, at > low1, at < high1)
            w1[at, here1] = 0.2 * center + weight * (total + f1[at, here1])
    for at in range(low1 - 2, high1 + 3):
        if at == low1 - 2:
            u1[at, here1] = w1[at + 1, here1]
        elif at == high1 + 2:
            u1[at, here1] = w1[at - 1, here1]
        else:
            center, total = around(w1, at, GUARD, rows1, lane1, 64, at > low1 - 1, at < high1 + 1)
            if low1 <= at <= high1:
                total = total + f1[at, here1]
            u1[at, here1] = total - (6.0 + c1[at, here1]) * center

    size2 = size_x // 4
    off2 = 5
    low2, high2 = off2 - 2, off2 + size2 + 1
    lane8, sub8 = lanes_of(8), subs_of(8)
    for ref in (v2, f2, c2, u2):
        ref[...] = jnp.zeros(ref.shape, F32)
    for x in range(-2, size2 + 2):
        own, past = halve_tiles(u1, (2 * x + off1, 2 * x + off1 + 1), lane8, sub8, rows1)
        put_tiles(f2, x + off2, 0.5 * own, 0.5 * past, lane8)
    for x in range(-1, size2 + 1):
        own, past = halve_tiles(c1, (2 * x + off1, 2 * x + off1 + 1), lane8, sub8, rows1)
        put_tiles(c2, x + off2, 0.125 * own, 0.125 * past, lane8)
    for k in range(2):
        own, past = (pl.ds(2 * wide + 2 * rows1 + 8 * (2 * k + j), 8) for j in (0, 1))
        put_tiles(
            c2, low2 - k, jnp.where(even_x, xb[own], xa[own]), jnp.where(even_x, xb[past], xa[past]), lane8
        )
        put_tiles(
            c2, high2 + k, jnp.where(even_x, xa[own], xb[own]), jnp.where(even_x, xa[past], xb[past]), lane8
        )
    for at in range(low2, high2 + 1):
        for t in (1, 2, 3):
            u2[at, t] = weight_of(c2[at, t]) * f2[at, t]
    for at in range(low2 - 1, high2 + 2):
        for t in (1, 2, 3):
            center, total = around_tile(u2, at, t, 1, lane8, sub8)
            v2[at, t] = 0.2 * center + weight_of(c2[at, t]) * (total + f2[at, t])
    for at in range(low2 - 2, high2 + 3):
        center, total = around_tile(v2, at, 2, 1, lane8, sub8)
        r2[at] = f2[at, 2] + total - (6.0 + c2[at, 2]) * center

    planes = [0.5 * pair_sums(r2[2 * k + 1] + r2[2 * k + 2], lane8, sub8) for k in range(size2 // 2 + 4)]
    planes += [
        0.125 * pair_sums(c2[off2 + 2 * k, 2] + c2[off2 + 2 * k + 1, 2], lane8, sub8) for k in range(size2 // 2)
    ]
    planes = [take_lanes(plane, 2 * (lane8 & 63)) for plane in planes]
    for k in range(2):
        even, odd = (
            jnp.where(lane8 < 64, planes[4 * k + j], planes[4 * k + j + 1]) for j in (0, 2)
        )
        tile = jnp.where((sub8 & 1) == 0, even, odd)
        for at in range(chunk.shape[0]):
            chunk[at, k] = tile

    pairs = [(v2, 2, off2 - k, off2 + size2 - 1 + k) for k in (1, 2, 3)]
    pairs += [(f2, 2, off2 - k, off2 + size2 - 1 + k) for k in (1, 2)]
    pairs += [(f1, here1, off1 + k, off1 + size1 - 1 - k) for k in (-2, -1, 0, 1, 2)]
    pairs += [(w1, here1, off1 + k, off1 + size1 - 1 - k) for k in (2, 3)]
    for k, (ref, rows, at_left, at_right) in enumerate(pairs):
        left, right = ref[at_left, rows], ref[at_right, rows]
        a, b, at = (near_a, near_b, 8 * k) if k < 5 else (to_a, to_b, (k - 5) * rows1)
        target = pl.ds(at, left.shape[0])
        a[target] = jnp.where(even_x, right, left)
        b[target] = jnp.where(even_x, left, right)

    for early, near in ((early_a, near_a), (early_b, near_b)):
        near[pl.ds(40, early.shape[0])] = early[...]

    for at in range(size2 + 6):
        level2[at] = v2[at + 2, 2]
    for at in range(size2 + 4):
        level2[size2 + 6 + at] = f2[at + 3, 2]
    c2_out[...] = c2[pl.ds(2, size2 + 6), pl.ds(1, 3)]
    v1_out[0] = w1[off1 - 3, here1]
    v1_out[1] = w1[off1 + size1 + 2, here1]
    for copy in copies:
        copy.wait()


def meet_kernel(level2, xa, xb, level1_a, level1_b, later_a, later_b, _, own, to_a, to_b):
    even_x = lax.axis_index("gx") % 2 == 0
    size2 = own.shape[0] // 2
    planes = [level2[3 + x] for x in range(size2)] + [level2[size2 + 8 + x] for x in range(size2)]
    for k, (base, step) in enumerate(((0, 0), (0, 1), (0, 2), (size2, 0), (size2, 1))):
        rows = pl.ds(8 * k, 8)
        left = jnp.where(even_x, xb[rows], xa[rows])
        right = jnp.where(even_x, xa[rows], xb[rows])
        planes[base + step] = planes[base + step] + left
        planes[base + size2 - 1 - step] = planes[base + size2 - 1 - step] + right
    for k, plane in enumerate(planes):
        own[k] = plane
    size = level1_a.shape[0]
    for first, second, target in ((level1_a, later_a, to_a), (level1_b, later_b, to_b)):
        target[pl.ds(0, size)] = first[...]
        target[pl.ds(size, second.shape[0])] = second[...]


def follow_kernel(values, _, out):
    out[...] = values[...]


def past_tiles(za, zb, k, odd_z, lane):
    below = jnp.where(odd_z, za[k], zb[k])
    above = jnp.where(odd_z, zb[k], za[k])
    return jnp.where(lane >= 96, below, jnp.where(lane < 32, above, 0.0))


def side_kernel(own, za, zb, _, to_a, to_b):
    odd_z = lax.axis_index("gc") == 1
    even_x = lax.axis_index("gx") % 2 == 0
    size2 = own.shape[0] // 2
    lane = lanes_of(8)
    tiles = [(own[k], past_tiles(za, zb, k, odd_z, lane)) for k in range(2 * size2)]
    at = 0
    for base, count in ((0, size2), (size2, size2 - 1)):
        for k in range(count):
            for left, right in zip(tiles[base + k], tiles[base + size2 - 1 - k], strict=True):
                to_a[at] = jnp.where(even_x, right, left)
                to_b[at] = jnp.where(even_x, left, right)
                at += 1


def loop(count, body):
    if count <= 16:
        for i in range(count):
            body(i)
    else:
        lax.fori_loop(0, count, lambda i, _: (body(i), None)[1], None)


def coarse_kernel(
    nx, nz, own, other, inverse_far,
    window3, e_out,
    v3, f3, g3, c3, u3, turned, flat, inverse, arrivals,
):
    core = lax.axis_index("gc")
    ny = nz // 2
    lane, sub = lanes_of(8), subs_of(8)
    copies = []
    piece = inverse.shape[0] // 4
    for k in range(4):
        rows = pl.ds(k * piece, piece)
        copies.append(pltpu.make_async_copy(inverse_far.at[rows], inverse.at[rows], arrivals.at[k]))
        copies[k].start()
    for ref in (v3, f3, g3, u3):
        ref[...] = jnp.zeros(ref.shape, F32)

    def collect(at):
        for y in range(ny):
            for source, t in ((own, 1 + 2 * y + core), (other, 2 + 2 * y - core)):
                planes = []
                for k in range(2):
                    tile = source[at * ny + y, k]
                    even = jnp.where((sub & 1) == 0, tile, pltpu.roll(tile, 1, 0))
                    odd = jnp.where((sub & 1) == 1, tile, pltpu.roll(tile, 7, 0))
                    planes += [take_lanes(part, (lane >> 1) + 64 * j) for part in (even, odd) for j in (0, 1)]
                for k in range(6):
                    f3[2 * at + 2 + k, t] += planes[k]
                for k in range(2):
                    c3[2 * at + 4 + k, t] = planes[6 + k]

    loop(nx, collect)

    def third(at):
        for k in range(2):
            x = 4 + 2 * at + k
            for t in range(1, nz + 1):
                g3[x, t] = RELAX_WEIGHT / (6.0 + c3[x, t])
                u3[x, t] = g3[x, t] * f3[x, t]

    loop(nx, third)

    def fourth(at):
        for k in range(2):
            x = 4 + 2 * at + k
            for t in range(1, nz + 1):
                center, total = around_tile(u3, x, t, 2, lane, sub)
                v3[x, t] = 0.2 * center + g3[x, t] * (total + f3[x, t])

    loop(nx, fourth)

    step_x = 2 * nx // COARSE
    group = nz // 4

    for t in range(1, nz + 1):
        rows = []
        for xc in range(COARSE):
            total = 0.0
            for k in range(step_x):
                x = 4 + xc * step_x + k
                center, beside = around_tile(v3, x, t, 2, lane, sub)
                total += f3[x, t] + beside - (6.0 + c3[x, t]) * center
            rows.append(jnp.sum(total, axis=0, keepdims=True))
        block = 0.125 * jnp.concatenate(rows, axis=0)
        spread = block
        for k in range(1, group):
            spread = spread + pltpu.roll(block, LANES - 32 * k, 1)
        tall = jnp.concatenate([spread, jnp.zeros((LANES - COARSE, LANES), F32)], axis=0)
        turned[...] = tall.T
        line = jnp.zeros((8, LANES), F32)
        for k in range(8):
            piece = pltpu.roll(turned[pl.ds(2 * k, 8, stride=16), :], 16 * k, 1) if k else turned[pl.ds(0, 8, stride=16), :]
            line = jnp.where((lane >= 16 * k) & (lane < 16 * k + 16), piece, line)
        count = 4 // group
        for q in range(count):
            at = 2 * ((t - 1) * count + q)
            flat[at : at + 2] = line[2 * group * q : 2 * group * q + 2]

    at_x = lax.axis_index("gx")
    at_z = 2 * lax.axis_index("gy") + core
    for k, ref in enumerate((v3, f3, g3)):
        for t in range(3):
            window3[k, :, t] = ref[pl.ds(2 * at_x, 10), at_z + t]

    for copy in copies:
        copy.wait()
    total = None
    for t in range(inverse.shape[1] // LANES):
        piece = inverse[:, t * LANES : (t + 1) * LANES] * flat[t : t + 1]
        total = piece if total is None else total + piece
    column = jnp.sum(total, axis=1, keepdims=True)
    copies = e_out.shape[0]
    width = -(-copies // LANES) * LANES
    e_out[...] = jnp.broadcast_to(column, (inverse.shape[0], width)).T[:copies]


def top_level(nx, nz, e, window3, u3, lifted3, w3, turned):
    at_x = lax.axis_index("gx")
    at_z = 2 * lax.axis_index("gy") + lax.axis_index("gc")
    lane, sub = lanes_of(8), subs_of(8)
    step_x = 2 * nx // COARSE
    group = nz // 4

    for ref in (lifted3, u3, w3):
        ref[...] = jnp.zeros(ref.shape, F32)
    for t in range(1, nz + 1):
        pieces = []
        for q in range(4):
            at = 2 * (((t - 1) * 4 + q) // group)
            pieces.append(e[at : at + 2])
        rows = jnp.concatenate(pieces, axis=0)
        for k in range(8):
            piece = pltpu.roll(rows, LANES - 16 * k, 1) if k else rows
            turned[pl.ds(2 * k, 8, stride=16), :] = piece
            turned[pl.ds(2 * k + 1, 8, stride=16), :] = piece
        lifted = turned[...].T
        for xc in range(COARSE):
            tile = jnp.broadcast_to(lifted[xc : xc + 1], (8, LANES))
            for k in range(step_x):
                lifted3[4 + xc * step_x + k, t] = tile
    for x in range(10):
        for t in range(3):
            u3[x, t + 1] = window3[0, x, t] + lifted3[2 * at_x + x, at_z + t]
    for source, target, margin in ((u3, w3, 1), (w3, u3, 2)):
        for x in range(margin, 10 - margin):
            for t in range(3):
                center, total = around_tile(source, x, t + 1, 2, lane, sub)
                target[x, t + 1] = 0.2 * center + window3[2, x, t] * (total + window3[1, x, t])


def up_kernel(
    nx, nz, e, window3, own2, za, zb, sides_a, sides_b, c2, v_mid, v_edges, f_far, c_far, sides_far, f1_far, c1_in, f_ends, c_ends, v1_in, xa, xb, later_a, later_b,
    pressure_far, residual_far,
    u3, lifted3, w3, turned, u2, w2, f2, f1, c1, u1, w1, lift1, ua, ub, g, lift0, before_in, after_in, sources, v_in, f_in, c_in, f_held, c_held, c_sides, f1_in, pressure, residual, arrivals,
):
    even_x = lax.axis_index("gx") % 2 == 0
    lane, sub = lanes_of(8), subs_of(8)
    zeros8 = jnp.zeros((GUARD, LANES), F32)
    size_x = f_ends.shape[0]
    pairs = (
        (f1_far, f1_in), (sides_far, c_sides), (v_mid, v_in.at[pl.ds(3, size_x - 2)]),
        (v_edges.at[pl.ds(0, 3)], v_in.at[pl.ds(0, 3)]), (v_edges.at[pl.ds(3, 3)], v_in.at[pl.ds(size_x + 1, 3)]),
        (c_far, c_held), (f_far, f_held),
    )
    copies = [pltpu.make_async_copy(*pair, arrivals.at[k]) for k, pair in enumerate(pairs)]
    for copy in copies:
        copy.start()
    for ref in (u2, w2, f2):
        ref[...] = jnp.zeros(ref.shape, F32)

    top_level(nx, nz, e, window3, u3, lifted3, w3, turned)

    odd_z = lax.axis_index("gc") == 1
    size2 = own2.shape[0] // 2
    planes2 = size2 + 8
    for k in range(2 * size2):
        target = u2 if k < size2 else f2
        put_tiles(target, 4 + k % size2, own2[k], past_tiles(za, zb, k, odd_z, lane), lane)
    at = 0
    for target, count in ((u2, size2), (f2, size2 - 1)):
        for k in range(count):
            left = [jnp.where(even_x, sides_b[at + j], sides_a[at + j]) for j in (0, 1)]
            right = [jnp.where(even_x, sides_a[at + j], sides_b[at + j]) for j in (0, 1)]
            put_tiles(target, 3 - k, *left, lane)
            put_tiles(target, 4 + size2 + k, *right, lane)
            at += 2
    for x in range(planes2):
        for t in (1, 2, 3):
            u2[x, t] += u3[2 + x // 2, t]
    for source, target, margin in ((u2, w2, 1), (w2, u2, 2)):
        for x in range(margin, planes2 - margin):
            for t in (1, 2, 3):
                center, total = around_tile(source, x, t, 1, lane, sub)
                target[x, t] = 0.2 * center + weight_of(c2[x - 1, t - 1]) * (total + f2[x, t])

    rows1 = f1_in.shape[1]
    size1 = 2 * size2
    off1 = 4
    here1 = pl.ds(GUARD, rows1)
    lane1 = lanes_of(rows1)
    side = lane >> 6
    fine = (lane & 63) >> 1
    for x in range(2, planes2 - 2):
        below, middle, above = u2[x, 1], u2[x, 2], u2[x, 3]
        index = [(((2 * side + q) & 3) << 5) + fine for q in (-1, 0, 1, 2)]
        tiles = [
            jnp.where(side == 0, take_lanes(below, index[0]), take_lanes(middle, index[0]))[4:],
            take_lanes(middle, index[1]),
            take_lanes(middle, index[2]),
            jnp.where(side == 0, take_lanes(middle, index[3]), take_lanes(above, index[3]))[:4],
        ]
        start = 0
        for tile in tiles:
            count = tile.shape[0]
            lift1[x - 2, pl.ds(start, count, stride=2), :] = tile
            lift1[x - 2, pl.ds(start + 1, count, stride=2), :] = tile
            start += 2 * count

    kept = v_in.shape[1]

    def arrived(start, rows, a=xa, b=xb):
        a, b = a[pl.ds(start, rows)], b[pl.ds(start, rows)]
        return jnp.where(even_x, b, a), jnp.where(even_x, a, b)

    copies[0].wait()
    for x in range(-2, size1 + 2):
        f1[x + off1, here1] = f1_in[x + 2]
    for x in range(-3, size1 + 3):
        c1[x + off1, here1] = weight_of(c1_in[x + 3])
    for k in range(7):
        left, right = arrived(k * rows1, rows1, later_a, later_b)
        if k < 4:
            f1[off1 + 1 - k, here1] += left
            f1[off1 + size1 - 2 + k, here1] += right
        elif k == 4:
            f1[off1 - 3, here1] = left
            f1[off1 + size1 + 2, here1] = right
        else:
            w1[off1 + 2 - k, here1] = left + v1_in[0] if k == 5 else left
            w1[off1 + size1 - 3 + k, here1] = right + v1_in[1] if k == 5 else right
    planes1 = size1 + 8
    for ref in (u1, w1):
        for at in range(planes1):
            ref[at, pl.ds(0, GUARD)] = zeros8
            ref[at, pl.ds(GUARD + rows1, GUARD)] = zeros8
    for at in range(1, planes1 - 1):
        u1[at, here1] = c1[at, here1] * f1[at, here1]
    for at in range(planes1):
        value = w1[at, here1]
        if 2 <= at < planes1 - 2:
            center, total = around(u1, at, GUARD, rows1, lane1, 64)
            value = 0.2 * center + c1[at, here1] * (total + f1[at, here1])
        w1[at, here1] = value + lift1[at // 2, pl.ds(0, rows1)]
    for source, target, margin in ((w1, u1, 1), (u1, w1, 2)):
        for at in range(margin, planes1 - margin):
            center, total = around(source, at, GUARD, rows1, lane1, 64)
            target[at, here1] = 0.2 * center + c1[at, here1] * (total + f1[at, here1])

    size_x = f_in.shape[0]
    size_z = kept - 2 * KEEP
    short = kept // 4
    index = lanes_of(short) >> 1
    for x in range(-2, size1 + 2):
        for part in range(2):
            source = w1[x + off1, pl.ds(GUARD + (4 if part == 0 else 8), short)]
            tile = take_lanes(source, index + 64 * part)
            lift0[x + 2, pl.ds(part * 2 * short, short, stride=2), :] = tile
            lift0[x + 2, pl.ds(part * 2 * short + 1, short, stride=2), :] = tile

    off = 3
    last = size_x + off - 1
    here = pl.ds(GUARD, kept)
    for ref in (ua, ub):
        for at in range(size_x + 6):
            ref[at, pl.ds(0, GUARD)] = zeros8
            ref[at, pl.ds(GUARD + kept, GUARD)] = zeros8
    for copy in copies[1:]:
        copy.wait()
    for held, part, target in ((f_held, f_ends, f_in), (c_held, c_ends, c_in)):
        for x in range(size_x):
            target[x, pl.ds(KEEP, size_z)] = held[x].T
        target[:, pl.ds(0, KEEP)] = part[:, pl.ds(0, KEEP)]
        target[:, pl.ds(KEEP + size_z, KEEP)] = part[:, pl.ds(KEEP, KEEP)]
    shift = -GUARD
    for x in range(-3, size_x + 3):
        value = lift0[(x + 4) // 2, pl.ds(0, kept)]
        if -2 <= x <= size_x + 1:
            value = value + v_in[x + 2, pl.ds(GUARD + shift, kept)]
        ua[x + off, here] = value
    half = kept // 2
    parts = [(GUARD, half), (GUARD + half, half)]
    laneh = lanes_of(half)
    beyond = {-2: 0, -1: 1, size_x: 2, size_x + 1: 3}
    for x in range(-2, size_x + 2):
        for start, rows in parts:
            at = pl.ds(start + shift, rows)
            g[x + 2, pl.ds(start, rows)] = weight_of(c_sides[beyond[x], at] if x in beyond else c_in[x, at])

    sent = size_z + 2 * SENT
    begin = GUARD + KEEP - SENT
    taken = pl.ds(begin, sent)
    lane_s = lanes_of(sent)
    for ref in (before_in, after_in, sources):
        ref[...] = jnp.zeros(ref.shape, F32)
    messages = [arrived(40 + k * sent, sent) for k in range(EARLY)]
    messages += [arrived(7 * rows1 + k * sent, sent, later_a, later_b) for k in range(5 - EARLY)]
    for side, (edge, inward) in enumerate(((off, 1), (last, -1))):
        before, after, source0, source1, source2 = (message[side] for message in messages)
        before_in[side, taken] = g[edge - 1, taken] * before
        after_in[side, taken] = after
        sources[side, taken] = source1
        sources[2 + side, taken] = source2
        center, total = around(before_in, side, begin, sent, lane_s, LANES, False, False)
        ua[edge, taken] += 0.2 * center + g[edge - 1, taken] * (total + after)
        ua[edge + inward, taken] += g[edge + inward - 1, taken] * center
        _, total = around(after_in, side, begin, sent, lane_s, LANES, False, False)
        ua[edge - inward, taken] += 0.2 * after + g[edge - inward - 1, taken] * (total + source0 + center)

    for sweep, (origin, target) in enumerate(((ua, ub), (ub, ua))):
        for at in range(1 + sweep, size_x + 5 - sweep):
            for start, rows in parts:
                center, total = around(origin, at, start, rows, laneh, LANES)
                x = at - off
                if 0 <= x < size_x:
                    total = total + f_in[x, pl.ds(start + shift, rows)]
                elif x in (-1, size_x):
                    total = total + sources[2 * sweep + (x > 0), pl.ds(start, rows)]
                target[at, pl.ds(start, rows)] = 0.2 * center + g[at - 1, pl.ds(start, rows)] * total
    lane_z = lanes_of(size_z)
    own = GUARD + KEEP
    piece = size_x // 4
    copies = []

    def leave(source, target, x):
        if (x + 1) % piece == 0:
            planes = pl.ds(x + 1 - piece, piece)
            copies.append(pltpu.make_async_copy(source.at[planes], target.at[planes], arrivals.at[len(copies)]))
            copies[-1].start()

    for x in range(size_x):
        pressure[x] = ua[x + off, pl.ds(own, size_z)].T
        leave(pressure, pressure_far, x)
    for x in range(size_x):
        center, total = around(ua, x + off, own, size_z, lane_z, LANES)
        mine = pl.ds(own + shift, size_z)
        total = total + f_in[x, mine]
        residual[x] = (total - (6.0 + c_in[x, mine]) * center).T
        leave(residual, residual_far, x)
    for copy in copies:
        copy.wait()


def pairs_of(count):
    even = [(i, i ^ 1) for i in range(count)]
    odd = [(i, ((i - 1) ^ 1) + 1) for i in range(1, count - 1)]
    return even, odd


def gather(copies, axes, always):
    return lax.cond(always, lambda x: lax.all_to_all(x, axes, 0, 0, tiled=True), lambda x: x, copies)


def local(nx, nz, right_side, reaction, initial, coarse_inverse):
    size_x, _, size_z = right_side.shape
    size1, size2 = size_x // 2, size_x // 4
    wide, kept, sent = (size_z + 2 * rows for rows in (DEEP, KEEP, SENT))
    deep = wide + 2 * GUARD
    rows1 = size_z // 4 + 2 * GUARD
    brick = (size_x, size_z, LANES)
    padded = (size_x, deep, LANES)
    padded1 = (size1, rows1 + 2 * GUARD, LANES)
    slab = (size_x, DEEP, LANES)
    always = lax.optimization_barrier(jnp.int32(1)) > 0
    flag = always.astype(jnp.int32).reshape(1, 1)
    c, f, mza, mzb = call(
        turn_kernel, "turn", (brick, brick, (2, *slab), (2, *slab)), (reaction, right_side, flag),
        [(2, *right_side.shape)], far_args=(0, 1), copies=8,
    )
    even_z, odd_z = pairs_of(nz)
    za = lax.ppermute(mza, ("gy", "gc"), even_z)
    zb = lax.ppermute(mzb, ("gy", "gc"), odd_z)
    v, mya, myb = call(turn_again_kernel, "turn_again", (brick, slab, slab), (initial, mza))
    ya = lax.ppermute(mya, ("gy", "gc"), even_z)
    yb = lax.ppermute(myb, ("gy", "gc"), odd_z)

    message = (2 * wide + 2 * rows1 + 32, LANES)
    mxa, mxb, c, c1 = call(
        coefficient_kernel, "coefficients", (message, message, padded, padded1), (c, za, zb, ya, yb)
    )
    even_x, odd_x = pairs_of(nx)
    xa = lax.ppermute(mxa, "gx", even_x)
    xb = lax.ppermute(mxb, "gx", odd_x)

    margin, later = (EARLY * sent, LANES), ((5 - EARLY) * sent, LANES)
    held, ends = (size_x, kept, LANES), (size_x, 2 * KEEP, LANES)
    f, v, edges, f1, mua, mub, mla, mlb, f_ends, c_ends, v_mid = call(
        inner_kernel, "inner",
        (padded, padded, (4, deep, LANES), (size1 - 2, rows1, LANES), margin, margin, later, later, ends, ends, (size_x - 2, kept, LANES)),
        (f, v, c, za, zb, ya, yb),
        [padded] * 4, far_outs=(10,), copies=1,
    )

    box2 = (size2 + 10, 5, 8, LANES)
    near, level1 = (40 + EARLY * sent, LANES), (7 * rows1, LANES)
    sides0, sides1 = (4, deep, LANES), (2, rows1, LANES)
    parts1 = (size1 + 4, rows1, LANES), (size1 + 6, rows1, LANES)
    field0 = (size_x + 4, deep, LANES)
    field1 = (size1 + 10, rows1 + 2 * GUARD, LANES)
    chunk, mna, mnb, m1a, m1b, v, c_sides, f1, c1, v1, level2, c2 = call(
        outer_kernel, "outer",
        (
            (nx * nz // 2, 2, 8, LANES), near, near, level1, level1,
            (6, kept, LANES), (4, kept, LANES), *parts1, sides1, (2 * size2 + 10, 8, LANES), (size2 + 6, 3, 8, LANES),
        ),
        (f, c, v, edges, f1, c1, mua, mub, xa, xb),
        [
            field0, sides0, (2, deep, LANES), (12, deep, LANES), field1, field1, field1, field1,
            box2, (size2 + 10, 8, LANES), box2, box2, box2,
        ],
        far_outs=range(5, 8), copies=4,
    )
    na = lax.ppermute(mna, "gx", even_x)
    nb = lax.ppermute(mnb, "gx", odd_x)
    own = gather(chunk, ("gx", "gy"), always)
    both = (7 * rows1 + (5 - EARLY) * sent, LANES)
    own2, mla, mlb = call(
        meet_kernel, "meet", ((2 * size2, 8, LANES), both, both), (level2, na, nb, m1a, m1b, mla, mlb, own)
    )
    la = lax.ppermute(mla, "gx", even_x)
    lb = lax.ppermute(mlb, "gx", odd_x)
    other = lax.ppermute(own, "gc", [(0, 1), (1, 0)])
    z2a = lax.ppermute(own2, ("gy", "gc"), even_z)
    z2b = lax.ppermute(own2, ("gy", "gc"), odd_z)
    grid3 = (2 * nx + 8, nz + 2, 8, LANES)
    rows = coarse_inverse.shape[0]
    window3, e = call(
        functools.partial(coarse_kernel, nx, nz), "coarse",
        ((3, 10, 3, 8, LANES), (nx * nz, rows)),
        (own, other, coarse_inverse),
        [*[grid3] * 5, (LANES, LANES), (COARSE**3 // LANES, LANES), coarse_inverse.shape],
        far_args=(2,), copies=4,
    )
    sides = (4 * size2 - 2, 8, LANES)
    msa, msb = call(side_kernel, "sides", (sides, sides), (own2, z2a, z2b, e))
    sa = lax.ppermute(msa, "gx", even_x)
    sb = lax.ppermute(msb, "gx", odd_x)
    (e,) = call(follow_kernel, "follow", (e.shape,), (e, msa))
    e = gather(e, ("gx", "gy", "gc"), always).reshape(COARSE**3 // LANES, LANES)

    near2 = (size2 + 8, 5, 8, LANES)
    box3 = (10, 5, 8, LANES)
    box = (size_x + 6, kept + 2 * GUARD, LANES)
    return call(
        functools.partial(up_kernel, nx, nz), "up",
        ((size_x, LANES, size_z), (size_x, LANES, size_z)),
        (e, window3, own2, z2a, z2b, sa, sb, c2, v_mid, v, right_side, reaction, c_sides, f1, c1, f_ends, c_ends, v1, na, nb, la, lb),
        [
            box3, grid3, box3, (LANES, LANES), near2, near2, near2,
            field1, field1, field1, field1, (size2 + 4, rows1 + 2 * GUARD, LANES),
            box, box, box, (size1 + 4, kept + 2 * GUARD, LANES), *[(2, kept + 2 * GUARD, LANES)] * 2, (4, kept + 2 * GUARD, LANES),
            (size_x + 4, kept, LANES), held, held, right_side.shape, right_side.shape, (4, kept, LANES), parts1[0],
            right_side.shape, right_side.shape,
        ],
        far_args=range(8, 14), far_outs=(0, 1), copies=8, results=True,
    )


def solution(mesh):
    nx, nz = mesh.shape["gx"], mesh.shape["gz"]
    fine = Mesh(mesh.devices.reshape(nx, nz // 2, 2), ("gx", "gy", "gc"))
    brick = P("gx", None, ("gy", "gc"))
    return jax.shard_map(
        lambda *args: tuple(local(nx, nz, *args)),
        mesh=fine,
        in_specs=(brick, brick, brick, P(("gx", "gy", "gc"), None)),
        out_specs=(brick, brick),
        check_vma=False,
    )
```
